32 devices in a mesh: fsdp: 8 (over z, y), expert: 4 (over x, core).
Axes of the slice: x: 2, y: 2, z: 4, core: 2. Of those that a mesh axis runs over, the one named last changes fastest.
Arguments:
- tokens: bfloat16 [32768, 768], P(('fsdp', 'expert')), may hold values from -6 to 6
- cotangent: bfloat16 [32768, 768], P(('fsdp', 'expert')), may hold values from -6 to 6
- prev_logits: bfloat16 [32768, 12], P(('fsdp', 'expert')), may hold values from -3 to 3
- routes: int32 [32768, 2], P(('fsdp', 'expert')), may hold values from 0 to 11, all different within a row
- capacity: int32 [8], replicated, may hold values from 64 to 128
- segments: int32 [32768], P(('fsdp', 'expert')), may hold values from 0 to 63, as said below
- positions: int32 [32768], P(('fsdp', 'expert')), may hold values from 0 to 511, as said below
- w_qkv: bfloat16 [768, 2304], P('fsdp'), may hold values from -0.21875 to 0.21875
- w_out: bfloat16 [768, 768], P('fsdp'), may hold values from -0.625 to 0.625
- gate_matrix: bfloat16 [768, 16], P('fsdp'), may hold values from -0.109375 to 0.109375
- const_values: bfloat16 [768, 2], P('fsdp'), may hold values from -5 to 5
- attn_gain: bfloat16 [768], P('fsdp'), may hold values from 0.5 to 1.5
- moe_gain: bfloat16 [768], P('fsdp'), may hold values from 0.5 to 1.5
- w_gate_up: bfloat16 [8, 768, 4096], P('expert', 'fsdp'), may hold values from -0.21875 to 0.21875
- w_down: bfloat16 [8, 2048, 768], P('expert', 'fsdp'), may hold values from -0.125 to 0.125
Outputs:
- output: bfloat16 [32768, 768], P(('fsdp', 'expert'))
- input_grad: float32 [32768, 768], P(('fsdp', 'expert'))
- prev_logits_grad: float32 [32768, 12], P(('fsdp', 'expert'))
- w_qkv_grad: float32 [768, 2304], P('fsdp')
- w_out_grad: float32 [768, 768], P('fsdp')
- gate_matrix_grad: float32 [768, 16], P('fsdp')
- const_values_grad: float32 [768, 2], P('fsdp')
- attn_gain_grad: float32 [768], P('fsdp')
- moe_gain_grad: float32 [768], P('fsdp')
- w_gate_up_grad: float32 [8, 768, 4096], P('expert', 'fsdp')
- w_down_grad: float32 [8, 2048, 768], P('expert', 'fsdp')
The draws below stay inside these ranges and needn't reach their ends.
Inputs may be any that keep to these rules, and one draw needn't show every extreme that they name: The two routes of a token differ; 0 to 7 are SwiGLU experts, 8 the zero expert, 9 the copy expert, 10 and 11 the constant experts. `segments`: within each aligned block of 512 tokens the numbers start at 0 and rise by one at each new document; documents start only at multiples of 8 within the block; the first block is one document, and in the second block a document starts at every multiple of 8. `positions`: 0 at a document's first token, rising by one along it.
All inputs are finite; a program needn't handle non-finite values.
Results may differ from the reference program's by a relative error of at most 0.02.
Values may be sent and summed in bfloat16 or wider, within the bound.
No kernel may reach another device: no remote copies, remote signals or barrier semaphores. Data moves between devices by JAX's collectives and lax.ppermute only.
A program may use at most 160 MiB of HBM per device.

```python
import math
import jax
import jax.numpy as jnp
from jax import lax

D = 768
HEADS = 12
HEAD_DIM = 64
FF = 2048
EXPERTS = 8
SEQ = 512
CAP = 128
CHOICES = 12
GATE_COLS = 16
TOKENS = 32768


def document_layout(key):
    blocks = TOKENS // SEQ
    rate_key, cut_key = jax.random.split(jax.random.fold_in(key, 7))
    rate_level = jax.random.randint(rate_key, (blocks, 1), 0, 4)
    spacing_table = jnp.array([1, 4, 16, 64], dtype=jnp.int32)
    spacing = jnp.sum((rate_level == jnp.arange(4, dtype=jnp.int32)[None, :]).astype(jnp.int32) * spacing_table[None, :], axis=1, keepdims=True)
    block_index = jnp.arange(blocks, dtype=jnp.int32)[:, None]
    spacing = jnp.where(block_index == 1, 1, spacing)
    draws_int = jax.random.randint(cut_key, (blocks, SEQ), 0, 1 << 20)
    seq_index = jnp.arange(SEQ, dtype=jnp.int32)[None, :]
    on_grid = seq_index % 8 == 0
    starts = (draws_int % spacing == 0) & on_grid | (seq_index == 0)
    starts = jnp.where(block_index == 0, seq_index == 0, starts)
    segment_ids = jnp.cumsum(starts.astype(jnp.int32), axis=1, dtype=jnp.int32) - 1
    start_index = lax.cummax(jnp.where(starts, seq_index, 0), axis=1)
    offsets = seq_index - start_index
    return (segment_ids.reshape(-1).astype(jnp.int32), offsets.reshape(-1).astype(jnp.int32))


def draw_segments(key, part):
    return document_layout(key)[0]


def draw_positions(key, part):
    return document_layout(key)[1]


def draw_capacity(key, part):
    value_key, ranking_key = jax.random.split(jax.random.fold_in(key, 11))
    values = jax.random.randint(value_key, (EXPERTS,), CAP // 2, CAP + 1)
    ranking = jax.random.permutation(ranking_key, EXPERTS)
    values = jnp.where(ranking == 0, CAP, values)
    return jnp.where(ranking == 1, CAP // 2, values).astype(jnp.int32)


def level_of(stream_key, extent, shards, smallest, largest):
    def one(axis_at, parts):
        draws = jax.random.uniform(jax.random.fold_in(jax.random.fold_in(stream_key, 6), axis_at), (parts,), jnp.float32, smallest / len(shards), largest / len(shards))
        return jnp.repeat(jnp.exp(draws), extent[axis_at] // parts).reshape((-1,) + (1,) * (len(extent) - axis_at - 1))

    level = one(*shards[0])
    for cut in shards[1:]:
        level = level * one(*cut)
    return level


def different_ones(rng, rows, amount, top, lift):
    order = jax.random.permutation(jax.random.fold_in(rng, 1), amount)
    boost = order
    for power in range(3):
        boost = boost * boost // amount
    boost = boost * lift // amount
    lots = jax.random.randint(jax.random.fold_in(rng, 2), (rows, amount), 0, 4096) + boost
    holders = jax.random.permutation(jax.random.fold_in(rng, 3), rows)[jnp.arange(amount) % rows]
    lots = jnp.where(jnp.arange(rows)[:, None] == holders[None, :], 1 << 14, lots)
    merit = lots * amount + jnp.arange(amount)
    return lax.top_k(merit.astype(jnp.int32), top)[1].astype(jnp.int32)


def gaussian(own_key, extent, scale, most, cuts=(), held_as=jnp.bfloat16):
    factor_of = level_of(own_key, extent, cuts, -0.22, 0.18) if cuts else 1.0
    values = jax.random.normal(own_key, extent, jnp.float32) * scale * factor_of
    return jnp.minimum(jnp.maximum(values, -most), most).astype(held_as)


def setup_inputs(seed: int = 0) -> dict:
    key_of = jax.random.split(jax.random.key(seed), 16)
    tokens = gaussian(key_of[0], (TOKENS, D), 1.0, 6.0, ((0, 32),))
    cotangent = gaussian(key_of[1], (TOKENS, D), 1.0, 6.0, ((0, 32),))
    prev_logits = gaussian(key_of[2], (TOKENS, CHOICES), 0.5, 3.0, ((0, 32),))
    routes = different_ones(key_of[3], TOKENS, CHOICES, 2, 1365)
    capacity = draw_capacity(jax.random.fold_in(key_of[15], 71), 0)
    segments = draw_segments(jax.random.fold_in(key_of[15], 71), 0)
    positions = draw_positions(jax.random.fold_in(key_of[15], 71), 0)
    w_qkv = gaussian(key_of[7], (D, 3 * D), D ** -0.5, 0.21875, ((0, 8),))
    w_out = gaussian(key_of[8], (D, D), (D // 8) ** -0.5, 0.625, ((0, 8),))
    gate_matrix = gaussian(key_of[9], (D, GATE_COLS), (4 * D) ** -0.5, 0.109375, ((0, 8),))
    const_values = gaussian(key_of[10], (D, 2), 1.0, 5.0, ((0, 8),))
    attn_gain = jnp.clip(1.0 + 0.1 * jax.random.normal(key_of[11], (D,), jnp.float32), 0.5, 1.5).astype(jnp.bfloat16)
    moe_gain = jnp.clip(1.0 + 0.1 * jax.random.normal(key_of[12], (D,), jnp.float32), 0.5, 1.5).astype(jnp.bfloat16)
    w_gate_up = gaussian(key_of[13], (EXPERTS, D, 2 * FF), D ** -0.5, 0.21875, ((0, 4), (1, 8)))
    w_down = gaussian(key_of[14], (EXPERTS, FF, D), FF ** -0.5, 0.125, ((0, 4), (1, 8)))
    return dict(tokens=tokens, cotangent=cotangent, prev_logits=prev_logits, routes=routes, capacity=capacity, segments=segments, positions=positions, w_qkv=w_qkv, w_out=w_out, gate_matrix=gate_matrix, const_values=const_values, attn_gain=attn_gain, moe_gain=moe_gain, w_gate_up=w_gate_up, w_down=w_down)


EPSILON = 1e-05
ROPE_BASE = 10000.0
FLOOR_SCORE = -1e+30
HIGHEST = lax.Precision.HIGHEST

@jax.custom_vjp
def low(v):
    return lax.optimization_barrier(v.astype(jnp.bfloat16)).astype(jnp.float32)

@jax.custom_vjp
def low_back(v):
    return v

def low_keep(v):
    return (low(v), None)

def low_pass(kept, grad):
    return (grad,)

def back_keep(v):
    return (v, None)

def back_low(kept, grad):
    return (low(grad),)
low.defvjp(low_keep, low_pass)
low_back.defvjp(back_keep, back_low)

def pair_tables(route, capacity):
    choice_ids = jnp.arange(EXPERTS + 4, dtype=jnp.int32)
    flat_routes = route.reshape(-1).astype(jnp.int32)
    route_flags = (flat_routes[:, None] == choice_ids[None, :]).astype(jnp.int32)
    earlier = jnp.cumsum(route_flags, axis=0, dtype=jnp.int32) - route_flags
    slot_rank = lax.optimization_barrier(jnp.sum(earlier * route_flags, axis=1, dtype=jnp.int32))
    cap_limit = lax.optimization_barrier(jnp.sum(route_flags[:, :EXPERTS] * capacity.astype(jnp.int32)[None, :], axis=1, dtype=jnp.int32))
    kept_pairs = (flat_routes < EXPERTS) & (slot_rank < cap_limit)
    slot_index = jnp.where(kept_pairs, flat_routes * CAP + slot_rank, -1).astype(jnp.int32).reshape(route.shape)
    route_hot = route_flags.reshape(route.shape[0], 2, EXPERTS + 4).astype(jnp.float32)
    copy_mask = route_hot[:, :, EXPERTS + 1]
    const_mask = route_hot[:, :, EXPERTS + 2:]
    return (slot_index, route_hot, copy_mask, const_mask)

def rope_tables(position, head_dim):
    half_dim = head_dim // 2
    frequency = jnp.exp(jnp.arange(half_dim, dtype=jnp.float32) * (-2.0 * math.log(ROPE_BASE) / head_dim))
    angles = position.astype(jnp.float32)[:, None] * frequency[None, :]
    return (jnp.cos(angles)[:, None, :], jnp.sin(angles)[:, None, :])

def rotate(values, cosine, sine_part):
    half_dim = values.shape[-1] // 2
    first_half, second_half = (values[..., :half_dim], values[..., half_dim:])
    return jnp.concatenate([first_half * cosine - second_half * sine_part, first_half * sine_part + second_half * cosine], axis=-1)

def norm_apply(inputs, gain):
    return inputs * lax.rsqrt(lax.optimization_barrier(jnp.mean(inputs * inputs, axis=-1, keepdims=True)) + EPSILON) * gain

def block_tables(route, capacity, segment, position):
    slot_index, route_hot, copy_mask, const_mask = pair_tables(route, capacity)
    slot_ids = jnp.arange(EXPERTS * CAP, dtype=jnp.int32)
    pick_table = (slot_index[None, :, :] == slot_ids[:, None, None]).astype(jnp.float32)
    seq_index = jnp.arange(SEQ, dtype=jnp.int32)
    allowed = (seq_index[:, None] >= seq_index[None, :]) & (segment[:, None] == segment[None, :])
    cosine, sine_part = rope_tables(position, HEAD_DIM)
    return (pick_table, route_hot, copy_mask, const_mask, allowed, cosine, sine_part)

def block_forward(params, inputs, prev, tables):
    w_qkv, w_out, gate_matrix, const_values, attn_gain, moe_gain, w_gate_up, w_down = params
    pick_table, route_hot, copy_mask, const_mask, allowed, cosine, sine_part = tables
    score_scale = 1.0 / math.sqrt(HEAD_DIM)
    act_one = low(norm_apply(inputs, attn_gain))
    qkv = low_back(jnp.dot(act_one, w_qkv, precision=HIGHEST))
    query_rot = low(rotate(qkv[:, :D].reshape(SEQ, HEADS, HEAD_DIM), cosine, sine_part))
    key_rot = low(rotate(qkv[:, D:2 * D].reshape(SEQ, HEADS, HEAD_DIM), cosine, sine_part))
    value_low = low(qkv[:, 2 * D:].reshape(SEQ, HEADS, HEAD_DIM))
    scores = jnp.einsum('qhd,khd->hqk', query_rot, key_rot, precision=HIGHEST) * score_scale
    scores = low_back(jnp.where(allowed[None], scores, FLOOR_SCORE))
    prob_low = low(jax.nn.softmax(scores, axis=-1))
    attended = jnp.einsum('hqk,khd->qhd', prob_low, value_low, precision=HIGHEST).reshape(SEQ, D)
    attended_low = low_back(low(attended))
    residual = inputs + low_back(jnp.dot(attended_low, w_out, precision=HIGHEST))
    normed_two = norm_apply(residual, moe_gain)
    act_two = low(normed_two)
    logits_all = low_back(jnp.dot(act_two, gate_matrix, precision=HIGHEST))
    router = logits_all[:, :EXPERTS + 4] + prev
    gates = jax.nn.softmax(lax.optimization_barrier(jnp.sum(router[:, None, :] * route_hot, axis=-1)), axis=1)
    const_gates = jax.nn.softmax(logits_all[:, EXPERTS + 4:].reshape(SEQ, 2, 2), axis=-1)
    sent_zero = jnp.dot(pick_table[:, :, 0], low_back(act_two), precision=HIGHEST)
    sent_one = jnp.dot(pick_table[:, :, 1], low_back(act_two), precision=HIGHEST)
    dispatched = (sent_zero + sent_one).reshape(EXPERTS, CAP, D)
    gate_up = low_back(jnp.einsum('ecd,edf->ecf', dispatched, w_gate_up, precision=HIGHEST))
    hidden_low = low_back(low(jax.nn.silu(gate_up[..., :FF]) * gate_up[..., FF:]))
    produced = low_back(low(jnp.einsum('ecf,efd->ecd', hidden_low, w_down, precision=HIGHEST))).reshape(EXPERTS * CAP, D)
    combined = jnp.einsum('esk,ed->skd', pick_table, produced, precision=HIGHEST)
    const_out = const_gates[..., 0:1] * normed_two[:, None, :] + const_gates[..., 1:2] * const_values.T[None, :, :]
    term = combined + copy_mask[..., None] * normed_two[:, None, :]
    term = term + const_mask[:, :, 0, None] * const_out[:, None, 0, :] + const_mask[:, :, 1, None] * const_out[:, None, 1, :]
    return residual + lax.optimization_barrier(jnp.sum(gates[..., None] * term, axis=1))

def reference(tokens, cotangent, prev_logits, routes, capacity, segments, positions, w_qkv, w_out, gate_matrix, const_values, attn_gain, moe_gain, w_gate_up, w_down):
    params = tuple((weight.astype(jnp.float32) for weight in (w_qkv, w_out, gate_matrix, const_values, attn_gain, moe_gain, w_gate_up, w_down)))
    blocks = tokens.shape[0] // SEQ
    stacked = (tokens.astype(jnp.float32).reshape(blocks, SEQ, D), cotangent.astype(jnp.float32).reshape(blocks, SEQ, D), prev_logits.astype(jnp.float32).reshape(blocks, SEQ, EXPERTS + 4), routes.reshape(blocks, SEQ, 2), segments.reshape(blocks, SEQ), positions.reshape(blocks, SEQ))

    def block_step(grad_sums, block_in):
        inputs, cot_block, prev_block, route, segment, position = block_in
        tables = block_tables(route, capacity, segment, position)

        def forward(param_set, inputs_in, prev_in):
            return block_forward(param_set, inputs_in, prev_in, tables)
        output, pullback = jax.vjp(forward, params, inputs, prev_block)
        param_grads, input_grad, prev_grad = pullback(cot_block)
        grad_sums = jax.tree.map(jnp.add, grad_sums, param_grads)
        return (grad_sums, (output.astype(jnp.bfloat16), input_grad, prev_grad))
    zero_sums = jax.tree.map(jnp.zeros_like, params)
    grad_sums, (outputs, input_grads, prev_grads) = lax.scan(block_step, zero_sums, stacked)
    return (outputs.reshape(-1, D), input_grads.reshape(-1, D), prev_grads.reshape(-1, EXPERTS + 4), grad_sums[0], grad_sums[1], grad_sums[2], grad_sums[3], grad_sums[4], grad_sums[5], grad_sums[6], grad_sums[7])
```

```python
import functools
import math

import jax
import jax.numpy as jnp
from jax import lax
from jax.experimental import pallas as pl
from jax.experimental.pallas import tpu as pltpu
from jax.sharding import Mesh
from jax.sharding import PartitionSpec as P

D = 768
HEADS = 12
HEAD_DIM = 64
FF = 2048
EXPERTS = 8
SEQ = 512
CAP = 128
CHOICES = EXPERTS + 4
SLOTS = EXPERTS * CAP

EPSILON = 1e-05
ROPE_BASE = 10000.0
FLOOR_SCORE = -1e30
HIGHEST = lax.Precision.HIGHEST
BF = jnp.bfloat16
F32 = jnp.float32
VMEM_MOST = 56 * 2**20


def dot(a, b):
    return jnp.dot(a, b, preferred_element_type=F32)


def dot_nt(a, b):
    return lax.dot_general(a, b, (((1,), (1,)), ((), ())), preferred_element_type=F32)


def dot_tn(a, b):
    return lax.dot_general(a, b, (((0,), (0,)), ((), ())), preferred_element_type=F32)


def pair_tables(route, capacity):
    choice_ids = jnp.arange(CHOICES, dtype=jnp.int32)
    route_hot = (route[:, :, None] == choice_ids).astype(F32)
    counts = jnp.sum(route_hot, axis=1)
    seq_index = jnp.arange(SEQ)
    before = (seq_index[:, None] > seq_index[None, :]).astype(BF)
    earlier = dot(before, counts.astype(BF))
    slot_rank = jnp.sum(earlier[:, None, :] * route_hot, axis=-1)
    cap_limit = jnp.sum(route_hot[:, :, :EXPERTS] * capacity.astype(F32), axis=-1)
    kept_pairs = (route < EXPERTS) & (slot_rank < cap_limit)
    slot_index = jnp.where(kept_pairs, route * CAP + slot_rank.astype(jnp.int32), -1)
    return slot_index, route_hot


def rope_tables(position, head_dim):
    half_dim = head_dim // 2
    frequency = jnp.exp(
        jnp.arange(half_dim, dtype=F32) * (-2.0 * math.log(ROPE_BASE) / head_dim)
    )
    angles = position.astype(F32)[:, None] * frequency[None, :]
    return (jnp.cos(angles)[:, None, :], jnp.sin(angles)[:, None, :])


def rotate(values, cosine, sine_part):
    half_dim = values.shape[-1] // 2
    first_half, second_half = (values[..., :half_dim], values[..., half_dim:])
    return jnp.concatenate(
        [
            first_half * cosine - second_half * sine_part,
            first_half * sine_part + second_half * cosine,
        ],
        axis=-1,
    )


def norm_forward(inputs, gain):
    inverse = lax.rsqrt(jnp.mean(inputs * inputs, axis=-1, keepdims=True) + EPSILON)
    return (inputs * inverse * gain, inverse)


def norm_backward(inputs, inverse, gain, grad_in):
    scaled = grad_in * gain
    gain_grad = jnp.sum(grad_in * inputs * inverse, axis=0)
    inner_mean = jnp.mean(scaled * inputs, axis=-1, keepdims=True)
    return (inverse * scaled - inputs * inverse * inverse * inverse * inner_mean, gain_grad)


def masked_scores(query_rot, key_rot, allowed):
    scores = jnp.einsum("qhd,khd->hqk", query_rot, key_rot, preferred_element_type=F32)
    return jnp.where(allowed[None], scores * (1.0 / math.sqrt(HEAD_DIM)), FLOOR_SCORE)


def forward_part(inputs_low, cot_low, prev_low, route, capacity, segment, position, mixer):
    w_qkv, w_out, gate_matrix, const_values, gain_one, gain_two = mixer
    inputs = inputs_low.astype(F32)
    normed_one, inverse_one = norm_forward(inputs, gain_one)
    act_one = normed_one.astype(BF)
    qkv = dot(act_one, w_qkv)
    cosine, sine_part = rope_tables(position, HEAD_DIM)
    query_rot = rotate(qkv[:, :D].reshape(SEQ, HEADS, HEAD_DIM), cosine, sine_part).astype(BF)
    key_rot = rotate(qkv[:, D : 2 * D].reshape(SEQ, HEADS, HEAD_DIM), cosine, sine_part).astype(BF)
    value_low = qkv[:, 2 * D :].reshape(SEQ, HEADS, HEAD_DIM).astype(BF)
    seq_index = jnp.arange(SEQ, dtype=jnp.int32)
    allowed = (seq_index[:, None] >= seq_index[None, :]) & (segment[:, None] == segment[None, :])
    scores = masked_scores(query_rot, key_rot, allowed)
    row_max = jnp.max(scores, axis=-1, keepdims=True)
    log_total = row_max + jnp.log(jnp.sum(jnp.exp(scores - row_max), axis=-1, keepdims=True))
    prob_low = jnp.exp(scores - log_total).astype(BF)
    attended = jnp.einsum("hqk,khd->qhd", prob_low, value_low, preferred_element_type=F32)
    attended_low = attended.reshape(SEQ, D).astype(BF)
    residual = inputs + dot(attended_low, w_out)
    normed_two, inverse_two = norm_forward(residual, gain_two)
    act_two = normed_two.astype(BF)
    logits_all = dot(act_two, gate_matrix)
    router = logits_all[:, :CHOICES] + prev_low.astype(F32)
    slot_index, route_hot = pair_tables(route, capacity)
    gates = jax.nn.softmax(jnp.sum(router[:, None, :] * route_hot, axis=-1), axis=1)
    const_gates = jax.nn.softmax(logits_all[:, CHOICES:].reshape(SEQ, 2, 2), axis=-1)
    slot_ids = jnp.arange(SLOTS, dtype=jnp.int32)
    pick_table = (slot_index[None, :, :] == slot_ids[:, None, None]).astype(BF)
    send_rows = dot(jnp.sum(pick_table, axis=2), act_two).astype(BF)
    grad_out = cot_low.astype(F32)
    term_grad_low = (gates[..., None] * grad_out[:, None, :]).astype(BF)
    slot_grad = jnp.einsum("esk,skd->ed", pick_table, term_grad_low, preferred_element_type=F32)
    sent = jnp.stack([send_rows, slot_grad.astype(BF)]).reshape(2, EXPERTS, CAP, D)
    kept = dict(
        inputs=inputs, inverse_one=inverse_one, act_one=act_one, cosine=cosine, sine_part=sine_part,
        query_rot=query_rot, key_rot=key_rot, value_low=value_low, allowed=allowed,
        log_total=log_total, attended_low=attended_low, residual=residual,
        normed_two=normed_two, inverse_two=inverse_two, act_two=act_two, gates=gates,
        const_gates=const_gates, pick_table=pick_table, route_hot=route_hot, grad_out=grad_out,
    )
    return sent.transpose(1, 0, 2, 3), kept


FC = 512


def expert_rows_body(x_ref, g_ref, wg_ref, wu_ref, wd_ref, hid_ref, dg_ref, du_ref, out_ref, acc, racc):
    step = pl.program_id(0)
    x = x_ref[:, 0].reshape(-1, D)
    g = g_ref[:, 0].reshape(-1, D)
    wg, wu, wd = wg_ref[...], wu_ref[...], wd_ref[...]
    gate = dot(x, wg)
    up = dot(x, wu)
    hgrad = dot_nt(g, wd).astype(BF).astype(F32)
    sig = 1.0 / (1.0 + jnp.exp(-gate))
    act = gate * sig
    hidden = (act * up).astype(BF)
    dgate = (hgrad * up * sig * (1.0 + gate * (1.0 - sig))).astype(BF)
    dup = (hgrad * act).astype(BF)
    hid_ref[...] = hidden
    dg_ref[...] = dgate
    du_ref[...] = dup
    prod = dot(hidden, wd)
    rgrad = dot_nt(dgate, wg) + dot_nt(dup, wu)

    @pl.when(step == 0)
    def _():
        acc[...] = prod
        racc[...] = rgrad

    @pl.when(step > 0)
    def _():
        acc[...] += prod
        racc[...] += rgrad

    @pl.when(step == pl.num_programs(0) - 1)
    def _():
        out_ref[:, 0] = acc[...].astype(BF).reshape(-1, CAP, D)
        out_ref[:, 1] = racc[...].astype(BF).reshape(-1, CAP, D)


def expert_rows(received, w_gate_up, w_down):
    n = received.shape[0]
    rows = n * CAP
    steps = FF // FC
    wide = jax.ShapeDtypeStruct((rows, FF), BF)
    block = pl.BlockSpec((rows, FC), lambda j: (0, j))
    return pl.pallas_call(
        expert_rows_body,
        grid=(steps,),
        in_specs=[
            pl.BlockSpec((n, 1, CAP, D), lambda j: (0, 0, 0, 0)),
            pl.BlockSpec((n, 1, CAP, D), lambda j: (0, 1, 0, 0)),
            pl.BlockSpec((D, FC), lambda j: (0, j)),
            pl.BlockSpec((D, FC), lambda j: (0, steps + j)),
            pl.BlockSpec((FC, D), lambda j: (j, 0)),
        ],
        out_specs=[block, block, block, pl.BlockSpec((n, 2, CAP, D), lambda j: (0, 0, 0, 0))],
        out_shape=[wide, wide, wide, jax.ShapeDtypeStruct((n, 2, CAP, D), BF)],
        scratch_shapes=[pltpu.VMEM((rows, D), F32), pltpu.VMEM((rows, D), F32)],
        compiler_params=pltpu.CompilerParams(
            dimension_semantics=("arbitrary",), vmem_limit_bytes=VMEM_MOST
        ),
        cost_estimate=pl.CostEstimate(
            flops=12 * rows * D * FF, bytes_accessed=18 * D * FF // 3 + 6 * rows * FF, transcendentals=rows * FF
        ),
    )(received, received, w_gate_up, w_gate_up, w_down)


FW = 512


def expert_wgrad_body(parts, *refs):
    received = refs[:parts]
    hid, dg, du = refs[parts : 2 * parts], refs[2 * parts : 3 * parts], refs[3 * parts : 4 * parts]
    dgate_ref, dup_ref, down_ref, xt, gb = refs[4 * parts :]
    rows = received[0].shape[0] * CAP

    @pl.when(pl.program_id(0) == 0)
    def _():
        for i in range(parts):
            xt[:, i * rows : (i + 1) * rows] = received[i][:, 0].reshape(rows, D).T
            gb[i * rows : (i + 1) * rows, :] = received[i][:, 1].reshape(rows, D)

    def joined(vs):
        return jnp.concatenate([v[...] for v in vs], axis=0)

    dgate_ref[...] = dot(xt[...], joined(dg)).astype(BF)
    dup_ref[...] = dot(xt[...], joined(du)).astype(BF)
    down_ref[...] = dot_tn(joined(hid), gb[...]).astype(BF)


def expert_wgrad(received, hid, dg, du):
    parts = len(received)
    n = received[0].shape[0]
    rows = n * CAP
    whole = pl.BlockSpec((n, 2, CAP, D), lambda j: (0, 0, 0, 0))
    block = pl.BlockSpec((rows, FW), lambda j: (0, j))
    half = jax.ShapeDtypeStruct((D, FF), BF)
    return pl.pallas_call(
        functools.partial(expert_wgrad_body, parts),
        grid=(FF // FW,),
        in_specs=[whole] * parts + [block] * (3 * parts),
        out_specs=[
            pl.BlockSpec((D, FW), lambda j: (0, j)),
            pl.BlockSpec((D, FW), lambda j: (0, j)),
            pl.BlockSpec((FW, D), lambda j: (j, 0)),
        ],
        out_shape=[half, half, jax.ShapeDtypeStruct((FF, D), BF)],
        scratch_shapes=[pltpu.VMEM((D, parts * rows), BF), pltpu.VMEM((parts * rows, D), BF)],
        compiler_params=pltpu.CompilerParams(
            dimension_semantics=("arbitrary",), vmem_limit_bytes=VMEM_MOST
        ),
        cost_estimate=pl.CostEstimate(
            flops=6 * parts * rows * D * FF, bytes_accessed=6 * parts * rows * FF + 6 * D * FF, transcendentals=0
        ),
    )(*received, *hid, *dg, *du)


def expert_part(received, w_gate_up, w_down):
    made = [expert_rows(r, w_gate_up, w_down) for r in received]
    grads = expert_wgrad(received, *[[m[i] for m in made] for i in range(3)])
    return [m[3] for m in made], grads


def backward_part(returned, kept, mixer):
    w_qkv, w_out, gate_matrix, const_values, gain_one, gain_two = mixer
    k = kept
    gates, grad_out, const_gates, normed_two = k["gates"], k["grad_out"], k["const_gates"], k["normed_two"]
    route_hot, pick_table = k["route_hot"], k["pick_table"]
    copy_mask = route_hot[:, :, EXPERTS + 1]
    const_mask = route_hot[:, :, EXPERTS + 2 :]
    const_vec = const_values.astype(F32)
    produced = returned[:, 0].reshape(SLOTS, D)
    back_rows = returned[:, 1].reshape(SLOTS, D)
    combined = jnp.einsum("esk,ed->skd", pick_table, produced, preferred_element_type=F32)
    const_out = (
        const_gates[..., 0:1] * normed_two[:, None, :]
        + const_gates[..., 1:2] * const_vec.T[None, :, :]
    )
    term = combined + copy_mask[..., None] * normed_two[:, None, :]
    term = (
        term
        + const_mask[:, :, 0, None] * const_out[:, None, 0, :]
        + const_mask[:, :, 1, None] * const_out[:, None, 1, :]
    )
    output = k["residual"] + jnp.sum(gates[..., None] * term, axis=1)
    gate_grad = jnp.sum(grad_out[:, None, :] * term, axis=-1)
    term_grad = gates[..., None] * grad_out[:, None, :]
    dispatch_grad = jnp.einsum(
        "es,ed->sd", jnp.sum(pick_table, axis=2), back_rows, preferred_element_type=F32
    )
    direct_weight = (
        copy_mask
        + const_mask[:, :, 0] * const_gates[:, None, 0, 0]
        + const_mask[:, :, 1] * const_gates[:, None, 1, 0]
    )
    direct_grad = jnp.sum(direct_weight[..., None] * term_grad, axis=1)
    along_normed = jnp.sum(term_grad * normed_two[:, None, :], axis=-1)
    along_vector = jnp.einsum("skd,dc->skc", term_grad, const_vec, precision=HIGHEST)
    in_normed = jnp.sum(const_mask * along_normed[..., None], axis=1)
    in_vector = jnp.sum(const_mask * along_vector, axis=1)
    const_in_grad = jnp.stack([in_normed, in_vector], axis=-1)
    const_logit_grad = const_gates * (
        const_in_grad - jnp.sum(const_gates * const_in_grad, axis=-1, keepdims=True)
    )
    vector_wgrad = jnp.einsum(
        "skc,skd->dc", const_mask * const_gates[:, None, :, 1], term_grad, precision=HIGHEST
    )
    picked_grad = gates * (gate_grad - jnp.sum(gates * gate_grad, axis=1, keepdims=True))
    router_grad = jnp.sum(picked_grad[..., None] * route_hot, axis=1)
    logit_grad = jnp.concatenate([router_grad, const_logit_grad.reshape(SEQ, 4)], axis=1).astype(BF)
    gate_wgrad = dot(k["act_two"].T, logit_grad)
    router_back = dot(logit_grad, gate_matrix.T)
    normed_grad = router_back + dispatch_grad + direct_grad
    residual_norm_grad, gain_two_grad = norm_backward(
        k["residual"], k["inverse_two"], gain_two, normed_grad
    )
    residual_grad = grad_out + residual_norm_grad
    out_grad_low = residual_grad.astype(BF)
    out_wgrad = dot(k["attended_low"].T, out_grad_low)
    attended_grad = dot(out_grad_low, w_out.T).astype(BF).reshape(SEQ, HEADS, HEAD_DIM)
    prob_full = jnp.exp(masked_scores(k["query_rot"], k["key_rot"], k["allowed"]) - k["log_total"])
    prob_grad = jnp.einsum("qhd,khd->hqk", attended_grad, k["value_low"], preferred_element_type=F32)
    row_inner = jnp.sum(prob_full * prob_grad, axis=-1, keepdims=True)
    score_grad = (prob_full * (prob_grad - row_inner)).astype(BF)
    scale = 1.0 / math.sqrt(HEAD_DIM)
    query_grad = jnp.einsum("hqk,khd->qhd", score_grad, k["key_rot"], preferred_element_type=F32) * scale
    key_grad = jnp.einsum("hqk,qhd->khd", score_grad, k["query_rot"], preferred_element_type=F32) * scale
    value_grad = jnp.einsum("hqk,qhd->khd", prob_full.astype(BF), attended_grad, preferred_element_type=F32)
    qkv_grad = jnp.concatenate(
        [
            rotate(query_grad, k["cosine"], -k["sine_part"]).reshape(SEQ, D),
            rotate(key_grad, k["cosine"], -k["sine_part"]).reshape(SEQ, D),
            value_grad.reshape(SEQ, D),
        ],
        axis=1,
    ).astype(BF)
    qkv_wgrad = dot(k["act_one"].T, qkv_grad)
    act_one_grad = dot(qkv_grad, w_qkv.T)
    input_norm_grad, gain_one_grad = norm_backward(k["inputs"], k["inverse_one"], gain_one, act_one_grad)
    input_grad = residual_grad + input_norm_grad
    grads = (qkv_wgrad, out_wgrad, gate_wgrad, vector_wgrad, gain_one_grad, gain_two_grad)
    return output.astype(BF), input_grad, router_grad, grads


class Paired:
    axes = ("half", "low", "inner", "side", "core")
    fsdp = ("half", "low", "inner")
    expert = ("side", "core")
    rows = ("side", "low", "inner")
    route_axes = ("half", "low", "inner", "core")

    def __init__(self, mesh):
        self.mesh = Mesh(mesh.devices.reshape(2, 2, 2, 2, 2), self.axes)
        self.routes = []
        for turn in range(4):
            pairs = []
            for z in range(4):
                for y in range(2):
                    for c in range(2):
                        half, inner = (z ^ turn) >> 1, (z ^ turn) & 1
                        pairs.append(((z * 2 + y) * 2 + c, ((half * 2 + c) * 2 + inner) * 2 + y))
            self.routes.append(pairs)

    @staticmethod
    def swap(value):
        return lax.ppermute(value, "core", [(0, 1), (1, 0)])

    @staticmethod
    def place():
        z = lax.axis_index("half") * 2 + lax.axis_index("low")
        here = lax.axis_index("half") * 2 + lax.axis_index("inner")
        return z, here, lax.axis_index("core")

    def gather(self, weight):
        z, here, core = self.place()
        own = []
        for turn in range(4):
            mine = lax.dynamic_index_in_dim(weight, (z ^ turn) & 1, 0, False)
            own.append(lax.ppermute(mine, self.route_axes, self.routes[turn]))
        other = [self.swap(v) for v in own]
        stack = jnp.stack(own + other)
        blocks = []
        for zz in range(4):
            for y in range(2):
                blocks.append(lax.dynamic_index_in_dim(stack, (y ^ core) * 4 + (zz ^ here), 0, False))
        return jnp.concatenate(blocks)

    def scatter(self, grad):
        z, here, core = self.place()
        grad = grad.reshape((4, 2, grad.shape[0] // 8) + grad.shape[1:])
        got = []
        for turn in range(4):
            part = lax.dynamic_index_in_dim(grad, here ^ turn, 0, False)
            keep = lax.dynamic_index_in_dim(part, core, 0, False)
            give = lax.dynamic_index_in_dim(part, 1 - core, 0, False)
            total = (keep.astype(F32) + self.swap(give).astype(F32)).astype(BF)
            back = [(b, a) for a, b in self.routes[turn]]
            got.append(lax.ppermute(total, self.route_axes, back).astype(F32))
        even = (z & 1) == 0
        first = jnp.where(even, got[0] + got[2], got[1] + got[3])
        second = jnp.where(even, got[1] + got[3], got[0] + got[2])
        return jnp.stack([first, second])


class Plain:
    axes = ("outer", "inner", "expert")
    fsdp = ("outer", "inner")
    expert = ("expert",)
    rows = ("expert", "inner")

    def __init__(self, mesh):
        fsdp, expert = mesh.shape["fsdp"], mesh.shape["expert"]
        inner = EXPERTS // expert
        self.mesh = Mesh(mesh.devices.reshape(fsdp // inner, inner, expert), self.axes)

    def gather(self, weight):
        own = lax.all_to_all(weight, "inner", 0, 0, tiled=True)
        full = lax.all_gather(own, "outer", axis=0, tiled=True)
        return full.reshape((-1,) + weight.shape[2:])

    def scatter(self, grad):
        inner = lax.axis_size("inner")
        part = lax.psum_scatter(grad, "outer", scatter_dimension=0, tiled=True)
        part = part.reshape((inner, part.shape[0] // inner) + part.shape[1:])
        return lax.all_to_all(part, "inner", 0, 0, tiled=True).astype(F32)


def solution(mesh):
    plan = Paired(mesh) if (mesh.shape["fsdp"], mesh.shape["expert"]) == (8, 4) else Plain(mesh)

    def on_device(
        tokens, cotangent, prev_logits, routes, capacity, segments, positions,
        w_qkv, w_out, gate_matrix, const_values, attn_gain, moe_gain, w_gate_up, w_down,
    ):
        rows = w_qkv.shape[0]
        pad = jnp.zeros((rows, 128 - 20), BF)
        small = jnp.concatenate(
            [gate_matrix, const_values, attn_gain[:, None], moe_gain[:, None], pad], axis=1
        )
        packed = lax.all_gather(
            jnp.concatenate([w_qkv, w_out, small], axis=1), plan.fsdp, axis=0, tiled=True
        )
        mixer = (
            packed[:, : 3 * D],
            packed[:, 3 * D : 4 * D],
            packed[:, 4 * D : 4 * D + 16],
            packed[:, 4 * D + 16 : 4 * D + 18],
            packed[:, 4 * D + 18].astype(F32),
            packed[:, 4 * D + 19].astype(F32),
        )
        gate_up_full = plan.gather(w_gate_up)
        down_full = plan.gather(w_down)
        parts = tokens.shape[0] // SEQ
        received, keeps = [], []
        for part in range(parts):
            span = slice(part * SEQ, (part + 1) * SEQ)
            sent, kept = forward_part(
                tokens[span], cotangent[span], prev_logits[span], routes[span], capacity,
                segments[span], positions[span], mixer,
            )
            received.append(lax.all_to_all(sent, plan.rows, 0, 0, tiled=True))
            keeps.append(kept)
        back, (gate_wgrad, up_wgrad, down_wgrad) = expert_part(received, gate_up_full, down_full)
        gate_up_total = jnp.concatenate([plan.scatter(gate_wgrad), plan.scatter(up_wgrad)], axis=2)
        down_total = plan.scatter(down_wgrad)
        outs, sums = [], None
        for part in range(parts):
            returned = lax.all_to_all(back[part], plan.rows, 0, 0, tiled=True)
            result = backward_part(returned, keeps[part], mixer)
            outs.append(result[:3])
            sums = result[3] if sums is None else jax.tree.map(jnp.add, sums, result[3])
        small_sum = jnp.concatenate(
            [sums[2], sums[3], sums[4][:, None], sums[5][:, None], jnp.zeros((D, 128 - 20), F32)], axis=1
        )
        total = jnp.concatenate([sums[0], sums[1], small_sum], axis=1).astype(BF)
        total = lax.psum_scatter(total, plan.axes, scatter_dimension=0, tiled=True)
        total = lax.all_gather(total, plan.expert, axis=0, tiled=True).astype(F32)
        return (
            jnp.concatenate([o[0] for o in outs]),
            jnp.concatenate([o[1] for o in outs]),
            jnp.concatenate([o[2] for o in outs]),
            total[:, : 3 * D],
            total[:, 3 * D : 4 * D],
            total[:, 4 * D : 4 * D + 16],
            total[:, 4 * D + 16 : 4 * D + 18],
            total[:, 4 * D + 18],
            total[:, 4 * D + 19],
            gate_up_total,
            down_total,
        )

    every = plan.fsdp + plan.expert
    split = P(every, None)
    shard = P(plan.fsdp, None)
    line = P(plan.fsdp)
    whole = P(plan.expert, plan.fsdp, None)
    return jax.shard_map(
        on_device,
        mesh=plan.mesh,
        in_specs=(
            split, split, split, split, P(), P(every), P(every),
            shard, shard, shard, shard, line, line, whole, whole,
        ),
        out_specs=(split, split, split, shard, shard, shard, shard, line, line, whole, whole),
        check_vma=False,
    )
```

```python
import functools
import math

import jax
import jax.numpy as jnp
from jax import lax
from jax.experimental import pallas as pl
from jax.experimental.pallas import tpu as pltpu
from jax.sharding import Mesh
from jax.sharding import PartitionSpec as P

D = 768
HEADS = 12
HEAD_DIM = 64
FF = 2048
EXPERTS = 8
SEQ = 512
CAP = 128
CHOICES = EXPERTS + 4
SLOTS = EXPERTS * CAP

EPSILON = 1e-05
ROPE_BASE = 10000.0
FLOOR_SCORE = -1e30
HIGHEST = lax.Precision.HIGHEST
BF = jnp.bfloat16
F32 = jnp.float32
VMEM_MOST = 56 * 2**20


def dot(a, b):
    return jnp.dot(a, b, preferred_element_type=F32)


def dot_nt(a, b):
    return lax.dot_general(a, b, (((1,), (1,)), ((), ())), preferred_element_type=F32)


def dot_tn(a, b):
    return lax.dot_general(a, b, (((0,), (0,)), ((), ())), preferred_element_type=F32)


def pair_slots(route, capacity):
    route_hot = (route[:, :, None] == jnp.arange(CHOICES, dtype=jnp.int32)).astype(F32)
    seq_index = jnp.arange(SEQ)
    before = (seq_index[:, None] > seq_index[None, :]).astype(BF)
    earlier = dot(before, jnp.sum(route_hot, axis=1).astype(BF))
    slot_rank = jnp.sum(earlier[:, None, :] * route_hot, axis=-1)
    cap_limit = jnp.sum(route_hot[:, :, :EXPERTS] * capacity.astype(F32), axis=-1)
    kept_pairs = (route < EXPERTS) & (slot_rank < cap_limit)
    return jnp.where(kept_pairs, route * CAP + slot_rank.astype(jnp.int32), -1)


HALF = SEQ // 2
FORWARD_LASTS = 100
PAIRS = HEADS // 2


def lanes(rows):
    return lax.broadcasted_iota(jnp.int32, (rows, 128), 1)


def swap_halves(v):
    low = lanes(v.shape[0]) % HEAD_DIM < HEAD_DIM // 2
    return jnp.where(low, pltpu.roll(v, 128 - HEAD_DIM // 2, 1), pltpu.roll(v, HEAD_DIM // 2, 1))


def row_mean(v):
    return jnp.sum(v, axis=1, keepdims=True) * (1.0 / D)


def head_masks():
    low = lax.broadcasted_iota(jnp.int32, (1, 128), 1) < HEAD_DIM
    return (jnp.where(low, 1.0, 0.0).astype(BF), jnp.where(low, 0.0, 1.0).astype(BF))


def forward_body(
    tok, cot, prev, route, slot_row, seg_col, seg_row, cos, sin, w_qkv, w_out, w_small, vecs,
    sent, qkv, att, resid, lse_out, aux, act, bias, tg0, tg1, lse,
):
    gain_one, gain_two = vecs[0:1, :], vecs[1:2, :]
    for r in range(2):
        rows = slice(r * HALF, (r + 1) * HALF)
        x = tok[rows, :].astype(F32)
        act[rows, :] = (x * lax.rsqrt(row_mean(x * x) + EPSILON) * gain_one).astype(BF)
        qi = lax.broadcasted_iota(jnp.int32, (HALF, SEQ), 0) + r * HALF
        ki = lax.broadcasted_iota(jnp.int32, (HALF, SEQ), 1)
        ok = (qi >= ki) & (seg_col[rows, :] == seg_row[...])
        bias[rows, :] = jnp.where(ok, 0.0, FLOOR_SCORE)
    for block in range(9):
        part = dot(act[...], w_qkv[:, block * 256 : block * 256 + 256])
        for i in range(2):
            v = part[:, i * 128 : i * 128 + 128]
            if block < 6:
                v = v * cos[...] + swap_halves(v) * sin[...]
            if block < 3:
                v = v * (1.0 / math.sqrt(HEAD_DIM))
            at = block * 256 + i * 128
            qkv[:, at : at + 128] = v.astype(BF)
    masks = head_masks()

    def pair(p, carry):
        q = qkv[:, pl.ds(pl.multiple_of(p * 128, 128), 128)]
        k = qkv[:, pl.ds(pl.multiple_of(D + p * 128, 128), 128)]
        v = qkv[:, pl.ds(pl.multiple_of(2 * D + p * 128, 128), 128)]
        for b in range(2):
            rows, reach = slice(b * HALF, (b + 1) * HALF), (b + 1) * HALF
            out = None
            for h in range(2):
                s = dot_nt(q[rows, :] * masks[h], k[:reach, :]) + bias[rows, :reach]
                top = jnp.max(s, axis=1, keepdims=True)
                e = jnp.exp(s - top)
                total = jnp.sum(e, axis=1, keepdims=True)
                o = dot((e * (1.0 / total)).astype(BF), v[:reach, :] * masks[h])
                out = o if out is None else out + o
                lse[rows, :] = jnp.where(lanes(HALF) == 2 * p + h, top + jnp.log(total), lse[rows, :])
            att[rows, pl.ds(pl.multiple_of(p * 128, 128), 128)] = out.astype(BF)
        return carry

    lax.fori_loop(0, PAIRS, pair, 0)
    lse_out[...] = lse[...].T[:16, :]
    lane = lanes(HALF)

    def column(v, at):
        return jnp.sum(jnp.where(lane == at, v, 0.0), axis=1, keepdims=True)

    for r in range(2):
        rows = slice(r * HALF, (r + 1) * HALF)
        res = tok[rows, :].astype(F32) + dot(att[rows, :], w_out[...])
        resid[rows, :] = res
        act2 = (res * lax.rsqrt(row_mean(res * res) + EPSILON) * gain_two).astype(BF)
        act[rows, :] = act2
        logits = dot(act2, w_small[...])
        router = logits + prev[rows, :].astype(F32)
        r0, r1 = column(router, route[rows, 0:1]), column(router, route[rows, 1:2])
        top = jnp.maximum(r0, r1)
        e0, e1 = jnp.exp(r0 - top), jnp.exp(r1 - top)
        g0, g1 = e0 / (e0 + e1), e1 / (e0 + e1)
        made = jnp.where(lane == 0, g0, jnp.where(lane == 1, g1, 0.0))
        for c in range(2):
            a, b = column(logits, CHOICES + 2 * c), column(logits, CHOICES + 2 * c + 1)
            top = jnp.maximum(a, b)
            ea, eb = jnp.exp(a - top), jnp.exp(b - top)
            made = jnp.where(lane == 2 + 2 * c, ea / (ea + eb), made)
            made = jnp.where(lane == 3 + 2 * c, eb / (ea + eb), made)
        aux[rows, :] = made
        g = cot[rows, :].astype(F32)
        tg0[rows, :] = (g0 * g).astype(BF)
        tg1[rows, :] = (g1 * g).astype(BF)

    def dispatch(b, carry):
        ids = lax.broadcasted_iota(jnp.int32, (256, SEQ), 0) + b * 256
        p0 = jnp.where(slot_row[0:1, :] == ids, 1.0, 0.0)
        p1 = jnp.where(slot_row[1:2, :] == ids, 1.0, 0.0)
        sent[pl.ds(b * 2, 2), 0] = dot((p0 + p1).astype(BF), act[...]).astype(BF).reshape(2, CAP, D)
        sg = dot(p0.astype(BF), tg0[...]) + dot(p1.astype(BF), tg1[...])
        sent[pl.ds(b * 2, 2), 1] = sg.astype(BF).reshape(2, CAP, D)
        return carry

    lax.fori_loop(0, SLOTS // 256, dispatch, 0)


def seq_block(width, part, col=0):
    return pl.BlockSpec((SEQ, width), lambda i, part=part, col=col: (part, col))


def fixed(shape, *at):
    at = at or (0,) * len(shape)
    return pl.BlockSpec(shape, lambda i, at=at: at)


def lasting(microseconds):
    return pl.CostEstimate(flops=microseconds * 10**9, bytes_accessed=0, transcendentals=0)


def kernel_params():
    return pltpu.CompilerParams(dimension_semantics=("arbitrary",), vmem_limit_bytes=VMEM_MOST)


def forward_part(part, t, packed, vecs):
    return pl.pallas_call(
        forward_body,
        grid=(1,),
        in_specs=[
            seq_block(D, part), seq_block(D, part), seq_block(128, part), seq_block(2, part),
            fixed((None, 2, SEQ), part, 0, 0), seq_block(1, part), fixed((None, 1, SEQ), part, 0, 0),
            seq_block(128, part), seq_block(128, part),
            fixed((D, 3 * D), 0, 0), fixed((D, D), 0, 3), fixed((D, 128), 0, 24), fixed((8, D)),
        ],
        out_specs=[
            fixed((EXPERTS, 2, CAP, D)), fixed((SEQ, 3 * D)), fixed((SEQ, D)), fixed((SEQ, D)),
            fixed((16, SEQ)), fixed((SEQ, 128)),
        ],
        out_shape=[
            jax.ShapeDtypeStruct((EXPERTS, 2, CAP, D), BF),
            jax.ShapeDtypeStruct((SEQ, 3 * D), BF),
            jax.ShapeDtypeStruct((SEQ, D), BF),
            jax.ShapeDtypeStruct((SEQ, D), F32),
            jax.ShapeDtypeStruct((16, SEQ), F32),
            jax.ShapeDtypeStruct((SEQ, 128), F32),
        ],
        scratch_shapes=[
            pltpu.VMEM((SEQ, D), BF), pltpu.VMEM((SEQ, SEQ), F32), pltpu.VMEM((SEQ, D), BF),
            pltpu.VMEM((SEQ, D), BF), pltpu.VMEM((SEQ, 128), F32),
        ],
        compiler_params=kernel_params(),
        cost_estimate=lasting(FORWARD_LASTS),
    )(
        t["tokens"], t["cotangent"], t["prev"], t["routes"], t["slot_row"], t["seg_col"], t["seg_row"],
        t["cos"], t["sin"], packed, packed, packed, vecs,
    )


def combine_body(
    prior, back, resid, cot, aux, slot, route, att, w_out, w_small, vecs, p_out, p_small, p_rows,
    out, rgrad, router_out, agrad, out_w, small_w, rows_w,
):
    @pl.when(pl.program_id(0) == 0)
    def _():
        if prior:
            out_w[...], small_w[...], rows_w[...] = p_out[...], p_small[...], p_rows[...]
        else:
            out_w[...] = jnp.zeros_like(out_w)
            small_w[...] = jnp.zeros_like(small_w)
            rows_w[...] = jnp.zeros_like(rows_w)

    gain_two = vecs[1:2, :]
    consts = (vecs[2:3, :], vecs[3:4, :])
    res = resid[...]
    g = cot[...].astype(F32)
    inverse = lax.rsqrt(row_mean(res * res) + EPSILON)
    unit = res * inverse
    normed = unit * gain_two
    lane = lanes(HALF)
    gates = (aux[:, 0:1], aux[:, 1:2])
    cg = ((aux[:, 2:3], aux[:, 3:4]), (aux[:, 4:5], aux[:, 5:6]))
    ids = lax.broadcasted_iota(jnp.int32, (HALF, SLOTS), 1)
    picks = [jnp.where(slot[:, k : k + 1] == ids, 1.0, 0.0) for k in range(2)]
    rows = back[:, 0].reshape(SLOTS, D)
    g_normed = jnp.sum(g * normed, axis=1, keepdims=True)
    g_const = [jnp.sum(g * v, axis=1, keepdims=True) for v in consts]
    gate_grads, straight, total = [], 0.0, res
    const_mask = [
        [jnp.where(route[:, k : k + 1] == EXPERTS + 2 + c, 1.0, 0.0) for c in range(2)] for k in range(2)
    ]
    for k in range(2):
        combined = dot(picks[k].astype(BF), rows)
        direct = jnp.where(route[:, k : k + 1] == EXPERTS + 1, 1.0, 0.0)
        for c in range(2):
            direct += const_mask[k][c] * cg[c][0]
        grad = jnp.sum(g * combined, axis=1, keepdims=True) + direct * g_normed
        for c in range(2):
            grad += const_mask[k][c] * cg[c][1] * g_const[c]
        gate_grads.append(grad)
        straight += gates[k] * direct
        total = total + gates[k] * combined
    total = total + straight * normed
    logit_grad = 0.0
    made = [jnp.zeros((1, D), F32)] * 2
    for c in range(2):
        share = const_mask[0][c] * gates[0] + const_mask[1][c] * gates[1]
        weight = share * cg[c][1]
        total = total + weight * consts[c]
        made[c] = jnp.sum(weight * g, axis=0, keepdims=True)
        first, second = share * g_normed, share * g_const[c]
        inner = cg[c][0] * first + cg[c][1] * second
        for i, v in enumerate((first, second)):
            logit_grad += jnp.where(lane == CHOICES + 2 * c + i, cg[c][i] * (v - inner), 0.0)
    out[...] = total.astype(BF)
    mean_grad = gates[0] * gate_grads[0] + gates[1] * gate_grads[1]
    router = 0.0
    for k in range(2):
        router += jnp.where(lane == route[:, k : k + 1], gates[k] * (gate_grads[k] - mean_grad), 0.0)
    router_out[...] = router[:, :CHOICES]
    logit_low = (router + logit_grad).astype(BF)
    small_w[...] += dot_tn(normed.astype(BF), logit_low)
    normed_grad = dot_nt(logit_low, w_small[...])
    normed_grad += dot((picks[0] + picks[1]).astype(BF), back[:, 1].reshape(SLOTS, D))
    normed_grad += straight * g
    scaled = normed_grad * gain_two
    gain_grad = jnp.sum(normed_grad * unit, axis=0, keepdims=True)
    residual_grad = g + inverse * (scaled - unit * row_mean(scaled * unit))
    rgrad[...] = residual_grad
    low = residual_grad.astype(BF)
    agrad[...] = dot_nt(low, w_out[...]).astype(BF)
    out_w[...] += dot_tn(att[...], low)
    rows_w[0:1, :] += made[0]
    rows_w[1:2, :] += made[1]
    rows_w[2:3, :] += gain_grad


def combine_part(part, back, kept, t, packed, vecs, prior):
    _, _, att, resid, _, aux = kept

    def tile(width, mine=True):
        base = 0 if mine else 2 * part
        return pl.BlockSpec((HALF, width), lambda i, base=base: (base + i, 0))

    sums = [
        jax.ShapeDtypeStruct((D, D), F32), jax.ShapeDtypeStruct((D, 128), F32), jax.ShapeDtypeStruct((8, D), F32)
    ]
    sum_specs = [fixed((D, D)), fixed((D, 128)), fixed((8, D))]
    body = functools.partial(combine_body, prior is not None)
    if prior is None:
        given = []

        def body(*refs):
            combine_body(False, *refs[:10], None, None, None, *refs[10:])

    else:
        given = list(prior)
    return pl.pallas_call(
        body,
        grid=(2,),
        in_specs=[
            fixed((EXPERTS, 2, CAP, D)), tile(D), tile(D, False), tile(128), tile(2, False), tile(2, False),
            tile(D), fixed((D, D), 0, 3), fixed((D, 128), 0, 24), fixed((8, D)),
        ] + (sum_specs if given else []),
        out_specs=[tile(D), tile(D), tile(CHOICES), tile(D)] + sum_specs,
        out_shape=[
            jax.ShapeDtypeStruct((SEQ, D), BF), jax.ShapeDtypeStruct((SEQ, D), F32),
            jax.ShapeDtypeStruct((SEQ, CHOICES), F32), jax.ShapeDtypeStruct((SEQ, D), BF),
        ] + sums,
        compiler_params=kernel_params(),
        cost_estimate=lasting(1),
    )(back, resid, t["cotangent"], aux, t["slots"], t["routes"], att, packed, packed, vecs, *given)


def attention_back_body(
    qkv, agrad, lse, seg_col, seg_row, cos, sin, w_qkv, tok, vecs, rgrad, grad_in, qkv_grad, act, gain_w, bias
):
    for b in range(2):
        rows = slice(b * HALF, (b + 1) * HALF)
        ki = lax.broadcasted_iota(jnp.int32, (HALF, SEQ), 0) + b * HALF
        qi = lax.broadcasted_iota(jnp.int32, (HALF, SEQ), 1)
        ok = (qi >= ki) & (seg_col[rows, :] == seg_row[...])
        bias[rows, :] = jnp.where(ok, 0.0, FLOOR_SCORE)
    masks = head_masks()
    scale = 1.0 / math.sqrt(HEAD_DIM)

    def one_pair(p, carry):
        at = [pl.ds(pl.multiple_of(i * D + p * 128, 128), 128) for i in range(3)]
        q, k, v = [qkv[:, a] for a in at]
        da = agrad[:, at[0]]
        kg, vg, qg = [None, None], [None, None], [None, None]

        def add(store, i, value):
            store[i] = value if store[i] is None else store[i] + value

        for h in range(2):
            qh, dh = q * masks[h], da * masks[h]
            probs, grads, keyed = [], [], []
            for b in range(2):
                keys, first = slice(b * HALF, (b + 1) * HALF), b * HALF
                kh = k[keys, :] * masks[h]
                st = dot_nt(kh, q[first:, :]) + bias[keys, first:]
                probs.append(jnp.exp(st - lse[pl.ds(2 * p + h, 1), first:]))
                grads.append(dot_nt(v[keys, :] * masks[h], da[first:, :]))
                keyed.append(kh)
            inner = [jnp.sum(probs[b] * grads[b], axis=0, keepdims=True) for b in range(2)]
            late = inner[0][:, HALF:] + inner[1]
            whole = jnp.concatenate([inner[0][:, :HALF], late], axis=1)
            for b, mean in enumerate((whole, late)):
                first = b * HALF
                ds = (probs[b] * (grads[b] - mean)).astype(BF)
                add(kg, b, dot(ds, qh[first:, :]))
                add(vg, b, dot(probs[b].astype(BF), dh[first:, :]))
                full = dot_tn(ds, keyed[b])
                if b == 0:
                    add(qg, 0, full[:HALF, :])
                    add(qg, 1, full[HALF:, :])
                else:
                    add(qg, 1, full)
        for b in range(2):
            rows = slice(b * HALF, (b + 1) * HALF)
            c, s = cos[rows, :], sin[rows, :]
            qb = qg[b] * scale
            qkv_grad[rows, at[0]] = (qb * c - swap_halves(qb) * s).astype(BF)
            qkv_grad[rows, at[1]] = (kg[b] * c - swap_halves(kg[b]) * s).astype(BF)
            qkv_grad[rows, at[2]] = vg[b].astype(BF)
        return carry

    lax.fori_loop(0, PAIRS, one_pair, 0)
    gain_one = vecs[0:1, :]
    gain_grad = 0.0
    for b in range(2):
        rows = slice(b * HALF, (b + 1) * HALF)
        x = tok[rows, :].astype(F32)
        inverse = lax.rsqrt(row_mean(x * x) + EPSILON)
        unit = x * inverse
        act[rows, :] = (unit * gain_one).astype(BF)
        grad = dot_nt(qkv_grad[rows, :], w_qkv[...])
        scaled = grad * gain_one
        gain_grad += jnp.sum(grad * unit, axis=0, keepdims=True)
        grad_in[rows, :] = rgrad[rows, :] + inverse * (scaled - unit * row_mean(scaled * unit))
    gain_w[...] = jnp.broadcast_to(gain_grad, gain_w.shape)


def attention_back(part, kept, rgrad, agrad, t, packed, vecs):
    _, qkv, _, _, lse, _ = kept
    return pl.pallas_call(
        attention_back_body,
        grid=(1,),
        in_specs=[
            fixed((SEQ, 3 * D)), fixed((SEQ, D)), fixed((16, SEQ)),
            seq_block(1, part), fixed((None, 1, SEQ), part, 0, 0), seq_block(128, part), seq_block(128, part),
            fixed((D, 3 * D), 0, 0), seq_block(D, part), fixed((8, D)), fixed((SEQ, D)),
        ],
        out_specs=[fixed((SEQ, D)), fixed((SEQ, 3 * D)), fixed((SEQ, D)), fixed((8, D))],
        out_shape=[
            jax.ShapeDtypeStruct((SEQ, D), F32), jax.ShapeDtypeStruct((SEQ, 3 * D), BF),
            jax.ShapeDtypeStruct((SEQ, D), BF), jax.ShapeDtypeStruct((8, D), F32),
        ],
        scratch_shapes=[pltpu.VMEM((SEQ, SEQ), F32)],
        compiler_params=kernel_params(),
        cost_estimate=lasting(1),
    )(
        qkv, agrad, lse, t["seg_col"], t["seg_row"], t["cos"], t["sin"], packed, t["tokens"], vecs, rgrad
    )


def qkv_wgrad_body(parts, *refs):
    acts, grads, out, turned = refs[:parts], refs[parts : 2 * parts], refs[2 * parts], refs[2 * parts + 1]

    @pl.when(pl.program_id(0) == 0)
    def _():
        for i in range(parts):
            turned[:, i * SEQ : (i + 1) * SEQ] = acts[i][...].T

    out[...] = dot(turned[...], jnp.concatenate([v[...] for v in grads], axis=0)).astype(BF)


def qkv_wgrad(acts, grads):
    parts = len(acts)
    return pl.pallas_call(
        functools.partial(qkv_wgrad_body, parts),
        grid=(3,),
        in_specs=[fixed((SEQ, D))] * parts + [pl.BlockSpec((SEQ, D), lambda i: (0, i))] * parts,
        out_specs=pl.BlockSpec((D, D), lambda i: (0, i)),
        out_shape=jax.ShapeDtypeStruct((D, 3 * D), BF),
        scratch_shapes=[pltpu.VMEM((D, parts * SEQ), BF)],
        compiler_params=kernel_params(),
        cost_estimate=lasting(1),
    )(*acts, *grads)


def tables(tokens, cotangent, prev_logits, routes, capacity, segments, positions):
    parts = tokens.shape[0] // SEQ
    slots = jnp.concatenate(
        [pair_slots(routes[i * SEQ : (i + 1) * SEQ], capacity) for i in range(parts)]
    )
    lane = jnp.arange(128) % HEAD_DIM
    frequency = jnp.exp((lane % (HEAD_DIM // 2)).astype(F32) * (-2.0 * math.log(ROPE_BASE) / HEAD_DIM))
    angles = positions.astype(F32)[:, None] * frequency[None, :]
    sign = jnp.where(lane < HEAD_DIM // 2, -1.0, 1.0)
    return dict(
        tokens=tokens,
        cotangent=cotangent,
        prev=jnp.pad(prev_logits, ((0, 0), (0, 128 - CHOICES))),
        routes=routes,
        slots=slots,
        slot_row=slots.reshape(parts, SEQ, 2).transpose(0, 2, 1),
        seg_col=segments[:, None],
        seg_row=segments.reshape(parts, 1, SEQ),
        cos=jnp.cos(angles),
        sin=jnp.sin(angles) * sign,
    )


FC = 512


def expert_rows_body(x_ref, g_ref, wg_ref, wu_ref, wd_ref, hid_ref, dg_ref, du_ref, out_ref, acc, racc):
    step = pl.program_id(0)
    x = x_ref[:, 0].reshape(-1, D)
    g = g_ref[:, 0].reshape(-1, D)
    wg, wu, wd = wg_ref[...], wu_ref[...], wd_ref[...]
    gate = dot(x, wg)
    up = dot(x, wu)
    hgrad = dot_nt(g, wd).astype(BF).astype(F32)
    sig = 1.0 / (1.0 + jnp.exp(-gate))
    act = gate * sig
    hidden = (act * up).astype(BF)
    dgate = (hgrad * up * sig * (1.0 + gate * (1.0 - sig))).astype(BF)
    dup = (hgrad * act).astype(BF)
    hid_ref[...] = hidden
    dg_ref[...] = dgate
    du_ref[...] = dup
    prod = dot(hidden, wd)
    rgrad = dot_nt(dgate, wg) + dot_nt(dup, wu)

    @pl.when(step == 0)
    def _():
        acc[...] = prod
        racc[...] = rgrad

    @pl.when(step > 0)
    def _():
        acc[...] += prod
        racc[...] += rgrad

    @pl.when(step == pl.num_programs(0) - 1)
    def _():
        out_ref[:, 0] = acc[...].astype(BF).reshape(-1, CAP, D)
        out_ref[:, 1] = racc[...].astype(BF).reshape(-1, CAP, D)


def expert_rows(received, w_gate_up, w_down):
    n = received.shape[0]
    rows = n * CAP
    steps = FF // FC
    wide = jax.ShapeDtypeStruct((rows, FF), BF)
    block = pl.BlockSpec((rows, FC), lambda j: (0, j))
    return pl.pallas_call(
        expert_rows_body,
        grid=(steps,),
        in_specs=[
            pl.BlockSpec((n, 1, CAP, D), lambda j: (0, 0, 0, 0)),
            pl.BlockSpec((n, 1, CAP, D), lambda j: (0, 1, 0, 0)),
            pl.BlockSpec((D, FC), lambda j: (0, j)),
            pl.BlockSpec((D, FC), lambda j: (0, steps + j)),
            pl.BlockSpec((FC, D), lambda j: (j, 0)),
        ],
        out_specs=[block, block, block, pl.BlockSpec((n, 2, CAP, D), lambda j: (0, 0, 0, 0))],
        out_shape=[wide, wide, wide, jax.ShapeDtypeStruct((n, 2, CAP, D), BF)],
        scratch_shapes=[pltpu.VMEM((rows, D), F32), pltpu.VMEM((rows, D), F32)],
        compiler_params=pltpu.CompilerParams(
            dimension_semantics=("arbitrary",), vmem_limit_bytes=VMEM_MOST
        ),
        cost_estimate=lasting(28),
    )(received, received, w_gate_up, w_gate_up, w_down)


FW = 512


def down_wgrad_body(parts, *refs):
    hid, received, out = refs[:parts], refs[parts : 2 * parts], refs[2 * parts]
    rows = jnp.concatenate([v[:, 0].reshape(-1, D) for v in received], axis=0)
    out[...] = dot_tn(jnp.concatenate([v[...] for v in hid], axis=0), rows).astype(BF)


def down_wgrad(received, hid):
    parts, (n, _, _, _) = len(received), received[0].shape
    return pl.pallas_call(
        functools.partial(down_wgrad_body, parts),
        grid=(FF // FW,),
        in_specs=[pl.BlockSpec((n * CAP, FW), lambda j: (0, j))] * parts
        + [pl.BlockSpec((n, 1, CAP, D), lambda j: (0, 1, 0, 0))] * parts,
        out_specs=pl.BlockSpec((FW, D), lambda j: (j, 0)),
        out_shape=jax.ShapeDtypeStruct((FF, D), BF),
        compiler_params=kernel_params(),
        cost_estimate=lasting(10),
    )(*hid, *received)


def gate_up_wgrad_body(parts, *refs):
    received, dg, du = refs[:parts], refs[parts : 2 * parts], refs[2 * parts : 3 * parts]
    out, xt = refs[3 * parts :]
    rows = received[0].shape[0] * CAP

    @pl.when(pl.program_id(0) == 0)
    def _():
        for i in range(parts):
            xt[:, i * rows : (i + 1) * rows] = received[i][:, 0].reshape(rows, D).T

    for k, grads in enumerate((dg, du)):
        out[k] = dot(xt[...], jnp.concatenate([v[...] for v in grads], axis=0)).astype(BF)


def gate_up_wgrad(received, dg, du):
    parts, (n, _, _, _) = len(received), received[0].shape
    return pl.pallas_call(
        functools.partial(gate_up_wgrad_body, parts),
        grid=(FF // FW,),
        in_specs=[pl.BlockSpec((n, 1, CAP, D), lambda j: (0, 0, 0, 0))] * parts
        + [pl.BlockSpec((n * CAP, FW), lambda j: (0, j))] * (2 * parts),
        out_specs=pl.BlockSpec((2, D, FW), lambda j: (0, 0, j)),
        out_shape=jax.ShapeDtypeStruct((2, D, FF), BF),
        scratch_shapes=[pltpu.VMEM((D, parts * n * CAP), BF)],
        compiler_params=kernel_params(),
        cost_estimate=lasting(20),
    )(*received, *dg, *du)


def place_body(spots, count, *refs):
    offsets, blocks, outs, sems = refs[0], refs[1 : 1 + count], refs[1 + count : -1], refs[-1]
    copies = []
    for i, (block, first, rows, out, column) in enumerate(spots):
        width = blocks[block].shape[1]
        start = pl.multiple_of(offsets[2 * i], 16)
        across = pl.ds(pl.multiple_of(offsets[2 * i + 1], 128), width) if column else pl.ds(0, width)
        copies.append(
            pltpu.make_async_copy(
                blocks[block].at[pl.ds(first, rows), :], outs[out].at[pl.ds(start, rows), across], sems.at[i]
            )
        )
    for copy in copies:
        copy.start()
    for copy in copies:
        copy.wait()


def place(blocks, spots, offsets, shapes):
    size = sum(math.prod(v) for v in shapes) * 4
    anywhere = pl.BlockSpec(memory_space=pl.ANY)
    return pl.pallas_call(
        functools.partial(place_body, spots, len(blocks)),
        in_specs=[pl.BlockSpec(memory_space=pltpu.SMEM)] + [anywhere] * len(blocks),
        out_specs=[pl.BlockSpec(memory_space=pltpu.VMEM)] * len(shapes),
        out_shape=[jax.ShapeDtypeStruct(v, BF) for v in shapes],
        scratch_shapes=[pltpu.SemaphoreType.DMA((len(spots),))],
        compiler_params=pltpu.CompilerParams(vmem_limit_bytes=VMEM_MOST),
        cost_estimate=lasting(size // 2**20),
    )(jnp.stack(offsets).astype(jnp.int32), *blocks)


def pick(value, index, axis=0):
    return lax.dynamic_index_in_dim(value, index, axis, False)


def added(*values):
    return sum(v.astype(F32) for v in values).astype(BF)


class Paired:
    axes = ("half", "low", "inner", "side", "core")
    fsdp = ("half", "low", "inner")
    expert = ("side", "core")
    rows = ("side", "low", "inner")
    route_axes = ("half", "low", "inner", "core")
    near = 896

    def __init__(self, mesh):
        self.mesh = Mesh(mesh.devices.reshape(2, 2, 2, 2, 2), self.axes)
        self.routes = []
        for turn in range(4):
            pairs = []
            for z in range(4):
                for y in range(2):
                    for c in range(2):
                        half, inner = (z ^ turn) >> 1, (z ^ turn) & 1
                        pairs.append(((z * 2 + y) * 2 + c, ((half * 2 + c) * 2 + inner) * 2 + y))
            self.routes.append(pairs)

    @staticmethod
    def swap(value, axis="core"):
        return lax.ppermute(value, axis, [(0, 1), (1, 0)])

    @staticmethod
    def along(value, turn):
        return lax.ppermute(value, ("half", "low"), [(i, i ^ turn) for i in range(4)])

    @staticmethod
    def spot():
        z = lax.axis_index("half") * 2 + lax.axis_index("low")
        return z, lax.axis_index("inner"), lax.axis_index("side"), lax.axis_index("core")

    def send(self, weights, which, turn):
        mine = pick(weights[which], (self.spot()[0] ^ turn) & 1)
        return lax.ppermute(mine, self.route_axes, self.routes[turn])

    def gather_shared(self, shard, weights, early):
        z, y, x, c = self.spot()
        rows, width = shard.shape
        rows, width = rows // 2, width // 2
        mine = lax.dynamic_slice(shard, (c * rows, x * width), (rows, width))
        stack = jnp.concatenate([mine] + [self.along(mine, turn) for turn in (1, 2, 3)])
        stack, weights, early = lax.optimization_barrier((stack, weights, early))
        sent = {(0, 2): self.send(weights, 0, 2)}
        over_y, over_x = self.swap(stack, "inner"), self.swap(stack, "side")
        far = self.swap(over_y[:, : self.near], "side"), self.swap(over_x[:, self.near :], "inner")
        blocks = [stack, over_y, over_x, *far]
        flips = [(0, 0, 0), (1, 0, 0), (0, 1, 0), (1, 1, 0), (1, 1, self.near)]
        spots, offsets = [], []
        for i, (dy, dx, column) in enumerate(flips + flips):
            core = c if i < len(flips) else 1 - c
            for turn in range(4):
                spots.append((i, turn * rows, rows, 0, True))
                offsets += [((z ^ turn) * 2 + (y ^ dy)) * 2 * rows + core * rows, (x ^ dx) * width + column]
        blocks += [self.swap(v) for v in blocks]
        blocks, weights, sent = lax.optimization_barrier((blocks, weights, sent))
        [full] = place(blocks, spots, offsets, [(16 * rows, 2 * width)])
        return full, early, (weights, sent)

    def gather_more(self, held, value, names):
        weights, sent = held
        more = [self.send(weights, *v) for v in names]
        value, weights, more = lax.optimization_barrier((value, weights, more))
        return (weights, {**sent, **dict(zip(names, more))}), value

    def reduce_shared(self, total):
        z, y, x, c = self.spot()
        rows, width = total.shape[0] // 16, total.shape[1] // 2
        near = (width // 128 + 1) // 2 * 128
        total = total.reshape(4, 2, 2, rows, 2 * width)
        total = added(pick(total, c, 2), self.swap(pick(total, 1 - c, 2)))
        parts = total.reshape(4, 2, rows, 2, width)
        one, two = parts[..., :near], parts[..., near:]
        one = added(pick(one, x, 3), self.swap(pick(one, 1 - x, 3), "side"))
        two = added(pick(two, y, 1), self.swap(pick(two, 1 - y, 1), "inner"))
        one = added(pick(one, y, 1), self.swap(pick(one, 1 - y, 1), "inner"))
        two = added(pick(two, x, 2), self.swap(pick(two, 1 - x, 2), "side"))
        both = jnp.concatenate([one, two], axis=2)
        mine = added(pick(both, z), *[self.along(pick(both, z ^ turn), turn) for turn in (1, 2, 3)])
        other = self.swap(mine, "side")
        line = jnp.where(x == 0, jnp.concatenate([mine, other], 1), jnp.concatenate([other, mine], 1))
        other = self.swap(line)
        both = jnp.where(c == 0, jnp.concatenate([line, other]), jnp.concatenate([other, line]))
        return both.astype(F32)

    def gather_expert(self, held):
        weights, sent = held
        c = lax.axis_index("core")
        here = lax.axis_index("half") * 2 + lax.axis_index("inner")
        names = [(which, turn) for which in range(2) for turn in range(4)]
        own = [sent[v] if v in sent else self.send(weights, *v) for v in names]
        blocks = own + [self.swap(v) for v in own]
        spots, offsets = [], []
        for i, block in enumerate(blocks):
            which, turn = i % len(own) // 4, i % 4
            rows = block.shape[0]
            core = c if i < len(own) else 1 - c
            spots.append((i, 0, rows, which, False))
            offsets += [((here ^ turn) * 2 + core) * rows, jnp.int32(0)]
        return place(blocks, spots, offsets, [(8 * w.shape[1], w.shape[2]) for w in weights])

    def scatter_start(self, grad, axis):
        c = lax.axis_index("core")
        shape = grad.shape
        grad = grad.reshape(shape[:axis] + (4, 2, shape[axis] // 8) + shape[axis + 1 :])
        return added(pick(grad, c, axis + 1), self.swap(pick(grad, 1 - c, axis + 1)))

    def scatter_send(self, parts, axis):
        here = lax.axis_index("half") * 2 + lax.axis_index("inner")
        got = {}
        for turn in (2, 3, 0, 1):
            back = [(b, a) for a, b in self.routes[turn]]
            got[turn] = lax.ppermute(pick(parts, here ^ turn, axis), self.route_axes, back)
        return got

    def scatter_end(self, got, axis):
        even = (self.spot()[0] & 1) == 0
        first, second = [got[i].astype(F32) + got[i + 2].astype(F32) for i in range(2)]
        return jnp.stack([jnp.where(even, first, second), jnp.where(even, second, first)])


class Plain:
    axes = ("outer", "inner", "expert")
    fsdp = ("outer", "inner")
    expert = ("expert",)
    rows = ("expert", "inner")

    def __init__(self, mesh):
        fsdp, expert = mesh.shape["fsdp"], mesh.shape["expert"]
        inner = EXPERTS // expert
        self.mesh = Mesh(mesh.devices.reshape(fsdp // inner, inner, expert), self.axes)

    def gather_shared(self, shard, weights, early):
        return lax.all_gather(shard, self.fsdp, axis=0, tiled=True), early, weights

    def gather_more(self, held, value, names):
        return held, value

    def reduce_shared(self, total):
        total = lax.psum_scatter(total, self.axes, scatter_dimension=0, tiled=True)
        return lax.all_gather(total, self.expert, axis=0, tiled=True).astype(F32)

    def gather_expert(self, weights):
        full = []
        for weight in weights:
            own = lax.all_to_all(weight, "inner", 0, 0, tiled=True)
            own = lax.all_gather(own, "outer", axis=0, tiled=True)
            full.append(own.reshape((-1,) + weight.shape[2:]))
        return full

    def scatter_start(self, grad, axis):
        return grad

    def scatter_send(self, grad, axis):
        return grad

    def scatter_end(self, grad, axis):
        inner = lax.axis_size("inner")
        part = lax.psum_scatter(grad, "outer", scatter_dimension=axis, tiled=True)
        shape = part.shape
        part = part.reshape(shape[:axis] + (inner, shape[axis] // inner) + shape[axis + 1 :])
        part = jnp.moveaxis(part, axis, 0)
        return lax.all_to_all(part, "inner", 0, 0, tiled=True).astype(F32)


def solution(mesh):
    plan = Paired(mesh) if (mesh.shape["fsdp"], mesh.shape["expert"]) == (8, 4) else Plain(mesh)

    def on_device(
        tokens, cotangent, prev_logits, routes, capacity, segments, positions,
        w_qkv, w_out, gate_matrix, const_values, attn_gain, moe_gain, w_gate_up, w_down,
    ):
        rows = w_qkv.shape[0]
        pad = jnp.zeros((rows, 256 - 20), BF)
        small = jnp.concatenate(
            [gate_matrix, const_values, attn_gain[:, None], moe_gain[:, None], pad], axis=1
        )
        shard = jnp.concatenate([w_qkv, w_out, small], axis=1)
        t = tables(tokens, cotangent, prev_logits, routes, capacity, segments, positions)
        packed, t, held = plan.gather_shared(shard, (w_gate_up, w_down), t)
        columns = packed[:, 4 * D + 16 : 4 * D + 20].astype(F32).T
        vecs = jnp.concatenate([columns[2:], columns[:2], jnp.zeros((4, D), F32)])
        parts = tokens.shape[0] // SEQ
        kept, shared = [], packed
        for i in range(parts):
            if i == 1:
                held, shared = plan.gather_more(held, packed, ((1, 2), (1, 3)))
            kept.append(forward_part(i, t, shared, vecs))
        sends = [k[0] for k in kept]
        held, sends[-1] = plan.gather_more(held, sends[-1], ((0, 3), (0, 0)))
        gate_up_full, down_full = plan.gather_expert(held)
        received = [lax.all_to_all(v, plan.rows, 0, 0, tiled=True) for v in sends]
        made = [expert_rows(r, gate_up_full, down_full) for r in received]
        returned = [lax.all_to_all(m[3], plan.rows, 0, 0, tiled=True) for m in made]
        hid, dg, du = [[m[i] for m in made] for i in range(3)]
        started = plan.scatter_start(down_wgrad(received, hid), 0)
        dg, started = lax.optimization_barrier((dg, started))
        down_got = plan.scatter_send(started, 0)
        started = plan.scatter_start(gate_up_wgrad(received, dg, du), 1)
        firsts, lasts, sums = [], [], None
        for i in range(parts):
            *first, out_w, small_w, rows_w = combine_part(i, returned[i], kept[i], t, packed, vecs, sums)
            sums = (out_w, small_w, rows_w)
            if i == 0:
                first[1], started, down_got = lax.optimization_barrier((first[1], started, down_got))
                down_total = plan.scatter_end(down_got, 0)
                gate_up_got = plan.scatter_send(started, 1)
            firsts.append(first)
            lasts.append(attention_back(i, kept[i], first[1], first[3], t, packed, vecs))
        out_w = plan.reduce_shared(sums[0].astype(BF))
        qkv_w = qkv_wgrad([v[2] for v in lasts], [v[1] for v in lasts])
        gate_up_got, _ = lax.optimization_barrier((gate_up_got, qkv_w))
        gate_up_total = plan.scatter_end(gate_up_got, 1)
        gate_up_total = jnp.concatenate([gate_up_total[:, 0], gate_up_total[:, 1]], axis=2)
        gain_one_grad = sum(v[3][0] for v in lasts)
        row_sums = jnp.concatenate([sums[2][:2], gain_one_grad[None], sums[2][2:3]])
        small_sum = jnp.concatenate(
            [sums[1][:, :16], row_sums.T, jnp.zeros((D, 256 - 20), F32)], axis=1
        )
        total = plan.reduce_shared(jnp.concatenate([qkv_w, small_sum.astype(BF)], axis=1))
        return (
            jnp.concatenate([v[0] for v in firsts]),
            jnp.concatenate([v[0] for v in lasts]),
            jnp.concatenate([v[2] for v in firsts]),
            total[:, : 3 * D],
            out_w,
            total[:, 3 * D : 3 * D + 16],
            total[:, 3 * D + 16 : 3 * D + 18],
            total[:, 3 * D + 18],
            total[:, 3 * D + 19],
            gate_up_total,
            down_total,
        )

    every = plan.fsdp + plan.expert
    split = P(every, None)
    shard = P(plan.fsdp, None)
    line = P(plan.fsdp)
    whole = P(plan.expert, plan.fsdp, None)
    return jax.shard_map(
        on_device,
        mesh=plan.mesh,
        in_specs=(
            split, split, split, split, P(), P(every), P(every),
            shard, shard, shard, shard, line, line, whole, whole,
        ),
        out_specs=(split, split, split, shard, shard, shard, shard, line, line, whole, whole),
        check_vma=False,
    )
```

```python
import functools
import math

import jax
import jax.numpy as jnp
from jax import lax
from jax.experimental import pallas as pl
from jax.experimental.pallas import tpu as pltpu
from jax.sharding import Mesh
from jax.sharding import PartitionSpec as P

D = 768
HEADS = 12
HEAD_DIM = 64
FF = 2048
EXPERTS = 8
SEQ = 512
CAP = 128
CHOICES = EXPERTS + 4
SLOTS = EXPERTS * CAP

EPSILON = 1e-05
ROPE_BASE = 10000.0
FLOOR_SCORE = -1e30
HIGHEST = lax.Precision.HIGHEST
BF = jnp.bfloat16
F32 = jnp.float32
VMEM_MOST = 56 * 2**20


def dot(a, b):
    return jnp.dot(a, b, preferred_element_type=F32)


def dot_nt(a, b):
    return lax.dot_general(a, b, (((1,), (1,)), ((), ())), preferred_element_type=F32)


def dot_tn(a, b):
    return lax.dot_general(a, b, (((0,), (0,)), ((), ())), preferred_element_type=F32)


def pair_slots(route, capacity):
    route_hot = (route[:, :, None] == jnp.arange(CHOICES, dtype=jnp.int32)).astype(F32)
    seq_index = jnp.arange(SEQ)
    before = (seq_index[:, None] > seq_index[None, :]).astype(BF)
    earlier = dot(before, jnp.sum(route_hot, axis=1).astype(BF))
    slot_rank = jnp.sum(earlier[:, None, :] * route_hot, axis=-1)
    cap_limit = jnp.sum(route_hot[:, :, :EXPERTS] * capacity.astype(F32), axis=-1)
    kept_pairs = (route < EXPERTS) & (slot_rank < cap_limit)
    return jnp.where(kept_pairs, route * CAP + slot_rank.astype(jnp.int32), -1)


HALF = SEQ // 2
PAIRS = HEADS // 2


def lanes(rows):
    return lax.broadcasted_iota(jnp.int32, (rows, 128), 1)


def swap_halves(v):
    low = lanes(v.shape[0]) % HEAD_DIM < HEAD_DIM // 2
    return jnp.where(low, pltpu.roll(v, 128 - HEAD_DIM // 2, 1), pltpu.roll(v, HEAD_DIM // 2, 1))


def row_mean(v):
    return jnp.sum(v, axis=1, keepdims=True) * (1.0 / D)


def head_masks():
    low = lax.broadcasted_iota(jnp.int32, (1, 128), 1) < HEAD_DIM
    return (jnp.where(low, 1.0, 0.0).astype(BF), jnp.where(low, 0.0, 1.0).astype(BF))


def forward_body(
    tok, cot, prev, route, slot_row, seg_col, seg_row, cos, sin, w_qkv, w_out, w_small, vecs,
    sent, qkv, att, resid, lse_out, aux, act, bias, tg0, tg1, lse,
):
    gain_one, gain_two = vecs[0:1, :], vecs[1:2, :]
    for r in range(2):
        rows = slice(r * HALF, (r + 1) * HALF)
        x = tok[rows, :].astype(F32)
        act[rows, :] = (x * lax.rsqrt(row_mean(x * x) + EPSILON) * gain_one).astype(BF)
        qi = lax.broadcasted_iota(jnp.int32, (HALF, SEQ), 0) + r * HALF
        ki = lax.broadcasted_iota(jnp.int32, (HALF, SEQ), 1)
        ok = (qi >= ki) & (seg_col[rows, :] == seg_row[...])
        bias[rows, :] = jnp.where(ok, 0.0, FLOOR_SCORE)
    for block in range(9):
        part = dot(act[...], w_qkv[:, block * 256 : block * 256 + 256])
        for i in range(2):
            v = part[:, i * 128 : i * 128 + 128]
            if block < 6:
                v = v * cos[...] + swap_halves(v) * sin[...]
            if block < 3:
                v = v * (1.0 / math.sqrt(HEAD_DIM))
            at = block * 256 + i * 128
            qkv[:, at : at + 128] = v.astype(BF)
    masks = head_masks()

    def pair(p, carry):
        q = qkv[:, pl.ds(pl.multiple_of(p * 128, 128), 128)]
        k = qkv[:, pl.ds(pl.multiple_of(D + p * 128, 128), 128)]
        v = qkv[:, pl.ds(pl.multiple_of(2 * D + p * 128, 128), 128)]
        for b in range(2):
            rows, reach = slice(b * HALF, (b + 1) * HALF), (b + 1) * HALF
            out = None
            for h in range(2):
                s = dot_nt(q[rows, :] * masks[h], k[:reach, :]) + bias[rows, :reach]
                top = jnp.max(s, axis=1, keepdims=True)
                e = jnp.exp(s - top)
                total = jnp.sum(e, axis=1, keepdims=True)
                o = dot((e * (1.0 / total)).astype(BF), v[:reach, :] * masks[h])
                out = o if out is None else out + o
                lse[rows, :] = jnp.where(lanes(HALF) == 2 * p + h, top + jnp.log(total), lse[rows, :])
            att[rows, pl.ds(pl.multiple_of(p * 128, 128), 128)] = out.astype(BF)
        return carry

    lax.fori_loop(0, PAIRS, pair, 0)
    lse_out[...] = lse[...].T[:16, :]
    lane = lanes(HALF)

    def column(v, at):
        return jnp.sum(jnp.where(lane == at, v, 0.0), axis=1, keepdims=True)

    for r in range(2):
        rows = slice(r * HALF, (r + 1) * HALF)
        res = tok[rows, :].astype(F32) + dot(att[rows, :], w_out[...])
        resid[rows, :] = res
        act2 = (res * lax.rsqrt(row_mean(res * res) + EPSILON) * gain_two).astype(BF)
        act[rows, :] = act2
        logits = dot(act2, w_small[...])
        router = logits + prev[rows, :].astype(F32)
        r0, r1 = column(router, route[rows, 0:1]), column(router, route[rows, 1:2])
        top = jnp.maximum(r0, r1)
        e0, e1 = jnp.exp(r0 - top), jnp.exp(r1 - top)
        g0, g1 = e0 / (e0 + e1), e1 / (e0 + e1)
        made = jnp.where(lane == 0, g0, jnp.where(lane == 1, g1, 0.0))
        for c in range(2):
            a, b = column(logits, CHOICES + 2 * c), column(logits, CHOICES + 2 * c + 1)
            top = jnp.maximum(a, b)
            ea, eb = jnp.exp(a - top), jnp.exp(b - top)
            made = jnp.where(lane == 2 + 2 * c, ea / (ea + eb), made)
            made = jnp.where(lane == 3 + 2 * c, eb / (ea + eb), made)
        aux[rows, :] = made
        g = cot[rows, :].astype(F32)
        tg0[rows, :] = (g0 * g).astype(BF)
        tg1[rows, :] = (g1 * g).astype(BF)

    def dispatch(b, carry):
        ids = lax.broadcasted_iota(jnp.int32, (256, SEQ), 0) + b * 256
        p0 = jnp.where(slot_row[0:1, :] == ids, 1.0, 0.0)
        p1 = jnp.where(slot_row[1:2, :] == ids, 1.0, 0.0)
        sent[pl.ds(b * 2, 2), 0] = dot((p0 + p1).astype(BF), act[...]).astype(BF).reshape(2, CAP, D)
        sg = dot(p0.astype(BF), tg0[...]) + dot(p1.astype(BF), tg1[...])
        sent[pl.ds(b * 2, 2), 1] = sg.astype(BF).reshape(2, CAP, D)
        return carry

    lax.fori_loop(0, SLOTS // 256, dispatch, 0)


def seq_block(width, part, col=0):
    return pl.BlockSpec((SEQ, width), lambda i, part=part, col=col: (part, col))


def fixed(shape, *at):
    at = at or (0,) * len(shape)
    return pl.BlockSpec(shape, lambda i, at=at: at)


def lasting(microseconds):
    return pl.CostEstimate(flops=microseconds * 10**9 + 1, bytes_accessed=0, transcendentals=0)


def kernel_params():
    return pltpu.CompilerParams(dimension_semantics=("arbitrary",), vmem_limit_bytes=VMEM_MOST)


def forward_part(part, t, packed, vecs):
    return pl.pallas_call(
        forward_body,
        grid=(1,),
        in_specs=[
            seq_block(D, part), seq_block(D, part), seq_block(128, part), seq_block(2, part),
            fixed((None, 2, SEQ), part, 0, 0), seq_block(1, part), fixed((None, 1, SEQ), part, 0, 0),
            seq_block(128, part), seq_block(128, part),
            fixed((D, 3 * D), 0, 0), fixed((D, D), 0, 3), fixed((D, 128), 0, 24), fixed((8, D)),
        ],
        out_specs=[
            fixed((EXPERTS, 2, CAP, D)), fixed((SEQ, 3 * D)), fixed((SEQ, D)), fixed((SEQ, D)),
            fixed((16, SEQ)), fixed((SEQ, 128)),
        ],
        out_shape=[
            jax.ShapeDtypeStruct((EXPERTS, 2, CAP, D), BF),
            jax.ShapeDtypeStruct((SEQ, 3 * D), BF),
            jax.ShapeDtypeStruct((SEQ, D), BF),
            jax.ShapeDtypeStruct((SEQ, D), F32),
            jax.ShapeDtypeStruct((16, SEQ), F32),
            jax.ShapeDtypeStruct((SEQ, 128), F32),
        ],
        scratch_shapes=[
            pltpu.VMEM((SEQ, D), BF), pltpu.VMEM((SEQ, SEQ), F32), pltpu.VMEM((SEQ, D), BF),
            pltpu.VMEM((SEQ, D), BF), pltpu.VMEM((SEQ, 128), F32),
        ],
        compiler_params=kernel_params(),
        cost_estimate=lasting(100),
    )(
        t["tokens"], t["cotangent"], t["prev"], t["routes"], t["slot_row"], t["seg_col"], t["seg_row"],
        t["cos"], t["sin"], packed, packed, packed, vecs,
    )


def combine_body(
    prior, back, resid, cot, aux, slot, route, att, w_out, w_small, vecs, p_out, p_small, p_rows,
    out, rgrad, router_out, agrad, out_w, small_w, rows_w,
):
    @pl.when(pl.program_id(0) == 0)
    def _():
        if prior:
            out_w[...], small_w[...], rows_w[...] = p_out[...], p_small[...], p_rows[...]
        else:
            out_w[...] = jnp.zeros_like(out_w)
            small_w[...] = jnp.zeros_like(small_w)
            rows_w[...] = jnp.zeros_like(rows_w)

    gain_two = vecs[1:2, :]
    consts = (vecs[2:3, :], vecs[3:4, :])
    res = resid[...]
    g = cot[...].astype(F32)
    inverse = lax.rsqrt(row_mean(res * res) + EPSILON)
    unit = res * inverse
    normed = unit * gain_two
    lane = lanes(HALF)
    gates = (aux[:, 0:1], aux[:, 1:2])
    cg = ((aux[:, 2:3], aux[:, 3:4]), (aux[:, 4:5], aux[:, 5:6]))
    ids = lax.broadcasted_iota(jnp.int32, (HALF, SLOTS), 1)
    picks = [jnp.where(slot[:, k : k + 1] == ids, 1.0, 0.0) for k in range(2)]
    rows = back[:, 0].reshape(SLOTS, D)
    g_normed = jnp.sum(g * normed, axis=1, keepdims=True)
    g_const = [jnp.sum(g * v, axis=1, keepdims=True) for v in consts]
    gate_grads, straight, total = [], 0.0, res
    const_mask = [
        [jnp.where(route[:, k : k + 1] == EXPERTS + 2 + c, 1.0, 0.0) for c in range(2)] for k in range(2)
    ]
    for k in range(2):
        combined = dot(picks[k].astype(BF), rows)
        direct = jnp.where(route[:, k : k + 1] == EXPERTS + 1, 1.0, 0.0)
        for c in range(2):
            direct += const_mask[k][c] * cg[c][0]
        grad = jnp.sum(g * combined, axis=1, keepdims=True) + direct * g_normed
        for c in range(2):
            grad += const_mask[k][c] * cg[c][1] * g_const[c]
        gate_grads.append(grad)
        straight += gates[k] * direct
        total = total + gates[k] * combined
    total = total + straight * normed
    logit_grad = 0.0
    made = [jnp.zeros((1, D), F32)] * 2
    for c in range(2):
        share = const_mask[0][c] * gates[0] + const_mask[1][c] * gates[1]
        weight = share * cg[c][1]
        total = total + weight * consts[c]
        made[c] = jnp.sum(weight * g, axis=0, keepdims=True)
        first, second = share * g_normed, share * g_const[c]
        inner = cg[c][0] * first + cg[c][1] * second
        for i, v in enumerate((first, second)):
            logit_grad += jnp.where(lane == CHOICES + 2 * c + i, cg[c][i] * (v - inner), 0.0)
    out[...] = total.astype(BF)
    mean_grad = gates[0] * gate_grads[0] + gates[1] * gate_grads[1]
    router = 0.0
    for k in range(2):
        router += jnp.where(lane == route[:, k : k + 1], gates[k] * (gate_grads[k] - mean_grad), 0.0)
    router_out[...] = router[:, :CHOICES]
    logit_low = (router + logit_grad).astype(BF)
    small_w[...] += dot_tn(normed.astype(BF), logit_low)
    normed_grad = dot_nt(logit_low, w_small[...])
    normed_grad += dot((picks[0] + picks[1]).astype(BF), back[:, 1].reshape(SLOTS, D))
    normed_grad += straight * g
    scaled = normed_grad * gain_two
    gain_grad = jnp.sum(normed_grad * unit, axis=0, keepdims=True)
    residual_grad = g + inverse * (scaled - unit * row_mean(scaled * unit))
    rgrad[...] = residual_grad
    low = residual_grad.astype(BF)
    agrad[...] = dot_nt(low, w_out[...]).astype(BF)
    out_w[...] += dot_tn(att[...], low)
    rows_w[0:1, :] += made[0]
    rows_w[1:2, :] += made[1]
    rows_w[2:3, :] += gain_grad


def combine_part(part, back, kept, t, packed, vecs, prior):
    _, _, att, resid, _, aux = kept

    def tile(width, mine=True):
        base = 0 if mine else 2 * part
        return pl.BlockSpec((HALF, width), lambda i, base=base: (base + i, 0))

    sums = [
        jax.ShapeDtypeStruct((D, D), F32), jax.ShapeDtypeStruct((D, 128), F32), jax.ShapeDtypeStruct((8, D), F32)
    ]
    sum_specs = [fixed((D, D)), fixed((D, 128)), fixed((8, D))]
    body = functools.partial(combine_body, prior is not None)
    if prior is None:
        given = []

        def body(*refs):
            combine_body(False, *refs[:10], None, None, None, *refs[10:])

    else:
        given = list(prior)
    return pl.pallas_call(
        body,
        grid=(2,),
        in_specs=[
            fixed((EXPERTS, 2, CAP, D)), tile(D), tile(D, False), tile(128), tile(2, False), tile(2, False),
            tile(D), fixed((D, D), 0, 3), fixed((D, 128), 0, 24), fixed((8, D)),
        ] + (sum_specs if given else []),
        out_specs=[tile(D), tile(D), tile(CHOICES), tile(D)] + sum_specs,
        out_shape=[
            jax.ShapeDtypeStruct((SEQ, D), BF), jax.ShapeDtypeStruct((SEQ, D), F32),
            jax.ShapeDtypeStruct((SEQ, CHOICES), F32), jax.ShapeDtypeStruct((SEQ, D), BF),
        ] + sums,
        compiler_params=kernel_params(),
        cost_estimate=lasting(0),
    )(back, resid, t["cotangent"], aux, t["slots"], t["routes"], att, packed, packed, vecs, *given)


def attention_back_body(
    qkv, agrad, lse, seg_col, seg_row, cos, sin, w_qkv, tok, vecs, rgrad, grad_in, qkv_grad, act, gain_w, bias
):
    for b in range(2):
        rows = slice(b * HALF, (b + 1) * HALF)
        ki = lax.broadcasted_iota(jnp.int32, (HALF, SEQ), 0) + b * HALF
        qi = lax.broadcasted_iota(jnp.int32, (HALF, SEQ), 1)
        ok = (qi >= ki) & (seg_col[rows, :] == seg_row[...])
        bias[rows, :] = jnp.where(ok, 0.0, FLOOR_SCORE)
    masks = head_masks()
    scale = 1.0 / math.sqrt(HEAD_DIM)

    def one_pair(p, carry):
        at = [pl.ds(pl.multiple_of(i * D + p * 128, 128), 128) for i in range(3)]
        q, k, v = [qkv[:, a] for a in at]
        da = agrad[:, at[0]]
        kg, vg, qg = [None, None], [None, None], [None, None]

        def add(store, i, value):
            store[i] = value if store[i] is None else store[i] + value

        for h in range(2):
            qh, dh = q * masks[h], da * masks[h]
            probs, grads, keyed = [], [], []
            for b in range(2):
                keys, first = slice(b * HALF, (b + 1) * HALF), b * HALF
                kh = k[keys, :] * masks[h]
                st = dot_nt(kh, q[first:, :]) + bias[keys, first:]
                probs.append(jnp.exp(st - lse[pl.ds(2 * p + h, 1), first:]))
                grads.append(dot_nt(v[keys, :] * masks[h], da[first:, :]))
                keyed.append(kh)
            inner = [jnp.sum(probs[b] * grads[b], axis=0, keepdims=True) for b in range(2)]
            late = inner[0][:, HALF:] + inner[1]
            whole = jnp.concatenate([inner[0][:, :HALF], late], axis=1)
            for b, mean in enumerate((whole, late)):
                first = b * HALF
                ds = (probs[b] * (grads[b] - mean)).astype(BF)
                add(kg, b, dot(ds, qh[first:, :]))
                add(vg, b, dot(probs[b].astype(BF), dh[first:, :]))
                full = dot_tn(ds, keyed[b])
                if b == 0:
                    add(qg, 0, full[:HALF, :])
                    add(qg, 1, full[HALF:, :])
                else:
                    add(qg, 1, full)
        for b in range(2):
            rows = slice(b * HALF, (b + 1) * HALF)
            c, s = cos[rows, :], sin[rows, :]
            qb = qg[b] * scale
            qkv_grad[rows, at[0]] = (qb * c - swap_halves(qb) * s).astype(BF)
            qkv_grad[rows, at[1]] = (kg[b] * c - swap_halves(kg[b]) * s).astype(BF)
            qkv_grad[rows, at[2]] = vg[b].astype(BF)
        return carry

    lax.fori_loop(0, PAIRS, one_pair, 0)
    gain_one = vecs[0:1, :]
    gain_grad = 0.0
    for b in range(2):
        rows = slice(b * HALF, (b + 1) * HALF)
        x = tok[rows, :].astype(F32)
        inverse = lax.rsqrt(row_mean(x * x) + EPSILON)
        unit = x * inverse
        act[rows, :] = (unit * gain_one).astype(BF)
        grad = dot_nt(qkv_grad[rows, :], w_qkv[...])
        scaled = grad * gain_one
        gain_grad += jnp.sum(grad * unit, axis=0, keepdims=True)
        grad_in[rows, :] = rgrad[rows, :] + inverse * (scaled - unit * row_mean(scaled * unit))
    gain_w[...] = jnp.broadcast_to(gain_grad, gain_w.shape)


def attention_back(part, kept, rgrad, agrad, t, packed, vecs):
    _, qkv, _, _, lse, _ = kept
    return pl.pallas_call(
        attention_back_body,
        grid=(1,),
        in_specs=[
            fixed((SEQ, 3 * D)), fixed((SEQ, D)), fixed((16, SEQ)),
            seq_block(1, part), fixed((None, 1, SEQ), part, 0, 0), seq_block(128, part), seq_block(128, part),
            fixed((D, 3 * D), 0, 0), seq_block(D, part), fixed((8, D)), fixed((SEQ, D)),
        ],
        out_specs=[fixed((SEQ, D)), fixed((SEQ, 3 * D)), fixed((SEQ, D)), fixed((8, D))],
        out_shape=[
            jax.ShapeDtypeStruct((SEQ, D), F32), jax.ShapeDtypeStruct((SEQ, 3 * D), BF),
            jax.ShapeDtypeStruct((SEQ, D), BF), jax.ShapeDtypeStruct((8, D), F32),
        ],
        scratch_shapes=[pltpu.VMEM((SEQ, SEQ), F32)],
        compiler_params=kernel_params(),
        cost_estimate=lasting(0),
    )(
        qkv, agrad, lse, t["seg_col"], t["seg_row"], t["cos"], t["sin"], packed, t["tokens"], vecs, rgrad
    )


def mixer_wgrad_body(parts, groups, *refs):
    core, acts, grads, gains = refs[0], refs[1 : 1 + parts], refs[1 + parts : 1 + 2 * parts], refs[1 + 2 * parts : 1 + 3 * parts]
    small, rows, give, keep, turned, last = refs[1 + 3 * parts :]
    step, half = pl.program_id(0), D // 2
    chunk = half // groups

    def scattered(store, across, value):
        for group in range(groups):
            for c in range(2):
                kept = (core[0] == c).astype(jnp.int32)
                at = pl.ds(pl.multiple_of(kept * half + group * chunk, 16), chunk)
                first = (2 * group + c) * chunk
                store[at, across] = value[first : first + chunk, :]

    @pl.when(step == 0)
    def _():
        for i in range(parts):
            scattered(turned, slice(i * SEQ, (i + 1) * SEQ), acts[i][...].T)

    @pl.when(step < 9)
    def _():
        made = dot(turned[...], jnp.concatenate([v[...] for v in grads], axis=0)).astype(BF)
        give[...] = made[:half, :]
        keep[...] = made[half:, :]

    @pl.when(step == 9)
    def _():
        gain_one = sum(v[0:1, :] for v in gains)
        line = lax.broadcasted_iota(jnp.int32, (128, D), 0)
        stacked = 0.0
        for i, row in enumerate((rows[0:1, :], rows[1:2, :], gain_one, rows[2:3, :])):
            stacked += jnp.where(line == 16 + i, row, 0.0)
        scattered(last, slice(0, 128), (small[...] + stacked.T).astype(BF))
        give[:, :128] = last[:half, :]
        keep[:, :128] = last[half:, :]
        give[:, 128:] = jnp.zeros((half, 128), BF)
        keep[:, 128:] = jnp.zeros((half, 128), BF)


def mixer_wgrad(acts, grads, gains, small, rows, groups, core):
    parts = len(acts)
    half = pl.BlockSpec((D // 2, 256), lambda i: (0, i))
    out = jax.ShapeDtypeStruct((D // 2, 3 * D + 256), BF)
    return pl.pallas_call(
        functools.partial(mixer_wgrad_body, parts, groups),
        grid=(10,),
        in_specs=[pl.BlockSpec(memory_space=pltpu.SMEM)]
        + [fixed((SEQ, D))] * parts
        + [pl.BlockSpec((SEQ, 256), lambda i: (0, jnp.minimum(i, 8)))] * parts
        + [fixed((8, D))] * parts
        + [fixed((D, 128)), fixed((8, D))],
        out_specs=[half, half],
        out_shape=[out, out],
        scratch_shapes=[pltpu.VMEM((D, parts * SEQ), BF), pltpu.VMEM((D, 128), BF)],
        compiler_params=kernel_params(),
        cost_estimate=lasting(0),
    )(jnp.stack([core]).astype(jnp.int32), *acts, *grads, *gains, small, rows)


def tables(tokens, cotangent, prev_logits, routes, capacity, segments, positions):
    parts = tokens.shape[0] // SEQ
    slots = jnp.concatenate(
        [pair_slots(routes[i * SEQ : (i + 1) * SEQ], capacity) for i in range(parts)]
    )
    lane = jnp.arange(128) % HEAD_DIM
    frequency = jnp.exp((lane % (HEAD_DIM // 2)).astype(F32) * (-2.0 * math.log(ROPE_BASE) / HEAD_DIM))
    angles = positions.astype(F32)[:, None] * frequency[None, :]
    sign = jnp.where(lane < HEAD_DIM // 2, -1.0, 1.0)
    return dict(
        tokens=tokens,
        cotangent=cotangent,
        prev=jnp.pad(prev_logits, ((0, 0), (0, 128 - CHOICES))),
        routes=routes,
        slots=slots,
        slot_row=slots.reshape(parts, SEQ, 2).transpose(0, 2, 1),
        seg_col=segments[:, None],
        seg_row=segments.reshape(parts, 1, SEQ),
        cos=jnp.cos(angles),
        sin=jnp.sin(angles) * sign,
    )


FC = 512


def expert_rows_body(x_ref, g_ref, wg_ref, wu_ref, wd_ref, hid_ref, dg_ref, du_ref, out_ref, acc, racc):
    step = pl.program_id(0)
    x = x_ref[:, 0].reshape(-1, D)
    g = g_ref[:, 0].reshape(-1, D)
    wg, wu, wd = wg_ref[...], wu_ref[...], wd_ref[...]
    gate = dot(x, wg)
    up = dot(x, wu)
    hgrad = dot_nt(g, wd).astype(BF).astype(F32)
    sig = 1.0 / (1.0 + jnp.exp(-gate))
    act = gate * sig
    hidden = (act * up).astype(BF)
    dgate = (hgrad * up * sig * (1.0 + gate * (1.0 - sig))).astype(BF)
    dup = (hgrad * act).astype(BF)
    hid_ref[...] = hidden
    dg_ref[...] = dgate
    du_ref[...] = dup
    prod = dot(hidden, wd)
    rgrad = dot_nt(dgate, wg) + dot_nt(dup, wu)

    @pl.when(step == 0)
    def _():
        acc[...] = prod
        racc[...] = rgrad

    @pl.when(step > 0)
    def _():
        acc[...] += prod
        racc[...] += rgrad

    @pl.when(step == pl.num_programs(0) - 1)
    def _():
        out_ref[:, 0] = acc[...].astype(BF).reshape(-1, CAP, D)
        out_ref[:, 1] = racc[...].astype(BF).reshape(-1, CAP, D)


def expert_rows(received, w_gate_up, w_down):
    n = received.shape[0]
    rows = n * CAP
    steps = FF // FC
    wide = jax.ShapeDtypeStruct((rows, FF), BF)
    block = pl.BlockSpec((rows, FC), lambda j: (0, j))
    return pl.pallas_call(
        expert_rows_body,
        grid=(steps,),
        in_specs=[
            pl.BlockSpec((n, 1, CAP, D), lambda j: (0, 0, 0, 0)),
            pl.BlockSpec((n, 1, CAP, D), lambda j: (0, 1, 0, 0)),
            pl.BlockSpec((D, FC), lambda j: (0, j)),
            pl.BlockSpec((D, FC), lambda j: (0, steps + j)),
            pl.BlockSpec((FC, D), lambda j: (j, 0)),
        ],
        out_specs=[block, block, block, pl.BlockSpec((n, 2, CAP, D), lambda j: (0, 0, 0, 0))],
        out_shape=[wide, wide, wide, jax.ShapeDtypeStruct((n, 2, CAP, D), BF)],
        scratch_shapes=[pltpu.VMEM((rows, D), F32), pltpu.VMEM((rows, D), F32)],
        compiler_params=pltpu.CompilerParams(
            dimension_semantics=("arbitrary",), vmem_limit_bytes=VMEM_MOST
        ),
        cost_estimate=lasting(28),
    )(received, received, w_gate_up, w_gate_up, w_down)


FW = 512


def down_wgrad_body(parts, *refs):
    hid, received, out = refs[:parts], refs[parts : 2 * parts], refs[2 * parts]
    rows = jnp.concatenate([v[:, 0].reshape(-1, D) for v in received], axis=0)
    out[...] = dot_tn(jnp.concatenate([v[...] for v in hid], axis=0), rows).astype(BF)


def down_wgrad(received, hid):
    parts, (n, _, _, _) = len(received), received[0].shape
    return pl.pallas_call(
        functools.partial(down_wgrad_body, parts),
        grid=(FF // FW,),
        in_specs=[pl.BlockSpec((n * CAP, FW), lambda j: (0, j))] * parts
        + [pl.BlockSpec((n, 1, CAP, D), lambda j: (0, 1, 0, 0))] * parts,
        out_specs=pl.BlockSpec((FW, D), lambda j: (j, 0)),
        out_shape=jax.ShapeDtypeStruct((FF, D), BF),
        compiler_params=kernel_params(),
        cost_estimate=lasting(10),
    )(*hid, *received)


def gate_up_wgrad_body(parts, *refs):
    received, dg, du = refs[:parts], refs[parts : 2 * parts], refs[2 * parts : 3 * parts]
    out, xt = refs[3 * parts :]
    rows = received[0].shape[0] * CAP

    @pl.when(pl.program_id(0) == 0)
    def _():
        for i in range(parts):
            xt[:, i * rows : (i + 1) * rows] = received[i][:, 0].reshape(rows, D).T

    for k, grads in enumerate((dg, du)):
        out[k] = dot(xt[...], jnp.concatenate([v[...] for v in grads], axis=0)).astype(BF)


def gate_up_wgrad(received, dg, du):
    parts, (n, _, _, _) = len(received), received[0].shape
    return pl.pallas_call(
        functools.partial(gate_up_wgrad_body, parts),
        grid=(FF // FW,),
        in_specs=[pl.BlockSpec((n, 1, CAP, D), lambda j: (0, 0, 0, 0))] * parts
        + [pl.BlockSpec((n * CAP, FW), lambda j: (0, j))] * (2 * parts),
        out_specs=pl.BlockSpec((2, D, FW), lambda j: (0, 0, j)),
        out_shape=jax.ShapeDtypeStruct((2, D, FF), BF),
        scratch_shapes=[pltpu.VMEM((D, parts * n * CAP), BF)],
        compiler_params=kernel_params(),
        cost_estimate=lasting(0),
    )(*received, *dg, *du)


def place_body(spots, count, *refs):
    offsets, blocks, outs, sems = refs[0], refs[1 : 1 + count], refs[1 + count : -1], refs[-1]
    copies = []
    for i, (block, row, rows, column, columns, out) in enumerate(spots):
        down = pl.ds(pl.multiple_of(offsets[2 * i], 16), rows)
        across = pl.ds(pl.multiple_of(offsets[2 * i + 1], 128), columns)
        copies.append(
            pltpu.make_async_copy(
                blocks[block].at[pl.ds(row, rows), pl.ds(column, columns)],
                outs[out].at[down, across],
                sems.at[i],
            )
        )
    for copy in copies:
        copy.start()
    for copy in copies:
        copy.wait()


def place(blocks, spots, offsets, shapes):
    anywhere = pl.BlockSpec(memory_space=pl.ANY)
    return pl.pallas_call(
        functools.partial(place_body, spots, len(blocks)),
        in_specs=[pl.BlockSpec(memory_space=pltpu.SMEM)] + [anywhere] * len(blocks),
        out_specs=[pl.BlockSpec(memory_space=pltpu.VMEM)] * len(shapes),
        out_shape=[jax.ShapeDtypeStruct(v, BF) for v in shapes],
        scratch_shapes=[pltpu.SemaphoreType.DMA((len(spots),))],
        compiler_params=pltpu.CompilerParams(vmem_limit_bytes=VMEM_MOST),
        cost_estimate=lasting(0),
    )(jnp.stack(offsets).astype(jnp.int32), *blocks)


def pick(value, index, axis=0):
    return lax.dynamic_index_in_dim(value, index, axis, False)


def added(*values):
    return sum(v.astype(F32) for v in values).astype(BF)


class Paired:
    axes = ("half", "low", "inner", "side", "core")
    fsdp = ("half", "low", "inner")
    expert = ("side", "core")
    rows = ("side", "low", "inner")
    route_axes = ("half", "low", "inner", "core")
    near = 896
    cut = 3072

    def __init__(self, mesh):
        self.mesh = Mesh(mesh.devices.reshape(2, 2, 2, 2, 2), self.axes)
        self.routes = []
        for turn in range(4):
            pairs = []
            for z in range(4):
                for y in range(2):
                    for c in range(2):
                        half, inner = (z ^ turn) >> 1, (z ^ turn) & 1
                        pairs.append(((z * 2 + y) * 2 + c, ((half * 2 + c) * 2 + inner) * 2 + y))
            self.routes.append(pairs)

    @staticmethod
    def swap(value, axis="core"):
        return lax.ppermute(value, axis, [(0, 1), (1, 0)])

    @staticmethod
    def along(value, turn):
        return lax.ppermute(value, ("half", "low"), [(i, i ^ turn) for i in range(4)])

    @staticmethod
    def spot():
        z = lax.axis_index("half") * 2 + lax.axis_index("low")
        return z, lax.axis_index("inner"), lax.axis_index("side"), lax.axis_index("core")

    @staticmethod
    def joined(gate_up, down):
        high, edge = gate_up.shape[1], D - 256
        tail = down[:, 2 * high :]
        half = tail.shape[1] // 2
        under = jnp.concatenate([tail[:, :half, edge:], tail[:, half:, edge:]], axis=2)
        last = jnp.concatenate([tail[:, :, :edge], under], axis=1)
        cut = Paired.cut
        rest = jnp.concatenate([gate_up[:, :, cut:], down[:, :high], down[:, high : 2 * high], last], axis=2)
        return gate_up[:, :, :cut], rest

    @staticmethod
    def rects(high, deep):
        half, edge, at = deep // 2 - high, D - 256, 2 * FF - Paired.cut
        yield 0, high, at, D, 0, 0
        yield 0, high, at + D, D, high, 0
        yield 0, 2 * half, at + 2 * D, edge, 2 * high, 0
        yield 2 * half, half, at + 2 * D, 256, 2 * high, edge
        yield 2 * half, half, at + 2 * D + 256, 256, 2 * high + half, edge

    def send(self, joined, turn, part):
        mine = pick(joined[part], (self.spot()[0] ^ turn) & 1)
        return lax.ppermute(mine, self.route_axes, self.routes[turn])

    def gather_shared(self, shard, weights, early):
        z, y, x, c = self.spot()
        rows, width = shard.shape
        rows, width = rows // 2, width // 2
        mine = lax.dynamic_slice(shard, (c * rows, x * width), (rows, width))
        stack = jnp.concatenate([mine] + [self.along(mine, turn) for turn in (1, 2, 3)])
        stack, joined, early = lax.optimization_barrier((stack, self.joined(*weights), early))
        sent = {(2, 0): self.send(joined, 2, 0)}
        over_y, over_x = self.swap(stack, "inner"), self.swap(stack, "side")
        far = self.swap(over_y[:, : self.near], "side"), self.swap(over_x[:, self.near :], "inner")
        blocks = [stack, over_y, over_x, *far]
        flips = [(0, 0, 0), (1, 0, 0), (0, 1, 0), (1, 1, 0), (1, 1, self.near)]
        spots, offsets = [], []
        for i, (dy, dx, column) in enumerate(flips + flips):
            core = c if i < len(flips) else 1 - c
            for turn in range(4):
                spots.append((i, turn * rows, rows, 0, blocks[i % len(flips)].shape[1], 0))
                offsets += [((z ^ turn) * 2 + (y ^ dy)) * 2 * rows + core * rows, (x ^ dx) * width + column]
        blocks += [self.swap(v) for v in blocks]
        blocks, joined, sent = lax.optimization_barrier((blocks, joined, sent))
        [full] = place(blocks, spots, offsets, [(16 * rows, 2 * width)])
        return full, early, (joined, sent)

    def gather_more(self, held, value, names):
        joined, sent = held
        more = {v: self.send(joined, *v) for v in names}
        value, joined, sent = lax.optimization_barrier((value, joined, {**sent, **more}))
        return (joined, sent), value

    def split(self):
        return 8, lax.axis_index("core")

    def halves(self, total):
        c = lax.axis_index("core")
        total = total.reshape(8, 2, total.shape[0] // 16, total.shape[1])
        return pick(total, 1 - c, 1), pick(total, c, 1)

    def reduce_first(self, give, keep):
        z, y, x, c = self.spot()
        width = give.shape[-1] // 2
        near = (width // 128 + 1) // 2 * 128
        parts = added(keep, self.swap(give)).reshape(4, 2, -1, 2 * width)

        def columns(value, first, count):
            return lax.dynamic_slice_in_dim(value, first, count, value.ndim - 1)

        one = added(columns(parts, x * width, near), self.swap(columns(parts, (1 - x) * width, near), "side"))
        two = jnp.concatenate([parts[..., near:width], parts[..., width + near :]], axis=3)
        two = added(pick(two, y, 1), self.swap(pick(two, 1 - y, 1), "inner"))
        return one, two

    def reduce_last(self, one, two):
        z, y, x, c = self.spot()
        rest = two.shape[2] // 2
        one = added(pick(one, y, 1), self.swap(pick(one, 1 - y, 1), "inner"))
        near = lax.dynamic_slice_in_dim(two, x * rest, rest, 2)
        two = added(near, self.swap(lax.dynamic_slice_in_dim(two, (1 - x) * rest, rest, 2), "side"))
        both = jnp.concatenate([one, two], axis=2)
        mine = added(pick(both, z), *[self.along(pick(both, z ^ turn), turn) for turn in (1, 2, 3)])
        other = self.swap(mine, "side")
        line = jnp.where(x == 0, jnp.concatenate([mine, other], 1), jnp.concatenate([other, mine], 1))
        other = self.swap(line)
        both = jnp.where(c == 0, jnp.concatenate([line, other]), jnp.concatenate([other, line]))
        return both.astype(F32)

    def gather_expert(self, held, shapes):
        sent = held[1]
        c = lax.axis_index("core")
        here = lax.axis_index("half") * 2 + lax.axis_index("inner")
        own = [sent[turn, part] for turn in range(4) for part in range(2)]
        blocks = own + [self.swap(v) for v in own]
        high, deep = shapes[0][1], shapes[1][1]
        spots, offsets, zero = [], [], jnp.int32(0)
        for i in range(0, 16, 2):
            shard = (here ^ (i // 2 % 4)) * 2 + (c if i < 8 else 1 - c)
            spots += [(i, 0, high, 0, self.cut, 0), (i + 1, 0, high, 0, 2 * FF - self.cut, 0)]
            offsets += [shard * high, zero, shard * high, zero + self.cut]
            for row, rows, column, columns, to_row, to_column in self.rects(high, deep):
                spots.append((i + 1, row, rows, column, columns, 1))
                offsets += [shard * deep + to_row, zero + to_column]
        return place(blocks, spots, offsets, [(8 * high, 2 * FF), (8 * deep, D)])

    def scatter_start(self, grad, axis):
        c = lax.axis_index("core")
        shape = grad.shape
        grad = grad.reshape(shape[:axis] + (4, 2, shape[axis] // 8) + shape[axis + 1 :])
        return added(pick(grad, c, axis + 1), self.swap(pick(grad, 1 - c, axis + 1)))

    def scatter_send(self, parts, axis):
        here = lax.axis_index("half") * 2 + lax.axis_index("inner")
        got = {}
        for turn in (2, 3, 0, 1):
            back = [(b, a) for a, b in self.routes[turn]]
            got[turn] = lax.ppermute(pick(parts, here ^ turn, axis), self.route_axes, back)
        return got

    def scatter_end(self, got, axis):
        even = (self.spot()[0] & 1) == 0
        first, second = [got[i].astype(F32) + got[i + 2].astype(F32) for i in range(2)]
        return jnp.stack([jnp.where(even, first, second), jnp.where(even, second, first)])


class Plain:
    axes = ("outer", "inner", "expert")
    fsdp = ("outer", "inner")
    expert = ("expert",)
    rows = ("expert", "inner")

    def __init__(self, mesh):
        fsdp, expert = mesh.shape["fsdp"], mesh.shape["expert"]
        inner = EXPERTS // expert
        self.mesh = Mesh(mesh.devices.reshape(fsdp // inner, inner, expert), self.axes)

    def gather_shared(self, shard, weights, early):
        return lax.all_gather(shard, self.fsdp, axis=0, tiled=True), early, weights

    def gather_more(self, held, value, names):
        return held, value

    def split(self):
        return 1, jnp.int32(1)

    def halves(self, total):
        return jnp.split(total, 2)

    def reduce_first(self, give, keep):
        return jnp.concatenate([give, keep]), None

    def reduce_last(self, total, _):
        total = lax.psum_scatter(total, self.axes, scatter_dimension=0, tiled=True)
        return lax.all_gather(total, self.expert, axis=0, tiled=True).astype(F32)

    def gather_expert(self, weights, shapes):
        full = []
        for weight in weights:
            own = lax.all_to_all(weight, "inner", 0, 0, tiled=True)
            own = lax.all_gather(own, "outer", axis=0, tiled=True)
            full.append(own.reshape((-1,) + weight.shape[2:]))
        return full

    def scatter_start(self, grad, axis):
        return grad

    def scatter_send(self, grad, axis):
        return grad

    def scatter_end(self, grad, axis):
        inner = lax.axis_size("inner")
        part = lax.psum_scatter(grad, "outer", scatter_dimension=axis, tiled=True)
        shape = part.shape
        part = part.reshape(shape[:axis] + (inner, shape[axis] // inner) + shape[axis + 1 :])
        part = jnp.moveaxis(part, axis, 0)
        return lax.all_to_all(part, "inner", 0, 0, tiled=True).astype(F32)


def solution(mesh):
    plan = Paired(mesh) if (mesh.shape["fsdp"], mesh.shape["expert"]) == (8, 4) else Plain(mesh)

    def on_device(
        tokens, cotangent, prev_logits, routes, capacity, segments, positions,
        w_qkv, w_out, gate_matrix, const_values, attn_gain, moe_gain, w_gate_up, w_down,
    ):
        rows = w_qkv.shape[0]
        pad = jnp.zeros((rows, 256 - 20), BF)
        small = jnp.concatenate(
            [gate_matrix, const_values, attn_gain[:, None], moe_gain[:, None], pad], axis=1
        )
        shard = jnp.concatenate([w_qkv, w_out, small], axis=1)
        t = tables(tokens, cotangent, prev_logits, routes, capacity, segments, positions)
        packed, t, held = plan.gather_shared(shard, (w_gate_up, w_down), t)
        columns = packed[:, 4 * D + 16 : 4 * D + 20].astype(F32).T
        vecs = jnp.concatenate([columns[2:], columns[:2], jnp.zeros((4, D), F32)])
        parts = tokens.shape[0] // SEQ
        kept, sends, shared = [], [], packed
        for i in range(parts):
            if i == 1:
                held, (shared, kept[0][5]) = plan.gather_more(held, (packed, kept[0][5]), ((2, 1), (0, 0), (0, 1), (1, 0)))
            kept.append(list(forward_part(i, t, shared, vecs)))
            sends.append(kept[i][0])
        held, sends[-1] = plan.gather_more(held, sends[-1], ((3, 0), (3, 1), (1, 1)))
        gate_up_full, down_full = plan.gather_expert(held, (w_gate_up.shape, w_down.shape))
        received = [lax.all_to_all(v, plan.rows, 0, 0, tiled=True) for v in sends]
        made = [expert_rows(r, gate_up_full, down_full) for r in received]
        hid, dg, du = [[m[i] for m in made] for i in range(3)]
        backs = [m[3] for m in made]
        down_w = down_wgrad(received, hid)
        backs[-1], down_w = lax.optimization_barrier((backs[-1], down_w))
        returned = [lax.all_to_all(v, plan.rows, 0, 0, tiled=True) for v in backs]
        dg, down_w = lax.optimization_barrier((dg, down_w))
        gate_up_w = gate_up_wgrad(received, dg, du)
        returned[0], gate_up_w = lax.optimization_barrier((returned[0], gate_up_w))
        down_got = plan.scatter_send(plan.scatter_start(down_w, 0), 0)
        gate_up_sums = plan.scatter_start(gate_up_w, 1)
        firsts, sums = [], None
        for i in range(parts):
            *first, out_w, small_w, rows_w = combine_part(i, returned[i], kept[i], t, packed, vecs, sums)
            sums = (out_w, small_w, rows_w)
            firsts.append(first)
        out_halves = plan.halves(sums[0].astype(BF))
        held = (out_halves, firsts[0][1], gate_up_sums, down_got)
        out_halves, firsts[0][1], gate_up_sums, down_got = lax.optimization_barrier(held)
        gate_up_got = plan.scatter_send(gate_up_sums, 1)
        down_total = plan.scatter_end(down_got, 0)
        out_summed = plan.reduce_first(*out_halves)
        lasts = []
        for i, first in enumerate(firsts):
            if i == parts - 1:
                out_summed, first[1] = lax.optimization_barrier((out_summed, first[1]))
                out_total = plan.reduce_last(*out_summed)
            lasts.append(attention_back(i, kept[i], first[1], first[3], t, packed, vecs))
        acts = [v[2] for v in lasts]
        halves = mixer_wgrad(
            acts, [v[1] for v in lasts], [v[3] for v in lasts], sums[1], sums[2], *plan.split()
        )
        halves, gate_up_got = lax.optimization_barrier((halves, gate_up_got))
        total = plan.reduce_last(*plan.reduce_first(*halves))
        gate_up_total = plan.scatter_end(gate_up_got, 1)
        gate_up_total = jnp.concatenate([gate_up_total[:, 0], gate_up_total[:, 1]], axis=2)
        return (
            jnp.concatenate([v[0] for v in firsts]),
            jnp.concatenate([v[0] for v in lasts]),
            jnp.concatenate([v[2] for v in firsts]),
            total[:, : 3 * D],
            out_total,
            total[:, 3 * D : 3 * D + 16],
            total[:, 3 * D + 16 : 3 * D + 18],
            total[:, 3 * D + 18],
            total[:, 3 * D + 19],
            gate_up_total,
            down_total,
        )

    every = plan.fsdp + plan.expert
    split = P(every, None)
    shard = P(plan.fsdp, None)
    line = P(plan.fsdp)
    whole = P(plan.expert, plan.fsdp, None)
    return jax.shard_map(
        on_device,
        mesh=plan.mesh,
        in_specs=(
            split, split, split, split, P(), P(every), P(every),
            shard, shard, shard, shard, line, line, whole, whole,
        ),
        out_specs=(split, split, split, shard, shard, shard, shard, line, line, whole, whole),
        check_vma=False,
    )
```

```python
import functools
import math

import jax
import jax.numpy as jnp
from jax import lax
from jax.experimental import pallas as pl
from jax.experimental.pallas import tpu as pltpu
from jax.sharding import Mesh
from jax.sharding import PartitionSpec as P

D = 768
HEADS = 12
HEAD_DIM = 64
FF = 2048
EXPERTS = 8
SEQ = 512
CAP = 128
CHOICES = EXPERTS + 4
SLOTS = EXPERTS * CAP

EPSILON = 1e-05
ROPE_BASE = 10000.0
FLOOR_SCORE = -1e30
HIGHEST = lax.Precision.HIGHEST
BF = jnp.bfloat16
F32 = jnp.float32
VMEM_MOST = 56 * 2**20


def dot(a, b):
    return jnp.dot(a, b, preferred_element_type=F32)


def dot_nt(a, b):
    return lax.dot_general(a, b, (((1,), (1,)), ((), ())), preferred_element_type=F32)


def dot_tn(a, b):
    return lax.dot_general(a, b, (((0,), (0,)), ((), ())), preferred_element_type=F32)


def pair_slots(route, capacity):
    route_hot = (route[:, :, None] == jnp.arange(CHOICES, dtype=jnp.int32)).astype(F32)
    seq_index = jnp.arange(SEQ)
    before = (seq_index[:, None] > seq_index[None, :]).astype(BF)
    earlier = dot(before, jnp.sum(route_hot, axis=1).astype(BF))
    slot_rank = jnp.sum(earlier[:, None, :] * route_hot, axis=-1)
    cap_limit = jnp.sum(route_hot[:, :, :EXPERTS] * capacity.astype(F32), axis=-1)
    kept_pairs = (route < EXPERTS) & (slot_rank < cap_limit)
    return jnp.where(kept_pairs, route * CAP + slot_rank.astype(jnp.int32), -1)


HALF = SEQ // 2
PAIRS = HEADS // 2


def lanes(rows):
    return lax.broadcasted_iota(jnp.int32, (rows, 128), 1)


def swap_halves(v):
    low = lanes(v.shape[0]) % HEAD_DIM < HEAD_DIM // 2
    return jnp.where(low, pltpu.roll(v, 128 - HEAD_DIM // 2, 1), pltpu.roll(v, HEAD_DIM // 2, 1))


def row_mean(v):
    return jnp.sum(v, axis=1, keepdims=True) * (1.0 / D)


def head_masks():
    low = lax.broadcasted_iota(jnp.int32, (1, 128), 1) < HEAD_DIM
    return (jnp.where(low, 1.0, 0.0).astype(BF), jnp.where(low, 0.0, 1.0).astype(BF))


def forward_body(
    tok, cot, prev, route, slot_row, seg_col, seg_row, cos, sin, w_qkv, w_out, w_small, vecs,
    sent, qkv, att, resid, lse_out, aux, act, bias, tg0, tg1, lse,
):
    gain_one, gain_two = vecs[0:1, :], vecs[1:2, :]
    for r in range(2):
        rows = slice(r * HALF, (r + 1) * HALF)
        x = tok[rows, :].astype(F32)
        act[rows, :] = (x * lax.rsqrt(row_mean(x * x) + EPSILON) * gain_one).astype(BF)
        qi = lax.broadcasted_iota(jnp.int32, (HALF, SEQ), 0) + r * HALF
        ki = lax.broadcasted_iota(jnp.int32, (HALF, SEQ), 1)
        ok = (qi >= ki) & (seg_col[rows, :] == seg_row[...])
        bias[rows, :] = jnp.where(ok, 0.0, FLOOR_SCORE)
    for block in range(9):
        part = dot(act[...], w_qkv[:, block * 256 : block * 256 + 256])
        for i in range(2):
            v = part[:, i * 128 : i * 128 + 128]
            if block < 6:
                v = v * cos[...] + swap_halves(v) * sin[...]
            if block < 3:
                v = v * (1.0 / math.sqrt(HEAD_DIM))
            at = block * 256 + i * 128
            qkv[:, at : at + 128] = v.astype(BF)
    masks = head_masks()

    def pair(p, carry):
        q = qkv[:, pl.ds(pl.multiple_of(p * 128, 128), 128)]
        k = qkv[:, pl.ds(pl.multiple_of(D + p * 128, 128), 128)]
        v = qkv[:, pl.ds(pl.multiple_of(2 * D + p * 128, 128), 128)]
        for b in range(2):
            rows, reach = slice(b * HALF, (b + 1) * HALF), (b + 1) * HALF
            out = None
            for h in range(2):
                s = dot_nt(q[rows, :] * masks[h], k[:reach, :]) + bias[rows, :reach]
                top = jnp.max(s, axis=1, keepdims=True)
                e = jnp.exp(s - top)
                total = jnp.sum(e, axis=1, keepdims=True)
                o = dot((e * (1.0 / total)).astype(BF), v[:reach, :] * masks[h])
                out = o if out is None else out + o
                lse[rows, :] = jnp.where(lanes(HALF) == 2 * p + h, top + jnp.log(total), lse[rows, :])
            att[rows, pl.ds(pl.multiple_of(p * 128, 128), 128)] = out.astype(BF)
        return carry

    lax.fori_loop(0, PAIRS, pair, 0)
    lse_out[...] = lse[...].T[:16, :]
    lane = lanes(HALF)

    def column(v, at):
        return jnp.sum(jnp.where(lane == at, v, 0.0), axis=1, keepdims=True)

    for r in range(2):
        rows = slice(r * HALF, (r + 1) * HALF)
        res = tok[rows, :].astype(F32) + dot(att[rows, :], w_out[...])
        resid[rows, :] = res
        act2 = (res * lax.rsqrt(row_mean(res * res) + EPSILON) * gain_two).astype(BF)
        act[rows, :] = act2
        logits = dot(act2, w_small[...])
        router = logits + prev[rows, :].astype(F32)
        r0, r1 = column(router, route[rows, 0:1]), column(router, route[rows, 1:2])
        top = jnp.maximum(r0, r1)
        e0, e1 = jnp.exp(r0 - top), jnp.exp(r1 - top)
        g0, g1 = e0 / (e0 + e1), e1 / (e0 + e1)
        made = jnp.where(lane == 0, g0, jnp.where(lane == 1, g1, 0.0))
        for c in range(2):
            a, b = column(logits, CHOICES + 2 * c), column(logits, CHOICES + 2 * c + 1)
            top = jnp.maximum(a, b)
            ea, eb = jnp.exp(a - top), jnp.exp(b - top)
            made = jnp.where(lane == 2 + 2 * c, ea / (ea + eb), made)
            made = jnp.where(lane == 3 + 2 * c, eb / (ea + eb), made)
        aux[rows, :] = made
        g = cot[rows, :].astype(F32)
        tg0[rows, :] = (g0 * g).astype(BF)
        tg1[rows, :] = (g1 * g).astype(BF)

    def dispatch(b, carry):
        ids = lax.broadcasted_iota(jnp.int32, (256, SEQ), 0) + b * 256
        p0 = jnp.where(slot_row[0:1, :] == ids, 1.0, 0.0)
        p1 = jnp.where(slot_row[1:2, :] == ids, 1.0, 0.0)
        sent[pl.ds(b * 2, 2), 0] = dot((p0 + p1).astype(BF), act[...]).astype(BF).reshape(2, CAP, D)
        sg = dot(p0.astype(BF), tg0[...]) + dot(p1.astype(BF), tg1[...])
        sent[pl.ds(b * 2, 2), 1] = sg.astype(BF).reshape(2, CAP, D)
        return carry

    lax.fori_loop(0, SLOTS // 256, dispatch, 0)


def seq_block(width, part, col=0):
    return pl.BlockSpec((SEQ, width), lambda i, part=part, col=col: (part, col))


def fixed(shape, *at):
    at = at or (0,) * len(shape)
    return pl.BlockSpec(shape, lambda i, at=at: at)


def lasting(microseconds):
    return pl.CostEstimate(flops=microseconds * 10**9 + 1, bytes_accessed=0, transcendentals=0)


def kernel_params():
    return pltpu.CompilerParams(dimension_semantics=("arbitrary",), vmem_limit_bytes=VMEM_MOST)


def forward_part(part, t, packed, vecs):
    return pl.pallas_call(
        forward_body,
        grid=(1,),
        in_specs=[
            seq_block(D, part), seq_block(D, part), seq_block(128, part), seq_block(2, part),
            fixed((None, 2, SEQ), part, 0, 0), seq_block(1, part), fixed((None, 1, SEQ), part, 0, 0),
            seq_block(128, part), seq_block(128, part),
            fixed((D, 3 * D), 0, 0), fixed((D, D), 0, 3), fixed((D, 128), 0, 24), fixed((8, D)),
        ],
        out_specs=[
            fixed((EXPERTS, 2, CAP, D)), fixed((SEQ, 3 * D)), fixed((SEQ, D)), fixed((SEQ, D)),
            fixed((16, SEQ)), fixed((SEQ, 128)),
        ],
        out_shape=[
            jax.ShapeDtypeStruct((EXPERTS, 2, CAP, D), BF),
            jax.ShapeDtypeStruct((SEQ, 3 * D), BF),
            jax.ShapeDtypeStruct((SEQ, D), BF),
            jax.ShapeDtypeStruct((SEQ, D), F32),
            jax.ShapeDtypeStruct((16, SEQ), F32),
            jax.ShapeDtypeStruct((SEQ, 128), F32),
        ],
        scratch_shapes=[
            pltpu.VMEM((SEQ, D), BF), pltpu.VMEM((SEQ, SEQ), F32), pltpu.VMEM((SEQ, D), BF),
            pltpu.VMEM((SEQ, D), BF), pltpu.VMEM((SEQ, 128), F32),
        ],
        compiler_params=kernel_params(),
        cost_estimate=lasting(100),
    )(
        t["tokens"], t["cotangent"], t["prev"], t["routes"], t["slot_row"], t["seg_col"], t["seg_row"],
        t["cos"], t["sin"], packed, packed, packed, vecs,
    )


def combine_body(
    prior, back, resid, cot, aux, slot, route, att, w_out, w_small, vecs, p_out, p_small, p_rows,
    out, rgrad, router_out, agrad, out_w, small_w, rows_w,
):
    @pl.when(pl.program_id(0) == 0)
    def _():
        if prior:
            out_w[...], small_w[...], rows_w[...] = p_out[...], p_small[...], p_rows[...]
        else:
            out_w[...] = jnp.zeros_like(out_w)
            small_w[...] = jnp.zeros_like(small_w)
            rows_w[...] = jnp.zeros_like(rows_w)

    gain_two = vecs[1:2, :]
    consts = (vecs[2:3, :], vecs[3:4, :])
    res = resid[...]
    g = cot[...].astype(F32)
    inverse = lax.rsqrt(row_mean(res * res) + EPSILON)
    unit = res * inverse
    normed = unit * gain_two
    lane = lanes(HALF)
    gates = (aux[:, 0:1], aux[:, 1:2])
    cg = ((aux[:, 2:3], aux[:, 3:4]), (aux[:, 4:5], aux[:, 5:6]))
    ids = lax.broadcasted_iota(jnp.int32, (HALF, SLOTS), 1)
    picks = [jnp.where(slot[:, k : k + 1] == ids, 1.0, 0.0) for k in range(2)]
    rows = back[:, 0].reshape(SLOTS, D)
    g_normed = jnp.sum(g * normed, axis=1, keepdims=True)
    g_const = [jnp.sum(g * v, axis=1, keepdims=True) for v in consts]
    gate_grads, straight, total = [], 0.0, res
    const_mask = [
        [jnp.where(route[:, k : k + 1] == EXPERTS + 2 + c, 1.0, 0.0) for c in range(2)] for k in range(2)
    ]
    for k in range(2):
        combined = dot(picks[k].astype(BF), rows)
        direct = jnp.where(route[:, k : k + 1] == EXPERTS + 1, 1.0, 0.0)
        for c in range(2):
            direct += const_mask[k][c] * cg[c][0]
        grad = jnp.sum(g * combined, axis=1, keepdims=True) + direct * g_normed
        for c in range(2):
            grad += const_mask[k][c] * cg[c][1] * g_const[c]
        gate_grads.append(grad)
        straight += gates[k] * direct
        total = total + gates[k] * combined
    total = total + straight * normed
    logit_grad = 0.0
    made = [jnp.zeros((1, D), F32)] * 2
    for c in range(2):
        share = const_mask[0][c] * gates[0] + const_mask[1][c] * gates[1]
        weight = share * cg[c][1]
        total = total + weight * consts[c]
        made[c] = jnp.sum(weight * g, axis=0, keepdims=True)
        first, second = share * g_normed, share * g_const[c]
        inner = cg[c][0] * first + cg[c][1] * second
        for i, v in enumerate((first, second)):
            logit_grad += jnp.where(lane == CHOICES + 2 * c + i, cg[c][i] * (v - inner), 0.0)
    out[...] = total.astype(BF)
    mean_grad = gates[0] * gate_grads[0] + gates[1] * gate_grads[1]
    router = 0.0
    for k in range(2):
        router += jnp.where(lane == route[:, k : k + 1], gates[k] * (gate_grads[k] - mean_grad), 0.0)
    router_out[...] = router[:, :CHOICES]
    logit_low = (router + logit_grad).astype(BF)
    small_w[...] += dot_tn(normed.astype(BF), logit_low)
    normed_grad = dot_nt(logit_low, w_small[...])
    normed_grad += dot((picks[0] + picks[1]).astype(BF), back[:, 1].reshape(SLOTS, D))
    normed_grad += straight * g
    scaled = normed_grad * gain_two
    gain_grad = jnp.sum(normed_grad * unit, axis=0, keepdims=True)
    residual_grad = g + inverse * (scaled - unit * row_mean(scaled * unit))
    rgrad[...] = residual_grad
    low = residual_grad.astype(BF)
    agrad[...] = dot_nt(low, w_out[...]).astype(BF)
    out_w[...] += dot_tn(att[...], low)
    rows_w[0:1, :] += made[0]
    rows_w[1:2, :] += made[1]
    rows_w[2:3, :] += gain_grad


def combine_part(part, back, kept, t, packed, vecs, prior):
    _, _, att, resid, _, aux = kept

    def tile(width, mine=True):
        base = 0 if mine else 2 * part
        return pl.BlockSpec((HALF, width), lambda i, base=base: (base + i, 0))

    sums = [
        jax.ShapeDtypeStruct((D, D), F32), jax.ShapeDtypeStruct((D, 128), F32), jax.ShapeDtypeStruct((8, D), F32)
    ]
    sum_specs = [fixed((D, D)), fixed((D, 128)), fixed((8, D))]
    body = functools.partial(combine_body, prior is not None)
    if prior is None:
        given = []

        def body(*refs):
            combine_body(False, *refs[:10], None, None, None, *refs[10:])

    else:
        given = list(prior)
    return pl.pallas_call(
        body,
        grid=(2,),
        in_specs=[
            fixed((EXPERTS, 2, CAP, D)), tile(D), tile(D, False), tile(128), tile(2, False), tile(2, False),
            tile(D), fixed((D, D), 0, 3), fixed((D, 128), 0, 24), fixed((8, D)),
        ] + (sum_specs if given else []),
        out_specs=[tile(D), tile(D), tile(CHOICES), tile(D)] + sum_specs,
        out_shape=[
            jax.ShapeDtypeStruct((SEQ, D), BF), jax.ShapeDtypeStruct((SEQ, D), F32),
            jax.ShapeDtypeStruct((SEQ, CHOICES), F32), jax.ShapeDtypeStruct((SEQ, D), BF),
        ] + sums,
        compiler_params=kernel_params(),
        cost_estimate=lasting(0),
    )(back, resid, t["cotangent"], aux, t["slots"], t["routes"], att, packed, packed, vecs, *given)


def attention_back_body(
    qkv, agrad, lse, seg_col, seg_row, cos, sin, w_qkv, tok, vecs, rgrad, grad_in, qkv_grad, act, gain_w, bias
):
    for b in range(2):
        rows = slice(b * HALF, (b + 1) * HALF)
        ki = lax.broadcasted_iota(jnp.int32, (HALF, SEQ), 0) + b * HALF
        qi = lax.broadcasted_iota(jnp.int32, (HALF, SEQ), 1)
        ok = (qi >= ki) & (seg_col[rows, :] == seg_row[...])
        bias[rows, :] = jnp.where(ok, 0.0, FLOOR_SCORE)
    masks = head_masks()
    scale = 1.0 / math.sqrt(HEAD_DIM)

    def one_pair(p, carry):
        at = [pl.ds(pl.multiple_of(i * D + p * 128, 128), 128) for i in range(3)]
        q, k, v = [qkv[:, a] for a in at]
        da = agrad[:, at[0]]
        kg, vg, qg = [None, None], [None, None], [None, None]

        def add(store, i, value):
            store[i] = value if store[i] is None else store[i] + value

        for h in range(2):
            qh, dh = q * masks[h], da * masks[h]
            probs, grads, keyed = [], [], []
            for b in range(2):
                keys, first = slice(b * HALF, (b + 1) * HALF), b * HALF
                kh = k[keys, :] * masks[h]
                st = dot_nt(kh, q[first:, :]) + bias[keys, first:]
                probs.append(jnp.exp(st - lse[pl.ds(2 * p + h, 1), first:]))
                grads.append(dot_nt(v[keys, :] * masks[h], da[first:, :]))
                keyed.append(kh)
            inner = [jnp.sum(probs[b] * grads[b], axis=0, keepdims=True) for b in range(2)]
            late = inner[0][:, HALF:] + inner[1]
            whole = jnp.concatenate([inner[0][:, :HALF], late], axis=1)
            for b, mean in enumerate((whole, late)):
                first = b * HALF
                ds = (probs[b] * (grads[b] - mean)).astype(BF)
                add(kg, b, dot(ds, qh[first:, :]))
                add(vg, b, dot(probs[b].astype(BF), dh[first:, :]))
                full = dot_tn(ds, keyed[b])
                if b == 0:
                    add(qg, 0, full[:HALF, :])
                    add(qg, 1, full[HALF:, :])
                else:
                    add(qg, 1, full)
        for b in range(2):
            rows = slice(b * HALF, (b + 1) * HALF)
            c, s = cos[rows, :], sin[rows, :]
            qb = qg[b] * scale
            qkv_grad[rows, at[0]] = (qb * c - swap_halves(qb) * s).astype(BF)
            qkv_grad[rows, at[1]] = (kg[b] * c - swap_halves(kg[b]) * s).astype(BF)
            qkv_grad[rows, at[2]] = vg[b].astype(BF)
        return carry

    lax.fori_loop(0, PAIRS, one_pair, 0)
    gain_one = vecs[0:1, :]
    gain_grad = 0.0
    for b in range(2):
        rows = slice(b * HALF, (b + 1) * HALF)
        x = tok[rows, :].astype(F32)
        inverse = lax.rsqrt(row_mean(x * x) + EPSILON)
        unit = x * inverse
        act[rows, :] = (unit * gain_one).astype(BF)
        grad = dot_nt(qkv_grad[rows, :], w_qkv[...])
        scaled = grad * gain_one
        gain_grad += jnp.sum(grad * unit, axis=0, keepdims=True)
        grad_in[rows, :] = rgrad[rows, :] + inverse * (scaled - unit * row_mean(scaled * unit))
    gain_w[...] = jnp.broadcast_to(gain_grad, gain_w.shape)


def attention_back(part, kept, rgrad, agrad, t, packed, vecs):
    _, qkv, _, _, lse, _ = kept
    return pl.pallas_call(
        attention_back_body,
        grid=(1,),
        in_specs=[
            fixed((SEQ, 3 * D)), fixed((SEQ, D)), fixed((16, SEQ)),
            seq_block(1, part), fixed((None, 1, SEQ), part, 0, 0), seq_block(128, part), seq_block(128, part),
            fixed((D, 3 * D), 0, 0), seq_block(D, part), fixed((8, D)), fixed((SEQ, D)),
        ],
        out_specs=[fixed((SEQ, D)), fixed((SEQ, 3 * D)), fixed((SEQ, D)), fixed((8, D))],
        out_shape=[
            jax.ShapeDtypeStruct((SEQ, D), F32), jax.ShapeDtypeStruct((SEQ, 3 * D), BF),
            jax.ShapeDtypeStruct((SEQ, D), BF), jax.ShapeDtypeStruct((8, D), F32),
        ],
        scratch_shapes=[pltpu.VMEM((SEQ, SEQ), F32)],
        compiler_params=kernel_params(),
        cost_estimate=lasting(0),
    )(
        qkv, agrad, lse, t["seg_col"], t["seg_row"], t["cos"], t["sin"], packed, t["tokens"], vecs, rgrad
    )


def mixer_wgrad_body(parts, groups, *refs):
    core, acts, grads, gains = refs[0], refs[1 : 1 + parts], refs[1 + parts : 1 + 2 * parts], refs[1 + 2 * parts : 1 + 3 * parts]
    small, rows, give, keep, turned, last = refs[1 + 3 * parts :]
    step, half = pl.program_id(0), D // 2
    chunk = half // groups

    def scattered(store, across, value):
        for group in range(groups):
            for c in range(2):
                kept = (core[0] == c).astype(jnp.int32)
                at = pl.ds(pl.multiple_of(kept * half + group * chunk, 16), chunk)
                first = (2 * group + c) * chunk
                store[at, across] = value[first : first + chunk, :]

    @pl.when(step == 0)
    def _():
        for i in range(parts):
            scattered(turned, slice(i * SEQ, (i + 1) * SEQ), acts[i][...].T)

    @pl.when(step < 9)
    def _():
        made = dot(turned[...], jnp.concatenate([v[...] for v in grads], axis=0)).astype(BF)
        give[...] = made[:half, :]
        keep[...] = made[half:, :]

    @pl.when(step == 9)
    def _():
        gain_one = sum(v[0:1, :] for v in gains)
        line = lax.broadcasted_iota(jnp.int32, (128, D), 0)
        stacked = 0.0
        for i, row in enumerate((rows[0:1, :], rows[1:2, :], gain_one, rows[2:3, :])):
            stacked += jnp.where(line == 16 + i, row, 0.0)
        scattered(last, slice(0, 128), (small[...] + stacked.T).astype(BF))
        give[:, :128] = last[:half, :]
        keep[:, :128] = last[half:, :]
        give[:, 128:] = jnp.zeros((half, 128), BF)
        keep[:, 128:] = jnp.zeros((half, 128), BF)


def mixer_wgrad(acts, grads, gains, small, rows, groups, core):
    parts = len(acts)
    half = pl.BlockSpec((D // 2, 256), lambda i: (0, i))
    out = jax.ShapeDtypeStruct((D // 2, 3 * D + 256), BF)
    return pl.pallas_call(
        functools.partial(mixer_wgrad_body, parts, groups),
        grid=(10,),
        in_specs=[pl.BlockSpec(memory_space=pltpu.SMEM)]
        + [fixed((SEQ, D))] * parts
        + [pl.BlockSpec((SEQ, 256), lambda i: (0, jnp.minimum(i, 8)))] * parts
        + [fixed((8, D))] * parts
        + [fixed((D, 128)), fixed((8, D))],
        out_specs=[half, half],
        out_shape=[out, out],
        scratch_shapes=[pltpu.VMEM((D, parts * SEQ), BF), pltpu.VMEM((D, 128), BF)],
        compiler_params=kernel_params(),
        cost_estimate=lasting(0),
    )(jnp.stack([core]).astype(jnp.int32), *acts, *grads, *gains, small, rows)


def tables(tokens, cotangent, prev_logits, routes, capacity, segments, positions):
    parts = tokens.shape[0] // SEQ
    slots = jnp.concatenate(
        [pair_slots(routes[i * SEQ : (i + 1) * SEQ], capacity) for i in range(parts)]
    )
    lane = jnp.arange(128) % HEAD_DIM
    frequency = jnp.exp((lane % (HEAD_DIM // 2)).astype(F32) * (-2.0 * math.log(ROPE_BASE) / HEAD_DIM))
    angles = positions.astype(F32)[:, None] * frequency[None, :]
    sign = jnp.where(lane < HEAD_DIM // 2, -1.0, 1.0)
    return dict(
        tokens=tokens,
        cotangent=cotangent,
        prev=jnp.pad(prev_logits, ((0, 0), (0, 128 - CHOICES))),
        routes=routes,
        slots=slots,
        slot_row=slots.reshape(parts, SEQ, 2).transpose(0, 2, 1),
        seg_col=segments[:, None],
        seg_row=segments.reshape(parts, 1, SEQ),
        cos=jnp.cos(angles),
        sin=jnp.sin(angles) * sign,
    )


FC = 512


def expert_rows_body(x_ref, g_ref, wg_ref, wu_ref, wd_ref, hid_ref, dg_ref, du_ref, out_ref, acc, racc):
    step = pl.program_id(0)
    x = x_ref[:, 0].reshape(-1, D)
    g = g_ref[:, 0].reshape(-1, D)
    wg, wu, wd = wg_ref[...], wu_ref[...], wd_ref[...]
    gate = dot(x, wg)
    up = dot(x, wu)
    hgrad = dot_nt(g, wd).astype(BF).astype(F32)
    sig = 1.0 / (1.0 + jnp.exp(-gate))
    act = gate * sig
    hidden = (act * up).astype(BF)
    dgate = (hgrad * up * sig * (1.0 + gate * (1.0 - sig))).astype(BF)
    dup = (hgrad * act).astype(BF)
    hid_ref[...] = hidden
    dg_ref[...] = dgate
    du_ref[...] = dup
    prod = dot(hidden, wd)
    rgrad = dot_nt(dgate, wg) + dot_nt(dup, wu)

    @pl.when(step == 0)
    def _():
        acc[...] = prod
        racc[...] = rgrad

    @pl.when(step > 0)
    def _():
        acc[...] += prod
        racc[...] += rgrad

    @pl.when(step == pl.num_programs(0) - 1)
    def _():
        out_ref[:, 0] = acc[...].astype(BF).reshape(-1, CAP, D)
        out_ref[:, 1] = racc[...].astype(BF).reshape(-1, CAP, D)


def expert_rows(received, w_gate_up, w_down):
    n = received.shape[0]
    rows = n * CAP
    steps = FF // FC
    wide = jax.ShapeDtypeStruct((rows, FF), BF)
    block = pl.BlockSpec((rows, FC), lambda j: (0, j))
    return pl.pallas_call(
        expert_rows_body,
        grid=(steps,),
        in_specs=[
            pl.BlockSpec((n, 1, CAP, D), lambda j: (0, 0, 0, 0)),
            pl.BlockSpec((n, 1, CAP, D), lambda j: (0, 1, 0, 0)),
            pl.BlockSpec((D, FC), lambda j: (0, j)),
            pl.BlockSpec((D, FC), lambda j: (0, steps + j)),
            pl.BlockSpec((FC, D), lambda j: (j, 0)),
        ],
        out_specs=[block, block, block, pl.BlockSpec((n, 2, CAP, D), lambda j: (0, 0, 0, 0))],
        out_shape=[wide, wide, wide, jax.ShapeDtypeStruct((n, 2, CAP, D), BF)],
        scratch_shapes=[pltpu.VMEM((rows, D), F32), pltpu.VMEM((rows, D), F32)],
        compiler_params=pltpu.CompilerParams(
            dimension_semantics=("arbitrary",), vmem_limit_bytes=VMEM_MOST
        ),
        cost_estimate=lasting(28),
    )(received, received, w_gate_up, w_gate_up, w_down)


FW = 512


def down_wgrad_body(parts, *refs):
    hid, received, out = refs[:parts], refs[parts : 2 * parts], refs[2 * parts]
    rows = jnp.concatenate([v[:, 0].reshape(-1, D) for v in received], axis=0)
    out[...] = dot_tn(jnp.concatenate([v[...] for v in hid], axis=0), rows).astype(BF)


def down_wgrad(received, hid):
    parts, (n, _, _, _) = len(received), received[0].shape
    return pl.pallas_call(
        functools.partial(down_wgrad_body, parts),
        grid=(FF // FW,),
        in_specs=[pl.BlockSpec((n * CAP, FW), lambda j: (0, j))] * parts
        + [pl.BlockSpec((n, 1, CAP, D), lambda j: (0, 1, 0, 0))] * parts,
        out_specs=pl.BlockSpec((FW, D), lambda j: (j, 0)),
        out_shape=jax.ShapeDtypeStruct((FF, D), BF),
        compiler_params=kernel_params(),
        cost_estimate=lasting(10),
    )(*hid, *received)


def gate_up_wgrad_body(parts, *refs):
    received, dg, du = refs[:parts], refs[parts : 2 * parts], refs[2 * parts : 3 * parts]
    out, xt = refs[3 * parts :]
    rows = received[0].shape[0] * CAP

    @pl.when(pl.program_id(0) == 0)
    def _():
        for i in range(parts):
            xt[:, i * rows : (i + 1) * rows] = received[i][:, 0].reshape(rows, D).T

    for k, grads in enumerate((dg, du)):
        out[k] = dot(xt[...], jnp.concatenate([v[...] for v in grads], axis=0)).astype(BF)


def gate_up_wgrad(received, dg, du):
    parts, (n, _, _, _) = len(received), received[0].shape
    return pl.pallas_call(
        functools.partial(gate_up_wgrad_body, parts),
        grid=(FF // FW,),
        in_specs=[pl.BlockSpec((n, 1, CAP, D), lambda j: (0, 0, 0, 0))] * parts
        + [pl.BlockSpec((n * CAP, FW), lambda j: (0, j))] * (2 * parts),
        out_specs=pl.BlockSpec((2, D, FW), lambda j: (0, 0, j)),
        out_shape=jax.ShapeDtypeStruct((2, D, FF), BF),
        scratch_shapes=[pltpu.VMEM((D, parts * n * CAP), BF)],
        compiler_params=kernel_params(),
        cost_estimate=lasting(0),
    )(*received, *dg, *du)


def place_body(spots, count, *refs):
    offsets, blocks, outs, sems = refs[0], refs[1 : 1 + count], refs[1 + count : -1], refs[-1]
    copies = []
    for i, (block, row, rows, column, columns, out) in enumerate(spots):
        down = pl.ds(pl.multiple_of(offsets[2 * i], 16), rows)
        across = pl.ds(pl.multiple_of(offsets[2 * i + 1], 128), columns)
        copies.append(
            pltpu.make_async_copy(
                blocks[block].at[pl.ds(row, rows), pl.ds(column, columns)],
                outs[out].at[down, across],
                sems.at[i],
            )
        )
    for copy in copies:
        copy.start()
    for copy in copies:
        copy.wait()


def place(blocks, spots, offsets, shapes):
    anywhere = pl.BlockSpec(memory_space=pl.ANY)
    return pl.pallas_call(
        functools.partial(place_body, spots, len(blocks)),
        in_specs=[pl.BlockSpec(memory_space=pltpu.SMEM)] + [anywhere] * len(blocks),
        out_specs=[pl.BlockSpec(memory_space=pltpu.VMEM)] * len(shapes),
        out_shape=[jax.ShapeDtypeStruct(v, BF) for v in shapes],
        scratch_shapes=[pltpu.SemaphoreType.DMA((len(spots),))],
        compiler_params=pltpu.CompilerParams(vmem_limit_bytes=VMEM_MOST),
        cost_estimate=lasting(0),
    )(jnp.stack(offsets).astype(jnp.int32), *blocks)


def pick(value, index, axis=0):
    return lax.dynamic_index_in_dim(value, index, axis, False)


def added(*values):
    return sum(v.astype(F32) for v in values).astype(BF)


class Paired:
    axes = ("half", "low", "inner", "side", "core")
    fsdp = ("half", "low", "inner")
    expert = ("side", "core")
    rows = ("side", "low", "inner")
    route_axes = ("half", "low", "inner", "core")
    near = 896
    cut = 3072

    def __init__(self, mesh):
        self.mesh = Mesh(mesh.devices.reshape(2, 2, 2, 2, 2), self.axes)
        self.routes = []
        for turn in range(4):
            pairs = []
            for z in range(4):
                for y in range(2):
                    for c in range(2):
                        half, inner = (z ^ turn) >> 1, (z ^ turn) & 1
                        pairs.append(((z * 2 + y) * 2 + c, ((half * 2 + c) * 2 + inner) * 2 + y))
            self.routes.append(pairs)

    @staticmethod
    def swap(value, axis="core"):
        return lax.ppermute(value, axis, [(0, 1), (1, 0)])

    @staticmethod
    def along(value, turn):
        return lax.ppermute(value, ("half", "low"), [(i, i ^ turn) for i in range(4)])

    @staticmethod
    def spot():
        z = lax.axis_index("half") * 2 + lax.axis_index("low")
        return z, lax.axis_index("inner"), lax.axis_index("side"), lax.axis_index("core")

    @staticmethod
    def joined(gate_up, down):
        high, edge = gate_up.shape[1], D - 256
        tail = down[:, 2 * high :]
        half = tail.shape[1] // 2
        under = jnp.concatenate([tail[:, :half, edge:], tail[:, half:, edge:]], axis=2)
        last = jnp.concatenate([tail[:, :, :edge], under], axis=1)
        cut = Paired.cut
        rest = jnp.concatenate([gate_up[:, :, cut:], down[:, :high], down[:, high : 2 * high], last], axis=2)
        return gate_up[:, :, :cut], rest

    @staticmethod
    def rects(high, deep):
        half, edge, at = deep // 2 - high, D - 256, 2 * FF - Paired.cut
        yield 0, high, at, D, 0, 0
        yield 0, high, at + D, D, high, 0
        yield 0, 2 * half, at + 2 * D, edge, 2 * high, 0
        yield 2 * half, half, at + 2 * D, 256, 2 * high, edge
        yield 2 * half, half, at + 2 * D + 256, 256, 2 * high + half, edge

    def send(self, joined, turn, part):
        mine = pick(joined[part], (self.spot()[0] ^ turn) & 1)
        return lax.ppermute(mine, self.route_axes, self.routes[turn])

    def gather_shared(self, shard, weights, early):
        z, y, x, c = self.spot()
        rows, width = shard.shape
        rows, width = rows // 2, width // 2
        mine = lax.dynamic_slice(shard, (c * rows, x * width), (rows, width))
        stack = jnp.concatenate([mine] + [self.along(mine, turn) for turn in (1, 2, 3)])
        stack, joined, early = lax.optimization_barrier((stack, self.joined(*weights), early))
        sent = {(2, 0): (self.send(joined, 2, 0), None)}
        over_y, over_x = self.swap(stack, "inner"), self.swap(stack, "side")
        far = self.swap(over_y[:, : self.near], "side"), self.swap(over_x[:, self.near :], "inner")
        blocks = [stack, over_y, over_x, *far]
        flips = [(0, 0, 0), (1, 0, 0), (0, 1, 0), (1, 1, 0), (1, 1, self.near)]
        spots, offsets = [], []
        for i, (dy, dx, column) in enumerate(flips + flips):
            core = c if i < len(flips) else 1 - c
            for turn in range(4):
                spots.append((i, turn * rows, rows, 0, blocks[i % len(flips)].shape[1], 0))
                offsets += [((z ^ turn) * 2 + (y ^ dy)) * 2 * rows + core * rows, (x ^ dx) * width + column]
        blocks += [self.swap(v) for v in blocks]
        blocks, joined, sent = lax.optimization_barrier((blocks, joined, sent))
        [full] = place(blocks, spots, offsets, [(16 * rows, 2 * width)])
        return full, early, (joined, sent)

    def gather_more(self, held, value, names):
        joined, sent = held
        more = {v: (self.send(joined, *v), None) for v in names}
        waiting = [v for v, (_, other) in sent.items() if other is None][:2]
        done = {**sent, **{v: (sent[v][0], self.swap(sent[v][0])) for v in waiting}}
        value, joined, sent = lax.optimization_barrier((value, joined, {**done, **more}))
        return (joined, sent), value

    def split(self):
        return 8, lax.axis_index("core")

    def halves(self, total):
        c = lax.axis_index("core")
        total = total.reshape(8, 2, total.shape[0] // 16, total.shape[1])
        return pick(total, 1 - c, 1), pick(total, c, 1)

    def reduce_first(self, give, keep):
        z, y, x, c = self.spot()
        width = give.shape[-1] // 2
        near = (width // 128 + 1) // 2 * 128
        parts = added(keep, self.swap(give)).reshape(4, 2, -1, 2 * width)

        def columns(value, first, count):
            return lax.dynamic_slice_in_dim(value, first, count, value.ndim - 1)

        one = added(columns(parts, x * width, near), self.swap(columns(parts, (1 - x) * width, near), "side"))
        two = jnp.concatenate([parts[..., near:width], parts[..., width + near :]], axis=3)
        two = added(pick(two, y, 1), self.swap(pick(two, 1 - y, 1), "inner"))
        return one, two

    def reduce_last(self, one, two):
        z, y, x, c = self.spot()
        rest = two.shape[2] // 2
        one = added(pick(one, y, 1), self.swap(pick(one, 1 - y, 1), "inner"))
        near = lax.dynamic_slice_in_dim(two, x * rest, rest, 2)
        two = added(near, self.swap(lax.dynamic_slice_in_dim(two, (1 - x) * rest, rest, 2), "side"))
        both = jnp.concatenate([one, two], axis=2)
        mine = added(pick(both, z), *[self.along(pick(both, z ^ turn), turn) for turn in (1, 2, 3)])
        other = self.swap(mine, "side")
        line = jnp.where(x == 0, jnp.concatenate([mine, other], 1), jnp.concatenate([other, mine], 1))
        other = self.swap(line)
        both = jnp.where(c == 0, jnp.concatenate([line, other]), jnp.concatenate([other, line]))
        return both.astype(F32)

    def gather_expert(self, held, shapes):
        sent = held[1]
        c = lax.axis_index("core")
        here = lax.axis_index("half") * 2 + lax.axis_index("inner")
        both = [sent[turn, part] for turn in range(4) for part in range(2)]
        blocks = [v for v, _ in both] + [self.swap(v) if other is None else other for v, other in both]
        high, deep = shapes[0][1], shapes[1][1]
        spots, offsets, zero = [], [], jnp.int32(0)
        for i in range(0, 16, 2):
            shard = (here ^ (i // 2 % 4)) * 2 + (c if i < 8 else 1 - c)
            spots += [(i, 0, high, 0, self.cut, 0), (i + 1, 0, high, 0, 2 * FF - self.cut, 0)]
            offsets += [shard * high, zero, shard * high, zero + self.cut]
            for row, rows, column, columns, to_row, to_column in self.rects(high, deep):
                spots.append((i + 1, row, rows, column, columns, 1))
                offsets += [shard * deep + to_row, zero + to_column]
        return place(blocks, spots, offsets, [(8 * high, 2 * FF), (8 * deep, D)])

    def scatter_start(self, grad, axis):
        c = lax.axis_index("core")
        shape = grad.shape
        grad = grad.reshape(shape[:axis] + (4, 2, shape[axis] // 8) + shape[axis + 1 :])
        return added(pick(grad, c, axis + 1), self.swap(pick(grad, 1 - c, axis + 1)))

    def scatter_send(self, parts, axis):
        here = lax.axis_index("half") * 2 + lax.axis_index("inner")
        got = {}
        for turn in (2, 3, 0, 1):
            back = [(b, a) for a, b in self.routes[turn]]
            got[turn] = lax.ppermute(pick(parts, here ^ turn, axis), self.route_axes, back)
        return got

    def scatter_end(self, got, axis):
        even = (self.spot()[0] & 1) == 0
        first, second = [got[i].astype(F32) + got[i + 2].astype(F32) for i in range(2)]
        return jnp.stack([jnp.where(even, first, second), jnp.where(even, second, first)])


class Plain:
    axes = ("outer", "inner", "expert")
    fsdp = ("outer", "inner")
    expert = ("expert",)
    rows = ("expert", "inner")

    def __init__(self, mesh):
        fsdp, expert = mesh.shape["fsdp"], mesh.shape["expert"]
        inner = EXPERTS // expert
        self.mesh = Mesh(mesh.devices.reshape(fsdp // inner, inner, expert), self.axes)

    def gather_shared(self, shard, weights, early):
        return lax.all_gather(shard, self.fsdp, axis=0, tiled=True), early, weights

    def gather_more(self, held, value, names):
        return held, value

    def split(self):
        return 1, jnp.int32(1)

    def halves(self, total):
        return jnp.split(total, 2)

    def reduce_first(self, give, keep):
        return jnp.concatenate([give, keep]), None

    def reduce_last(self, total, _):
        total = lax.psum_scatter(total, self.axes, scatter_dimension=0, tiled=True)
        return lax.all_gather(total, self.expert, axis=0, tiled=True).astype(F32)

    def gather_expert(self, weights, shapes):
        full = []
        for weight in weights:
            own = lax.all_to_all(weight, "inner", 0, 0, tiled=True)
            own = lax.all_gather(own, "outer", axis=0, tiled=True)
            full.append(own.reshape((-1,) + weight.shape[2:]))
        return full

    def scatter_start(self, grad, axis):
        return grad

    def scatter_send(self, grad, axis):
        return grad

    def scatter_end(self, grad, axis):
        inner = lax.axis_size("inner")
        part = lax.psum_scatter(grad, "outer", scatter_dimension=axis, tiled=True)
        shape = part.shape
        part = part.reshape(shape[:axis] + (inner, shape[axis] // inner) + shape[axis + 1 :])
        part = jnp.moveaxis(part, axis, 0)
        return lax.all_to_all(part, "inner", 0, 0, tiled=True).astype(F32)


def solution(mesh):
    plan = Paired(mesh) if (mesh.shape["fsdp"], mesh.shape["expert"]) == (8, 4) else Plain(mesh)

    def on_device(
        tokens, cotangent, prev_logits, routes, capacity, segments, positions,
        w_qkv, w_out, gate_matrix, const_values, attn_gain, moe_gain, w_gate_up, w_down,
    ):
        rows = w_qkv.shape[0]
        pad = jnp.zeros((rows, 256 - 20), BF)
        small = jnp.concatenate(
            [gate_matrix, const_values, attn_gain[:, None], moe_gain[:, None], pad], axis=1
        )
        shard = jnp.concatenate([w_qkv, w_out, small], axis=1)
        t = tables(tokens, cotangent, prev_logits, routes, capacity, segments, positions)
        packed, t, held = plan.gather_shared(shard, (w_gate_up, w_down), t)
        columns = packed[:, 4 * D + 16 : 4 * D + 20].astype(F32).T
        vecs = jnp.concatenate([columns[2:], columns[:2], jnp.zeros((4, D), F32)])
        parts = tokens.shape[0] // SEQ
        kept, sends, shared = [], [], packed
        for i in range(parts):
            if i == 1:
                held, (shared, kept[0][5]) = plan.gather_more(held, (packed, kept[0][5]), ((2, 1), (0, 0), (0, 1), (1, 0)))
            kept.append(list(forward_part(i, t, shared, vecs)))
            sends.append(kept[i][0])
        held, sends[-1] = plan.gather_more(held, sends[-1], ((3, 0), (3, 1), (1, 1)))
        gate_up_full, down_full = plan.gather_expert(held, (w_gate_up.shape, w_down.shape))
        received = [lax.all_to_all(v, plan.rows, 0, 0, tiled=True) for v in sends]
        made = [expert_rows(r, gate_up_full, down_full) for r in received]
        hid, dg, du = [[m[i] for m in made] for i in range(3)]
        backs = [m[3] for m in made]
        gate_up_w = gate_up_wgrad(received, dg, du)
        backs[-1], hid, gate_up_w = lax.optimization_barrier((backs[-1], hid, gate_up_w))
        returned = [lax.all_to_all(v, plan.rows, 0, 0, tiled=True) for v in backs]
        gate_up_sums = plan.scatter_start(gate_up_w, 1)
        down_w = down_wgrad(received, hid)
        returned[0], gate_up_sums, down_w = lax.optimization_barrier((returned[0], gate_up_sums, down_w))
        gate_up_got = plan.scatter_send(gate_up_sums, 1)
        down_sums = plan.scatter_start(down_w, 0)
        firsts, lasts, sums = [], [], None
        for i in range(parts):
            *first, out_w, small_w, rows_w = combine_part(i, returned[i], kept[i], t, packed, vecs, sums)
            sums = (out_w, small_w, rows_w)
            firsts.append(first)
            if i == parts - 1:
                held = (gate_up_got, down_sums, first[1], [v[3] for v in lasts])
                gate_up_got, down_sums, first[1], _ = lax.optimization_barrier(held)
                down_got = plan.scatter_send(down_sums, 0)
            lasts.append(attention_back(i, kept[i], first[1], first[3], t, packed, vecs))
            if i == 0:
                returned[-1], sums, _ = lax.optimization_barrier((returned[-1], sums, lasts[0][3]))
        out_total = plan.reduce_last(*plan.reduce_first(*plan.halves(sums[0].astype(BF))))
        acts = [v[2] for v in lasts]
        halves = mixer_wgrad(
            acts, [v[1] for v in lasts], [v[3] for v in lasts], sums[1], sums[2], *plan.split()
        )
        halves, down_got = lax.optimization_barrier((halves, down_got))
        down_total = plan.scatter_end(down_got, 0)
        total = plan.reduce_last(*plan.reduce_first(*halves))
        gate_up_total = plan.scatter_end(gate_up_got, 1)
        gate_up_total = jnp.concatenate([gate_up_total[:, 0], gate_up_total[:, 1]], axis=2)
        return (
            jnp.concatenate([v[0] for v in firsts]),
            jnp.concatenate([v[0] for v in lasts]),
            jnp.concatenate([v[2] for v in firsts]),
            total[:, : 3 * D],
            out_total,
            total[:, 3 * D : 3 * D + 16],
            total[:, 3 * D + 16 : 3 * D + 18],
            total[:, 3 * D + 18],
            total[:, 3 * D + 19],
            gate_up_total,
            down_total,
        )

    every = plan.fsdp + plan.expert
    split = P(every, None)
    shard = P(plan.fsdp, None)
    line = P(plan.fsdp)
    whole = P(plan.expert, plan.fsdp, None)
    return jax.shard_map(
        on_device,
        mesh=plan.mesh,
        in_specs=(
            split, split, split, split, P(), P(every), P(every),
            shard, shard, shard, shard, line, line, whole, whole,
        ),
        out_specs=(split, split, split, shard, shard, shard, shard, line, line, whole, whole),
        check_vma=False,
    )
```

```python
import functools
import math

import jax
import jax.numpy as jnp
from jax import lax
from jax.experimental import pallas as pl
from jax.experimental.pallas import tpu as pltpu
from jax.sharding import Mesh
from jax.sharding import PartitionSpec as P

D = 768
HEADS = 12
HEAD_DIM = 64
FF = 2048
EXPERTS = 8
SEQ = 512
CAP = 128
CHOICES = EXPERTS + 4
SLOTS = EXPERTS * CAP

EPSILON = 1e-05
ROPE_BASE = 10000.0
FLOOR_SCORE = -1e30
HIGHEST = lax.Precision.HIGHEST
BF = jnp.bfloat16
F32 = jnp.float32
VMEM_MOST = 56 * 2**20


def dot(a, b):
    return jnp.dot(a, b, preferred_element_type=F32)


def dot_nt(a, b):
    return lax.dot_general(a, b, (((1,), (1,)), ((), ())), preferred_element_type=F32)


def dot_tn(a, b):
    return lax.dot_general(a, b, (((0,), (0,)), ((), ())), preferred_element_type=F32)


def pair_slots(route, capacity):
    route_hot = (route[:, :, None] == jnp.arange(CHOICES, dtype=jnp.int32)).astype(F32)
    seq_index = jnp.arange(SEQ)
    before = (seq_index[:, None] > seq_index[None, :]).astype(BF)
    earlier = dot(before, jnp.sum(route_hot, axis=1).astype(BF))
    slot_rank = jnp.sum(earlier[:, None, :] * route_hot, axis=-1)
    cap_limit = jnp.sum(route_hot[:, :, :EXPERTS] * capacity.astype(F32), axis=-1)
    kept_pairs = (route < EXPERTS) & (slot_rank < cap_limit)
    return jnp.where(kept_pairs, route * CAP + slot_rank.astype(jnp.int32), -1)


HALF = SEQ // 2
PAIRS = HEADS // 2


def lanes(rows):
    return lax.broadcasted_iota(jnp.int32, (rows, 128), 1)


def swap_halves(v):
    low = lanes(v.shape[0]) % HEAD_DIM < HEAD_DIM // 2
    return jnp.where(low, pltpu.roll(v, 128 - HEAD_DIM // 2, 1), pltpu.roll(v, HEAD_DIM // 2, 1))


def row_mean(v):
    return jnp.sum(v, axis=1, keepdims=True) * (1.0 / D)


def head_masks():
    low = lax.broadcasted_iota(jnp.int32, (1, 128), 1) < HEAD_DIM
    return (jnp.where(low, 1.0, 0.0).astype(BF), jnp.where(low, 0.0, 1.0).astype(BF))


def forward_body(
    tok, cot, prev, route, slot_row, seg_col, seg_row, cos, sin, w_qkv, w_out, w_small, vecs,
    sent, qkv, att, resid, lse_out, aux, act, bias, tg0, tg1, lse,
):
    gain_one, gain_two = vecs[0:1, :], vecs[1:2, :]
    for r in range(2):
        rows = slice(r * HALF, (r + 1) * HALF)
        x = tok[rows, :].astype(F32)
        act[rows, :] = (x * lax.rsqrt(row_mean(x * x) + EPSILON) * gain_one).astype(BF)
        qi = lax.broadcasted_iota(jnp.int32, (HALF, SEQ), 0) + r * HALF
        ki = lax.broadcasted_iota(jnp.int32, (HALF, SEQ), 1)
        ok = (qi >= ki) & (seg_col[rows, :] == seg_row[...])
        bias[rows, :] = jnp.where(ok, 0.0, FLOOR_SCORE)
    for block in range(9):
        part = dot(act[...], w_qkv[:, block * 256 : block * 256 + 256])
        for i in range(2):
            v = part[:, i * 128 : i * 128 + 128]
            if block < 6:
                v = v * cos[...] + swap_halves(v) * sin[...]
            if block < 3:
                v = v * (1.0 / math.sqrt(HEAD_DIM))
            at = block * 256 + i * 128
            qkv[:, at : at + 128] = v.astype(BF)
    masks = head_masks()

    def pair(p, carry):
        q = qkv[:, pl.ds(pl.multiple_of(p * 128, 128), 128)]
        k = qkv[:, pl.ds(pl.multiple_of(D + p * 128, 128), 128)]
        v = qkv[:, pl.ds(pl.multiple_of(2 * D + p * 128, 128), 128)]
        for b in range(2):
            rows, reach = slice(b * HALF, (b + 1) * HALF), (b + 1) * HALF
            out = None
            for h in range(2):
                s = dot_nt(q[rows, :] * masks[h], k[:reach, :]) + bias[rows, :reach]
                top = jnp.max(s, axis=1, keepdims=True)
                e = jnp.exp(s - top)
                total = jnp.sum(e, axis=1, keepdims=True)
                o = dot((e * (1.0 / total)).astype(BF), v[:reach, :] * masks[h])
                out = o if out is None else out + o
                lse[rows, :] = jnp.where(lanes(HALF) == 2 * p + h, top + jnp.log(total), lse[rows, :])
            att[rows, pl.ds(pl.multiple_of(p * 128, 128), 128)] = out.astype(BF)
        return carry

    lax.fori_loop(0, PAIRS, pair, 0)
    lse_out[...] = lse[...].T[:16, :]
    lane = lanes(HALF)

    def column(v, at):
        return jnp.sum(jnp.where(lane == at, v, 0.0), axis=1, keepdims=True)

    for r in range(2):
        rows = slice(r * HALF, (r + 1) * HALF)
        res = tok[rows, :].astype(F32) + dot(att[rows, :], w_out[...])
        resid[rows, :] = res
        act2 = (res * lax.rsqrt(row_mean(res * res) + EPSILON) * gain_two).astype(BF)
        act[rows, :] = act2
        logits = dot(act2, w_small[...])
        router = logits + prev[rows, :].astype(F32)
        r0, r1 = column(router, route[rows, 0:1]), column(router, route[rows, 1:2])
        top = jnp.maximum(r0, r1)
        e0, e1 = jnp.exp(r0 - top), jnp.exp(r1 - top)
        g0, g1 = e0 / (e0 + e1), e1 / (e0 + e1)
        made = jnp.where(lane == 0, g0, jnp.where(lane == 1, g1, 0.0))
        for c in range(2):
            a, b = column(logits, CHOICES + 2 * c), column(logits, CHOICES + 2 * c + 1)
            top = jnp.maximum(a, b)
            ea, eb = jnp.exp(a - top), jnp.exp(b - top)
            made = jnp.where(lane == 2 + 2 * c, ea / (ea + eb), made)
            made = jnp.where(lane == 3 + 2 * c, eb / (ea + eb), made)
        aux[rows, :] = made
        g = cot[rows, :].astype(F32)
        tg0[rows, :] = (g0 * g).astype(BF)
        tg1[rows, :] = (g1 * g).astype(BF)

    def dispatch(b, carry):
        ids = lax.broadcasted_iota(jnp.int32, (256, SEQ), 0) + b * 256
        p0 = jnp.where(slot_row[0:1, :] == ids, 1.0, 0.0)
        p1 = jnp.where(slot_row[1:2, :] == ids, 1.0, 0.0)
        sent[pl.ds(b * 2, 2), 0] = dot((p0 + p1).astype(BF), act[...]).astype(BF).reshape(2, CAP, D)
        sg = dot(p0.astype(BF), tg0[...]) + dot(p1.astype(BF), tg1[...])
        sent[pl.ds(b * 2, 2), 1] = sg.astype(BF).reshape(2, CAP, D)
        return carry

    lax.fori_loop(0, SLOTS // 256, dispatch, 0)


def seq_block(width, part, col=0):
    return pl.BlockSpec((SEQ, width), lambda i, part=part, col=col: (part, col))


def fixed(shape, *at):
    at = at or (0,) * len(shape)
    return pl.BlockSpec(shape, lambda i, at=at: at)


def lasting(microseconds):
    return pl.CostEstimate(flops=microseconds * 10**9 + 1, bytes_accessed=0, transcendentals=0)


def kernel_params():
    return pltpu.CompilerParams(dimension_semantics=("arbitrary",), vmem_limit_bytes=VMEM_MOST)


def forward_part(part, t, packed, vecs):
    return pl.pallas_call(
        forward_body,
        grid=(1,),
        in_specs=[
            seq_block(D, part), seq_block(D, part), seq_block(128, part), seq_block(2, part),
            fixed((None, 2, SEQ), part, 0, 0), seq_block(1, part), fixed((None, 1, SEQ), part, 0, 0),
            seq_block(128, part), seq_block(128, part),
            fixed((D, 3 * D), 0, 0), fixed((D, D), 0, 3), fixed((D, 128), 0, 24), fixed((8, D)),
        ],
        out_specs=[
            fixed((EXPERTS, 2, CAP, D)), fixed((SEQ, 3 * D)), fixed((SEQ, D)), fixed((SEQ, D)),
            fixed((16, SEQ)), fixed((SEQ, 128)),
        ],
        out_shape=[
            jax.ShapeDtypeStruct((EXPERTS, 2, CAP, D), BF),
            jax.ShapeDtypeStruct((SEQ, 3 * D), BF),
            jax.ShapeDtypeStruct((SEQ, D), BF),
            jax.ShapeDtypeStruct((SEQ, D), F32),
            jax.ShapeDtypeStruct((16, SEQ), F32),
            jax.ShapeDtypeStruct((SEQ, 128), F32),
        ],
        scratch_shapes=[
            pltpu.VMEM((SEQ, D), BF), pltpu.VMEM((SEQ, SEQ), F32), pltpu.VMEM((SEQ, D), BF),
            pltpu.VMEM((SEQ, D), BF), pltpu.VMEM((SEQ, 128), F32),
        ],
        compiler_params=kernel_params(),
        cost_estimate=lasting(100),
    )(
        t["tokens"], t["cotangent"], t["prev"], t["routes"], t["slot_row"], t["seg_col"], t["seg_row"],
        t["cos"], t["sin"], packed, packed, packed, vecs,
    )


def combine_body(
    prior, back, resid, cot, aux, slot, route, att, w_out, w_small, vecs, p_out, p_small, p_rows,
    out, rgrad, router_out, agrad, out_w, small_w, rows_w,
):
    @pl.when(pl.program_id(0) == 0)
    def _():
        if prior:
            out_w[...], small_w[...], rows_w[...] = p_out[...], p_small[...], p_rows[...]
        else:
            out_w[...] = jnp.zeros_like(out_w)
            small_w[...] = jnp.zeros_like(small_w)
            rows_w[...] = jnp.zeros_like(rows_w)

    gain_two = vecs[1:2, :]
    consts = (vecs[2:3, :], vecs[3:4, :])
    res = resid[...]
    g = cot[...].astype(F32)
    inverse = lax.rsqrt(row_mean(res * res) + EPSILON)
    unit = res * inverse
    normed = unit * gain_two
    lane = lanes(HALF)
    gates = (aux[:, 0:1], aux[:, 1:2])
    cg = ((aux[:, 2:3], aux[:, 3:4]), (aux[:, 4:5], aux[:, 5:6]))
    ids = lax.broadcasted_iota(jnp.int32, (HALF, SLOTS), 1)
    picks = [jnp.where(slot[:, k : k + 1] == ids, 1.0, 0.0) for k in range(2)]
    rows = back[:, 0].reshape(SLOTS, D)
    g_normed = jnp.sum(g * normed, axis=1, keepdims=True)
    g_const = [jnp.sum(g * v, axis=1, keepdims=True) for v in consts]
    gate_grads, straight, total = [], 0.0, res
    const_mask = [
        [jnp.where(route[:, k : k + 1] == EXPERTS + 2 + c, 1.0, 0.0) for c in range(2)] for k in range(2)
    ]
    for k in range(2):
        combined = dot(picks[k].astype(BF), rows)
        direct = jnp.where(route[:, k : k + 1] == EXPERTS + 1, 1.0, 0.0)
        for c in range(2):
            direct += const_mask[k][c] * cg[c][0]
        grad = jnp.sum(g * combined, axis=1, keepdims=True) + direct * g_normed
        for c in range(2):
            grad += const_mask[k][c] * cg[c][1] * g_const[c]
        gate_grads.append(grad)
        straight += gates[k] * direct
        total = total + gates[k] * combined
    total = total + straight * normed
    logit_grad = 0.0
    made = [jnp.zeros((1, D), F32)] * 2
    for c in range(2):
        share = const_mask[0][c] * gates[0] + const_mask[1][c] * gates[1]
        weight = share * cg[c][1]
        total = total + weight * consts[c]
        made[c] = jnp.sum(weight * g, axis=0, keepdims=True)
        first, second = share * g_normed, share * g_const[c]
        inner = cg[c][0] * first + cg[c][1] * second
        for i, v in enumerate((first, second)):
            logit_grad += jnp.where(lane == CHOICES + 2 * c + i, cg[c][i] * (v - inner), 0.0)
    out[...] = total.astype(BF)
    mean_grad = gates[0] * gate_grads[0] + gates[1] * gate_grads[1]
    router = 0.0
    for k in range(2):
        router += jnp.where(lane == route[:, k : k + 1], gates[k] * (gate_grads[k] - mean_grad), 0.0)
    router_out[...] = router[:, :CHOICES]
    logit_low = (router + logit_grad).astype(BF)
    small_w[...] += dot_tn(normed.astype(BF), logit_low)
    normed_grad = dot_nt(logit_low, w_small[...])
    normed_grad += dot((picks[0] + picks[1]).astype(BF), back[:, 1].reshape(SLOTS, D))
    normed_grad += straight * g
    scaled = normed_grad * gain_two
    gain_grad = jnp.sum(normed_grad * unit, axis=0, keepdims=True)
    residual_grad = g + inverse * (scaled - unit * row_mean(scaled * unit))
    rgrad[...] = residual_grad
    low = residual_grad.astype(BF)
    agrad[...] = dot_nt(low, w_out[...]).astype(BF)
    out_w[...] += dot_tn(att[...], low)
    rows_w[0:1, :] += made[0]
    rows_w[1:2, :] += made[1]
    rows_w[2:3, :] += gain_grad


def combine_part(part, back, kept, t, packed, vecs, prior):
    _, _, att, resid, _, aux = kept

    def tile(width, mine=True):
        base = 0 if mine else 2 * part
        return pl.BlockSpec((HALF, width), lambda i, base=base: (base + i, 0))

    sums = [
        jax.ShapeDtypeStruct((D, D), F32), jax.ShapeDtypeStruct((D, 128), F32), jax.ShapeDtypeStruct((8, D), F32)
    ]
    sum_specs = [fixed((D, D)), fixed((D, 128)), fixed((8, D))]
    body = functools.partial(combine_body, prior is not None)
    if prior is None:
        given = []

        def body(*refs):
            combine_body(False, *refs[:10], None, None, None, *refs[10:])

    else:
        given = list(prior)
    return pl.pallas_call(
        body,
        grid=(2,),
        in_specs=[
            fixed((EXPERTS, 2, CAP, D)), tile(D), tile(D, False), tile(128), tile(2, False), tile(2, False),
            tile(D), fixed((D, D), 0, 3), fixed((D, 128), 0, 24), fixed((8, D)),
        ] + (sum_specs if given else []),
        out_specs=[tile(D), tile(D), tile(CHOICES), tile(D)] + sum_specs,
        out_shape=[
            jax.ShapeDtypeStruct((SEQ, D), BF), jax.ShapeDtypeStruct((SEQ, D), F32),
            jax.ShapeDtypeStruct((SEQ, CHOICES), F32), jax.ShapeDtypeStruct((SEQ, D), BF),
        ] + sums,
        compiler_params=kernel_params(),
        cost_estimate=lasting(0),
    )(back, resid, t["cotangent"], aux, t["slots"], t["routes"], att, packed, packed, vecs, *given)


def attention_back_body(
    qkv, agrad, lse, seg_col, seg_row, cos, sin, w_qkv, tok, vecs, rgrad, grad_in, qkv_grad, act, gain_w, bias
):
    for b in range(2):
        rows = slice(b * HALF, (b + 1) * HALF)
        ki = lax.broadcasted_iota(jnp.int32, (HALF, SEQ), 0) + b * HALF
        qi = lax.broadcasted_iota(jnp.int32, (HALF, SEQ), 1)
        ok = (qi >= ki) & (seg_col[rows, :] == seg_row[...])
        bias[rows, :] = jnp.where(ok, 0.0, FLOOR_SCORE)
    masks = head_masks()
    scale = 1.0 / math.sqrt(HEAD_DIM)

    def one_pair(p, carry):
        at = [pl.ds(pl.multiple_of(i * D + p * 128, 128), 128) for i in range(3)]
        q, k, v = [qkv[:, a] for a in at]
        da = agrad[:, at[0]]
        kg, vg, qg = [None, None], [None, None], [None, None]

        def add(store, i, value):
            store[i] = value if store[i] is None else store[i] + value

        for h in range(2):
            qh, dh = q * masks[h], da * masks[h]
            probs, grads, keyed = [], [], []
            for b in range(2):
                keys, first = slice(b * HALF, (b + 1) * HALF), b * HALF
                kh = k[keys, :] * masks[h]
                st = dot_nt(kh, q[first:, :]) + bias[keys, first:]
                probs.append(jnp.exp(st - lse[pl.ds(2 * p + h, 1), first:]))
                grads.append(dot_nt(v[keys, :] * masks[h], da[first:, :]))
                keyed.append(kh)
            inner = [jnp.sum(probs[b] * grads[b], axis=0, keepdims=True) for b in range(2)]
            late = inner[0][:, HALF:] + inner[1]
            whole = jnp.concatenate([inner[0][:, :HALF], late], axis=1)
            for b, mean in enumerate((whole, late)):
                first = b * HALF
                ds = (probs[b] * (grads[b] - mean)).astype(BF)
                add(kg, b, dot(ds, qh[first:, :]))
                add(vg, b, dot(probs[b].astype(BF), dh[first:, :]))
                full = dot_tn(ds, keyed[b])
                if b == 0:
                    add(qg, 0, full[:HALF, :])
                    add(qg, 1, full[HALF:, :])
                else:
                    add(qg, 1, full)
        for b in range(2):
            rows = slice(b * HALF, (b + 1) * HALF)
            c, s = cos[rows, :], sin[rows, :]
            qb = qg[b] * scale
            qkv_grad[rows, at[0]] = (qb * c - swap_halves(qb) * s).astype(BF)
            qkv_grad[rows, at[1]] = (kg[b] * c - swap_halves(kg[b]) * s).astype(BF)
            qkv_grad[rows, at[2]] = vg[b].astype(BF)
        return carry

    lax.fori_loop(0, PAIRS, one_pair, 0)
    gain_one = vecs[0:1, :]
    gain_grad = 0.0
    for b in range(2):
        rows = slice(b * HALF, (b + 1) * HALF)
        x = tok[rows, :].astype(F32)
        inverse = lax.rsqrt(row_mean(x * x) + EPSILON)
        unit = x * inverse
        act[rows, :] = (unit * gain_one).astype(BF)
        grad = dot_nt(qkv_grad[rows, :], w_qkv[...])
        scaled = grad * gain_one
        gain_grad += jnp.sum(grad * unit, axis=0, keepdims=True)
        grad_in[rows, :] = rgrad[rows, :] + inverse * (scaled - unit * row_mean(scaled * unit))
    gain_w[...] = jnp.broadcast_to(gain_grad, gain_w.shape)


def attention_back(part, kept, rgrad, agrad, t, packed, vecs):
    _, qkv, _, _, lse, _ = kept
    return pl.pallas_call(
        attention_back_body,
        grid=(1,),
        in_specs=[
            fixed((SEQ, 3 * D)), fixed((SEQ, D)), fixed((16, SEQ)),
            seq_block(1, part), fixed((None, 1, SEQ), part, 0, 0), seq_block(128, part), seq_block(128, part),
            fixed((D, 3 * D), 0, 0), seq_block(D, part), fixed((8, D)), fixed((SEQ, D)),
        ],
        out_specs=[fixed((SEQ, D)), fixed((SEQ, 3 * D)), fixed((SEQ, D)), fixed((8, D))],
        out_shape=[
            jax.ShapeDtypeStruct((SEQ, D), F32), jax.ShapeDtypeStruct((SEQ, 3 * D), BF),
            jax.ShapeDtypeStruct((SEQ, D), BF), jax.ShapeDtypeStruct((8, D), F32),
        ],
        scratch_shapes=[pltpu.VMEM((SEQ, SEQ), F32)],
        compiler_params=kernel_params(),
        cost_estimate=lasting(0),
    )(
        qkv, agrad, lse, t["seg_col"], t["seg_row"], t["cos"], t["sin"], packed, t["tokens"], vecs, rgrad
    )


def mixer_wgrad_body(parts, groups, *refs):
    core, acts, grads, gains = refs[0], refs[1 : 1 + parts], refs[1 + parts : 1 + 2 * parts], refs[1 + 2 * parts : 1 + 3 * parts]
    out_w, small, rows, give, keep, turned, last = refs[1 + 3 * parts :]
    step, half = pl.program_id(0), D // 2
    chunk = half // groups

    def scattered(store, across, value):
        for group in range(groups):
            for c in range(2):
                kept = (core[0] == c).astype(jnp.int32)
                at = pl.ds(pl.multiple_of(kept * half + group * chunk, 16), chunk)
                first = (2 * group + c) * chunk
                store[at, across] = value[first : first + chunk, :]

    @pl.when(step == 0)
    def _():
        for i in range(parts):
            scattered(turned, slice(i * SEQ, (i + 1) * SEQ), acts[i][...].T)

    @pl.when(step < 9)
    def _():
        made = dot(turned[...], jnp.concatenate([v[...] for v in grads], axis=0)).astype(BF)
        give[...] = made[:half, :]
        keep[...] = made[half:, :]

    @pl.when((step >= 9) & (step < 12))
    def _():
        scattered(last, slice(0, 256), out_w[...].astype(BF))
        give[...] = last[:half, :]
        keep[...] = last[half:, :]

    @pl.when(step == 12)
    def _():
        gain_one = sum(v[0:1, :] for v in gains)
        line = lax.broadcasted_iota(jnp.int32, (128, D), 0)
        stacked = 0.0
        for i, row in enumerate((rows[0:1, :], rows[1:2, :], gain_one, rows[2:3, :])):
            stacked += jnp.where(line == 16 + i, row, 0.0)
        scattered(last, slice(0, 128), (small[...] + stacked.T).astype(BF))
        give[:, :128] = last[:half, :128]
        keep[:, :128] = last[half:, :128]
        give[:, 128:] = jnp.zeros((half, 128), BF)
        keep[:, 128:] = jnp.zeros((half, 128), BF)


def mixer_wgrad(acts, grads, gains, out_w, small, rows, groups, core):
    parts = len(acts)
    half = pl.BlockSpec((D // 2, 256), lambda i: (0, i))
    out = jax.ShapeDtypeStruct((D // 2, 4 * D + 256), BF)
    return pl.pallas_call(
        functools.partial(mixer_wgrad_body, parts, groups),
        grid=(13,),
        in_specs=[pl.BlockSpec(memory_space=pltpu.SMEM)]
        + [fixed((SEQ, D))] * parts
        + [pl.BlockSpec((SEQ, 256), lambda i: (0, jnp.minimum(i, 8)))] * parts
        + [fixed((8, D))] * parts
        + [pl.BlockSpec((D, 256), lambda i: (0, jnp.clip(i - 9, 0, 2))), fixed((D, 128)), fixed((8, D))],
        out_specs=[half, half],
        out_shape=[out, out],
        scratch_shapes=[pltpu.VMEM((D, parts * SEQ), BF), pltpu.VMEM((D, 256), BF)],
        compiler_params=kernel_params(),
        cost_estimate=lasting(0),
    )(jnp.stack([core]).astype(jnp.int32), *acts, *grads, *gains, out_w, small, rows)


def tables(tokens, cotangent, prev_logits, routes, capacity, segments, positions):
    parts = tokens.shape[0] // SEQ
    slots = jnp.concatenate(
        [pair_slots(routes[i * SEQ : (i + 1) * SEQ], capacity) for i in range(parts)]
    )
    lane = jnp.arange(128) % HEAD_DIM
    frequency = jnp.exp((lane % (HEAD_DIM // 2)).astype(F32) * (-2.0 * math.log(ROPE_BASE) / HEAD_DIM))
    angles = positions.astype(F32)[:, None] * frequency[None, :]
    sign = jnp.where(lane < HEAD_DIM // 2, -1.0, 1.0)
    return dict(
        tokens=tokens,
        cotangent=cotangent,
        prev=jnp.pad(prev_logits, ((0, 0), (0, 128 - CHOICES))),
        routes=routes,
        slots=slots,
        slot_row=slots.reshape(parts, SEQ, 2).transpose(0, 2, 1),
        seg_col=segments[:, None],
        seg_row=segments.reshape(parts, 1, SEQ),
        cos=jnp.cos(angles),
        sin=jnp.sin(angles) * sign,
    )


FC = 512


def expert_rows_body(x_ref, g_ref, wg_ref, wu_ref, wd_ref, hid_ref, dg_ref, du_ref, out_ref, acc, racc):
    step = pl.program_id(0)
    x = x_ref[:, 0].reshape(-1, D)
    g = g_ref[:, 0].reshape(-1, D)
    wg, wu, wd = wg_ref[...], wu_ref[...], wd_ref[...]
    gate = dot(x, wg)
    up = dot(x, wu)
    hgrad = dot_nt(g, wd).astype(BF).astype(F32)
    sig = 1.0 / (1.0 + jnp.exp(-gate))
    act = gate * sig
    hidden = (act * up).astype(BF)
    dgate = (hgrad * up * sig * (1.0 + gate * (1.0 - sig))).astype(BF)
    dup = (hgrad * act).astype(BF)
    hid_ref[...] = hidden
    dg_ref[...] = dgate
    du_ref[...] = dup
    prod = dot(hidden, wd)
    rgrad = dot_nt(dgate, wg) + dot_nt(dup, wu)

    @pl.when(step == 0)
    def _():
        acc[...] = prod
        racc[...] = rgrad

    @pl.when(step > 0)
    def _():
        acc[...] += prod
        racc[...] += rgrad

    @pl.when(step == pl.num_programs(0) - 1)
    def _():
        out_ref[:, 0] = acc[...].astype(BF).reshape(-1, CAP, D)
        out_ref[:, 1] = racc[...].astype(BF).reshape(-1, CAP, D)


def expert_rows(received, w_gate_up, w_down):
    n = received.shape[0]
    rows = n * CAP
    steps = FF // FC
    wide = jax.ShapeDtypeStruct((rows, FF), BF)
    block = pl.BlockSpec((rows, FC), lambda j: (0, j))
    return pl.pallas_call(
        expert_rows_body,
        grid=(steps,),
        in_specs=[
            pl.BlockSpec((n, 1, CAP, D), lambda j: (0, 0, 0, 0)),
            pl.BlockSpec((n, 1, CAP, D), lambda j: (0, 1, 0, 0)),
            pl.BlockSpec((D, FC), lambda j: (0, j)),
            pl.BlockSpec((D, FC), lambda j: (0, steps + j)),
            pl.BlockSpec((FC, D), lambda j: (j, 0)),
        ],
        out_specs=[block, block, block, pl.BlockSpec((n, 2, CAP, D), lambda j: (0, 0, 0, 0))],
        out_shape=[wide, wide, wide, jax.ShapeDtypeStruct((n, 2, CAP, D), BF)],
        scratch_shapes=[pltpu.VMEM((rows, D), F32), pltpu.VMEM((rows, D), F32)],
        compiler_params=pltpu.CompilerParams(
            dimension_semantics=("arbitrary",), vmem_limit_bytes=VMEM_MOST
        ),
        cost_estimate=lasting(28),
    )(received, received, w_gate_up, w_gate_up, w_down)


FW = 512


def down_wgrad_body(parts, *refs):
    hid, received, out = refs[:parts], refs[parts : 2 * parts], refs[2 * parts]
    rows = jnp.concatenate([v[:, 0].reshape(-1, D) for v in received], axis=0)
    out[...] = dot_tn(jnp.concatenate([v[...] for v in hid], axis=0), rows).astype(BF)


def down_wgrad(received, hid):
    parts, (n, _, _, _) = len(received), received[0].shape
    return pl.pallas_call(
        functools.partial(down_wgrad_body, parts),
        grid=(FF // FW,),
        in_specs=[pl.BlockSpec((n * CAP, FW), lambda j: (0, j))] * parts
        + [pl.BlockSpec((n, 1, CAP, D), lambda j: (0, 1, 0, 0))] * parts,
        out_specs=pl.BlockSpec((FW, D), lambda j: (j, 0)),
        out_shape=jax.ShapeDtypeStruct((FF, D), BF),
        compiler_params=kernel_params(),
        cost_estimate=lasting(10),
    )(*hid, *received)


def gate_up_wgrad_body(parts, *refs):
    received, dg, du = refs[:parts], refs[parts : 2 * parts], refs[2 * parts : 3 * parts]
    out, xt = refs[3 * parts :]
    rows = received[0].shape[0] * CAP

    @pl.when(pl.program_id(0) == 0)
    def _():
        for i in range(parts):
            xt[:, i * rows : (i + 1) * rows] = received[i][:, 0].reshape(rows, D).T

    for k, grads in enumerate((dg, du)):
        out[k] = dot(xt[...], jnp.concatenate([v[...] for v in grads], axis=0)).astype(BF)


def gate_up_wgrad(received, dg, du):
    parts, (n, _, _, _) = len(received), received[0].shape
    return pl.pallas_call(
        functools.partial(gate_up_wgrad_body, parts),
        grid=(FF // FW,),
        in_specs=[pl.BlockSpec((n, 1, CAP, D), lambda j: (0, 0, 0, 0))] * parts
        + [pl.BlockSpec((n * CAP, FW), lambda j: (0, j))] * (2 * parts),
        out_specs=pl.BlockSpec((2, D, FW), lambda j: (0, 0, j)),
        out_shape=jax.ShapeDtypeStruct((2, D, FF), BF),
        scratch_shapes=[pltpu.VMEM((D, parts * n * CAP), BF)],
        compiler_params=kernel_params(),
        cost_estimate=lasting(0),
    )(*received, *dg, *du)


def place_body(spots, count, *refs):
    offsets, blocks, outs, sems = refs[0], refs[1 : 1 + count], refs[1 + count : -1], refs[-1]
    copies = []
    for i, (block, row, rows, column, columns, out) in enumerate(spots):
        down = pl.ds(pl.multiple_of(offsets[2 * i], 16), rows)
        across = pl.ds(pl.multiple_of(offsets[2 * i + 1], 128), columns)
        copies.append(
            pltpu.make_async_copy(
                blocks[block].at[pl.ds(row, rows), pl.ds(column, columns)],
                outs[out].at[down, across],
                sems.at[i],
            )
        )
    for copy in copies:
        copy.start()
    for copy in copies:
        copy.wait()


def place(blocks, spots, offsets, shapes):
    anywhere = pl.BlockSpec(memory_space=pl.ANY)
    return pl.pallas_call(
        functools.partial(place_body, spots, len(blocks)),
        in_specs=[pl.BlockSpec(memory_space=pltpu.SMEM)] + [anywhere] * len(blocks),
        out_specs=[pl.BlockSpec(memory_space=pltpu.VMEM)] * len(shapes),
        out_shape=[jax.ShapeDtypeStruct(v, BF) for v in shapes],
        scratch_shapes=[pltpu.SemaphoreType.DMA((len(spots),))],
        compiler_params=pltpu.CompilerParams(vmem_limit_bytes=VMEM_MOST),
        cost_estimate=lasting(0),
    )(jnp.stack(offsets).astype(jnp.int32), *blocks)


def pick(value, index, axis=0):
    return lax.dynamic_index_in_dim(value, index, axis, False)


def added(*values):
    return sum(v.astype(F32) for v in values).astype(BF)


class Paired:
    axes = ("half", "low", "inner", "side", "core")
    fsdp = ("half", "low", "inner")
    expert = ("side", "core")
    rows = ("side", "low", "inner")
    route_axes = ("half", "low", "inner", "core")
    near = 896
    cut = 3072

    def __init__(self, mesh):
        self.mesh = Mesh(mesh.devices.reshape(2, 2, 2, 2, 2), self.axes)
        self.routes = []
        for turn in range(4):
            pairs = []
            for z in range(4):
                for y in range(2):
                    for c in range(2):
                        half, inner = (z ^ turn) >> 1, (z ^ turn) & 1
                        pairs.append(((z * 2 + y) * 2 + c, ((half * 2 + c) * 2 + inner) * 2 + y))
            self.routes.append(pairs)

    @staticmethod
    def swap(value, axis="core"):
        return lax.ppermute(value, axis, [(0, 1), (1, 0)])

    @staticmethod
    def along(value, turn):
        return lax.ppermute(value, ("half", "low"), [(i, i ^ turn) for i in range(4)])

    @staticmethod
    def spot():
        z = lax.axis_index("half") * 2 + lax.axis_index("low")
        return z, lax.axis_index("inner"), lax.axis_index("side"), lax.axis_index("core")

    @staticmethod
    def joined(gate_up, down):
        high, edge = gate_up.shape[1], D - 256
        tail = down[:, 2 * high :]
        half = tail.shape[1] // 2
        under = jnp.concatenate([tail[:, :half, edge:], tail[:, half:, edge:]], axis=2)
        last = jnp.concatenate([tail[:, :, :edge], under], axis=1)
        cut = Paired.cut
        rest = jnp.concatenate([gate_up[:, :, cut:], down[:, :high], down[:, high : 2 * high], last], axis=2)
        return gate_up[:, :, :cut], rest

    @staticmethod
    def rects(high, deep):
        half, edge, at = deep // 2 - high, D - 256, 2 * FF - Paired.cut
        yield 0, high, at, D, 0, 0
        yield 0, high, at + D, D, high, 0
        yield 0, 2 * half, at + 2 * D, edge, 2 * high, 0
        yield 2 * half, half, at + 2 * D, 256, 2 * high, edge
        yield 2 * half, half, at + 2 * D + 256, 256, 2 * high + half, edge

    def send(self, joined, turn, part):
        mine = pick(joined[part], (self.spot()[0] ^ turn) & 1)
        return lax.ppermute(mine, self.route_axes, self.routes[turn])

    def gather_shared(self, shard, weights, early):
        z, y, x, c = self.spot()
        rows, width = shard.shape
        rows, width = rows // 2, width // 2
        mine = lax.dynamic_slice(shard, (c * rows, x * width), (rows, width))
        stack = jnp.concatenate([mine] + [self.along(mine, turn) for turn in (1, 2, 3)])
        stack, joined, early = lax.optimization_barrier((stack, self.joined(*weights), early))
        sent = {(2, 0): (self.send(joined, 2, 0), None)}
        over_y, over_x = self.swap(stack, "inner"), self.swap(stack, "side")
        far = self.swap(over_y[:, : self.near], "side"), self.swap(over_x[:, self.near :], "inner")
        blocks = [stack, over_y, over_x, *far]
        flips = [(0, 0, 0), (1, 0, 0), (0, 1, 0), (1, 1, 0), (1, 1, self.near)]
        spots, offsets = [], []
        for i, (dy, dx, column) in enumerate(flips + flips):
            core = c if i < len(flips) else 1 - c
            for turn in range(4):
                spots.append((i, turn * rows, rows, 0, blocks[i % len(flips)].shape[1], 0))
                offsets += [((z ^ turn) * 2 + (y ^ dy)) * 2 * rows + core * rows, (x ^ dx) * width + column]
        blocks += [self.swap(v) for v in blocks]
        blocks, joined, sent = lax.optimization_barrier((blocks, joined, sent))
        [full] = place(blocks, spots, offsets, [(16 * rows, 2 * width)])
        return full, early, (joined, sent)

    def gather_more(self, held, value, names):
        joined, sent = held
        more = {v: (self.send(joined, *v), None) for v in names}
        waiting = [v for v, (_, other) in sent.items() if other is None][:2]
        done = {**sent, **{v: (sent[v][0], self.swap(sent[v][0])) for v in waiting}}
        value, joined, sent = lax.optimization_barrier((value, joined, {**done, **more}))
        return (joined, sent), value

    def split(self):
        return 8, lax.axis_index("core")

    def reduce_first(self, give, keep):
        z, y, x, c = self.spot()
        width = give.shape[-1] // 2
        near = (width // 128 + 1) // 2 * 128
        parts = added(keep, self.swap(give)).reshape(4, 2, -1, 2 * width)

        def columns(value, first, count):
            return lax.dynamic_slice_in_dim(value, first, count, value.ndim - 1)

        one = added(columns(parts, x * width, near), self.swap(columns(parts, (1 - x) * width, near), "side"))
        two = jnp.concatenate([parts[..., near:width], parts[..., width + near :]], axis=3)
        two = added(pick(two, y, 1), self.swap(pick(two, 1 - y, 1), "inner"))
        return one, two

    def reduce_last(self, one, two):
        z, y, x, c = self.spot()
        rest = two.shape[2] // 2
        one = added(pick(one, y, 1), self.swap(pick(one, 1 - y, 1), "inner"))
        near = lax.dynamic_slice_in_dim(two, x * rest, rest, 2)
        two = added(near, self.swap(lax.dynamic_slice_in_dim(two, (1 - x) * rest, rest, 2), "side"))
        both = jnp.concatenate([one, two], axis=2)
        mine = added(pick(both, z), *[self.along(pick(both, z ^ turn), turn) for turn in (1, 2, 3)])
        other = self.swap(mine, "side")
        line = jnp.where(x == 0, jnp.concatenate([mine, other], 1), jnp.concatenate([other, mine], 1))
        other = self.swap(line)
        both = jnp.where(c == 0, jnp.concatenate([line, other]), jnp.concatenate([other, line]))
        return both.astype(F32)

    def gather_expert(self, held, shapes):
        sent = held[1]
        c = lax.axis_index("core")
        here = lax.axis_index("half") * 2 + lax.axis_index("inner")
        both = [sent[turn, part] for turn in range(4) for part in range(2)]
        blocks = [v for v, _ in both] + [self.swap(v) if other is None else other for v, other in both]
        high, deep = shapes[0][1], shapes[1][1]
        spots, offsets, zero = [], [], jnp.int32(0)
        for i in range(0, 16, 2):
            shard = (here ^ (i // 2 % 4)) * 2 + (c if i < 8 else 1 - c)
            spots += [(i, 0, high, 0, self.cut, 0), (i + 1, 0, high, 0, 2 * FF - self.cut, 0)]
            offsets += [shard * high, zero, shard * high, zero + self.cut]
            for row, rows, column, columns, to_row, to_column in self.rects(high, deep):
                spots.append((i + 1, row, rows, column, columns, 1))
                offsets += [shard * deep + to_row, zero + to_column]
        return place(blocks, spots, offsets, [(8 * high, 2 * FF), (8 * deep, D)])

    def scatter_start(self, grad, axis):
        c = lax.axis_index("core")
        shape = grad.shape
        grad = grad.reshape(shape[:axis] + (4, 2, shape[axis] // 8) + shape[axis + 1 :])
        return added(pick(grad, c, axis + 1), self.swap(pick(grad, 1 - c, axis + 1)))

    def scatter_send(self, parts, axis):
        here = lax.axis_index("half") * 2 + lax.axis_index("inner")
        got = {}
        for turn in (2, 3, 0, 1):
            back = [(b, a) for a, b in self.routes[turn]]
            got[turn] = lax.ppermute(pick(parts, here ^ turn, axis), self.route_axes, back)
        return got

    def scatter_end(self, got, axis):
        even = (self.spot()[0] & 1) == 0
        first, second = [got[i].astype(F32) + got[i + 2].astype(F32) for i in range(2)]
        return jnp.stack([jnp.where(even, first, second), jnp.where(even, second, first)])


class Plain:
    axes = ("outer", "inner", "expert")
    fsdp = ("outer", "inner")
    expert = ("expert",)
    rows = ("expert", "inner")

    def __init__(self, mesh):
        fsdp, expert = mesh.shape["fsdp"], mesh.shape["expert"]
        inner = EXPERTS // expert
        self.mesh = Mesh(mesh.devices.reshape(fsdp // inner, inner, expert), self.axes)

    def gather_shared(self, shard, weights, early):
        return lax.all_gather(shard, self.fsdp, axis=0, tiled=True), early, weights

    def gather_more(self, held, value, names):
        return held, value

    def split(self):
        return 1, jnp.int32(1)

    def reduce_first(self, give, keep):
        return jnp.concatenate([give, keep]), None

    def reduce_last(self, total, _):
        total = lax.psum_scatter(total, self.axes, scatter_dimension=0, tiled=True)
        return lax.all_gather(total, self.expert, axis=0, tiled=True).astype(F32)

    def gather_expert(self, weights, shapes):
        full = []
        for weight in weights:
            own = lax.all_to_all(weight, "inner", 0, 0, tiled=True)
            own = lax.all_gather(own, "outer", axis=0, tiled=True)
            full.append(own.reshape((-1,) + weight.shape[2:]))
        return full

    def scatter_start(self, grad, axis):
        return grad

    def scatter_send(self, grad, axis):
        return grad

    def scatter_end(self, grad, axis):
        inner = lax.axis_size("inner")
        part = lax.psum_scatter(grad, "outer", scatter_dimension=axis, tiled=True)
        shape = part.shape
        part = part.reshape(shape[:axis] + (inner, shape[axis] // inner) + shape[axis + 1 :])
        part = jnp.moveaxis(part, axis, 0)
        return lax.all_to_all(part, "inner", 0, 0, tiled=True).astype(F32)


def solution(mesh):
    plan = Paired(mesh) if (mesh.shape["fsdp"], mesh.shape["expert"]) == (8, 4) else Plain(mesh)

    def on_device(
        tokens, cotangent, prev_logits, routes, capacity, segments, positions,
        w_qkv, w_out, gate_matrix, const_values, attn_gain, moe_gain, w_gate_up, w_down,
    ):
        rows = w_qkv.shape[0]
        pad = jnp.zeros((rows, 256 - 20), BF)
        small = jnp.concatenate(
            [gate_matrix, const_values, attn_gain[:, None], moe_gain[:, None], pad], axis=1
        )
        shard = jnp.concatenate([w_qkv, w_out, small], axis=1)
        t = tables(tokens, cotangent, prev_logits, routes, capacity, segments, positions)
        packed, t, held = plan.gather_shared(shard, (w_gate_up, w_down), t)
        columns = packed[:, 4 * D + 16 : 4 * D + 20].astype(F32).T
        vecs = jnp.concatenate([columns[2:], columns[:2], jnp.zeros((4, D), F32)])
        parts = tokens.shape[0] // SEQ
        kept, sends, shared = [], [], packed
        for i in range(parts):
            if i == 1:
                held, (shared, kept[0][5]) = plan.gather_more(held, (packed, kept[0][5]), ((2, 1), (0, 0), (0, 1), (1, 0)))
            kept.append(list(forward_part(i, t, shared, vecs)))
            sends.append(kept[i][0])
        held, sends[-1] = plan.gather_more(held, sends[-1], ((3, 0), (3, 1), (1, 1)))
        gate_up_full, down_full = plan.gather_expert(held, (w_gate_up.shape, w_down.shape))
        received = [lax.all_to_all(v, plan.rows, 0, 0, tiled=True) for v in sends]
        made = [expert_rows(r, gate_up_full, down_full) for r in received]
        hid, dg, du = [[m[i] for m in made] for i in range(3)]
        backs = [m[3] for m in made]
        gate_up_w = gate_up_wgrad(received, dg, du)
        backs[-1], hid, gate_up_w = lax.optimization_barrier((backs[-1], hid, gate_up_w))
        returned = [lax.all_to_all(v, plan.rows, 0, 0, tiled=True) for v in backs]
        gate_up_sums = plan.scatter_start(gate_up_w, 1)
        down_w = down_wgrad(received, hid)
        returned[0], gate_up_sums, down_w = lax.optimization_barrier((returned[0], gate_up_sums, down_w))
        gate_up_got = plan.scatter_send(gate_up_sums, 1)
        down_sums = plan.scatter_start(down_w, 0)
        firsts, lasts, sums = [], [], None
        for i in range(parts):
            *first, out_w, small_w, rows_w = combine_part(i, returned[i], kept[i], t, packed, vecs, sums)
            sums = (out_w, small_w, rows_w)
            firsts.append(first)
            if i == parts - 1:
                held = (down_sums, first[1], [v[3] for v in lasts])
                down_sums, first[1], _ = lax.optimization_barrier(held)
            lasts.append(attention_back(i, kept[i], first[1], first[3], t, packed, vecs))
            if i == 0:
                returned[-1], sums, _ = lax.optimization_barrier((returned[-1], sums, lasts[0][3]))
        held = ([v[2] for v in lasts], gate_up_got, down_sums)
        acts, gate_up_got, down_sums = lax.optimization_barrier(held)
        halves = mixer_wgrad(
            acts, [v[1] for v in lasts], [v[3] for v in lasts], *sums, *plan.split()
        )
        down_got = plan.scatter_send(down_sums, 0)
        near = plan.reduce_first(*halves)
        total = plan.reduce_last(*near)
        down_total = plan.scatter_end(down_got, 0)
        gate_up_total = plan.scatter_end(gate_up_got, 1)
        gate_up_total = jnp.concatenate([gate_up_total[:, 0], gate_up_total[:, 1]], axis=2)
        return (
            jnp.concatenate([v[0] for v in firsts]),
            jnp.concatenate([v[0] for v in lasts]),
            jnp.concatenate([v[2] for v in firsts]),
            total[:, : 3 * D],
            total[:, 3 * D : 4 * D],
            total[:, 4 * D : 4 * D + 16],
            total[:, 4 * D + 16 : 4 * D + 18],
            total[:, 4 * D + 18],
            total[:, 4 * D + 19],
            gate_up_total,
            down_total,
        )

    every = plan.fsdp + plan.expert
    split = P(every, None)
    shard = P(plan.fsdp, None)
    line = P(plan.fsdp)
    whole = P(plan.expert, plan.fsdp, None)
    return jax.shard_map(
        on_device,
        mesh=plan.mesh,
        in_specs=(
            split, split, split, split, P(), P(every), P(every),
            shard, shard, shard, shard, line, line, whole, whole,
        ),
        out_specs=(split, split, split, shard, shard, shard, shard, line, line, whole, whole),
        check_vma=False,
    )
```

```python
import functools
import math

import jax
import jax.numpy as jnp
from jax import lax
from jax.experimental import pallas as pl
from jax.experimental.pallas import tpu as pltpu
from jax.sharding import Mesh
from jax.sharding import PartitionSpec as P

D = 768
HEADS = 12
HEAD_DIM = 64
FF = 2048
EXPERTS = 8
SEQ = 512
CAP = 128
CHOICES = EXPERTS + 4
SLOTS = EXPERTS * CAP

EPSILON = 1e-05
ROPE_BASE = 10000.0
FLOOR_SCORE = -1e30
HIGHEST = lax.Precision.HIGHEST
BF = jnp.bfloat16
F32 = jnp.float32
VMEM_MOST = 56 * 2**20


def dot(a, b):
    return jnp.dot(a, b, preferred_element_type=F32)


def dot_nt(a, b):
    return lax.dot_general(a, b, (((1,), (1,)), ((), ())), preferred_element_type=F32)


def dot_tn(a, b):
    return lax.dot_general(a, b, (((0,), (0,)), ((), ())), preferred_element_type=F32)


def pair_slots(route, capacity):
    route_hot = (route[:, :, None] == jnp.arange(CHOICES, dtype=jnp.int32)).astype(F32)
    seq_index = jnp.arange(SEQ)
    before = (seq_index[:, None] > seq_index[None, :]).astype(BF)
    earlier = dot(before, jnp.sum(route_hot, axis=1).astype(BF))
    slot_rank = jnp.sum(earlier[:, None, :] * route_hot, axis=-1)
    cap_limit = jnp.sum(route_hot[:, :, :EXPERTS] * capacity.astype(F32), axis=-1)
    kept_pairs = (route < EXPERTS) & (slot_rank < cap_limit)
    return jnp.where(kept_pairs, route * CAP + slot_rank.astype(jnp.int32), -1)


HALF = SEQ // 2
PAIRS = HEADS // 2


def lanes(rows):
    return lax.broadcasted_iota(jnp.int32, (rows, 128), 1)


def swap_halves(v):
    low = lanes(v.shape[0]) % HEAD_DIM < HEAD_DIM // 2
    return jnp.where(low, pltpu.roll(v, 128 - HEAD_DIM // 2, 1), pltpu.roll(v, HEAD_DIM // 2, 1))


def row_mean(v):
    return jnp.sum(v, axis=1, keepdims=True) * (1.0 / D)


def head_masks():
    low = lax.broadcasted_iota(jnp.int32, (1, 128), 1) < HEAD_DIM
    return (jnp.where(low, 1.0, 0.0).astype(BF), jnp.where(low, 0.0, 1.0).astype(BF))


def forward_body(
    tok, cot, prev, route, slot_row, seg_col, seg_row, cos, sin, w_qkv, w_out, w_small, vecs,
    sent, qkv, att, resid, lse_out, aux, act, bias, tg0, tg1, lse,
):
    gain_one, gain_two = vecs[0:1, :], vecs[1:2, :]
    for r in range(2):
        rows = slice(r * HALF, (r + 1) * HALF)
        x = tok[rows, :].astype(F32)
        act[rows, :] = (x * lax.rsqrt(row_mean(x * x) + EPSILON) * gain_one).astype(BF)
        qi = lax.broadcasted_iota(jnp.int32, (HALF, SEQ), 0) + r * HALF
        ki = lax.broadcasted_iota(jnp.int32, (HALF, SEQ), 1)
        ok = (qi >= ki) & (seg_col[rows, :] == seg_row[...])
        bias[rows, :] = jnp.where(ok, 0.0, FLOOR_SCORE)
    for block in range(9):
        part = dot(act[...], w_qkv[:, block * 256 : block * 256 + 256])
        for i in range(2):
            v = part[:, i * 128 : i * 128 + 128]
            if block < 6:
                v = v * cos[...] + swap_halves(v) * sin[...]
            if block < 3:
                v = v * (1.0 / math.sqrt(HEAD_DIM))
            at = block * 256 + i * 128
            qkv[:, at : at + 128] = v.astype(BF)
    masks = head_masks()

    def pair(p, carry):
        q = qkv[:, pl.ds(pl.multiple_of(p * 128, 128), 128)]
        k = qkv[:, pl.ds(pl.multiple_of(D + p * 128, 128), 128)]
        v = qkv[:, pl.ds(pl.multiple_of(2 * D + p * 128, 128), 128)]
        for b in range(2):
            rows, reach = slice(b * HALF, (b + 1) * HALF), (b + 1) * HALF
            out = None
            for h in range(2):
                s = dot_nt(q[rows, :] * masks[h], k[:reach, :]) + bias[rows, :reach]
                top = jnp.max(s, axis=1, keepdims=True)
                e = jnp.exp(s - top)
                total = jnp.sum(e, axis=1, keepdims=True)
                o = dot((e * (1.0 / total)).astype(BF), v[:reach, :] * masks[h])
                out = o if out is None else out + o
                lse[rows, :] = jnp.where(lanes(HALF) == 2 * p + h, top + jnp.log(total), lse[rows, :])
            att[rows, pl.ds(pl.multiple_of(p * 128, 128), 128)] = out.astype(BF)
        return carry

    lax.fori_loop(0, PAIRS, pair, 0)
    lse_out[...] = lse[...].T[:16, :]
    lane = lanes(HALF)

    def column(v, at):
        return jnp.sum(jnp.where(lane == at, v, 0.0), axis=1, keepdims=True)

    for r in range(2):
        rows = slice(r * HALF, (r + 1) * HALF)
        res = tok[rows, :].astype(F32) + dot(att[rows, :], w_out[...])
        resid[rows, :] = res
        act2 = (res * lax.rsqrt(row_mean(res * res) + EPSILON) * gain_two).astype(BF)
        act[rows, :] = act2
        logits = dot(act2, w_small[...])
        router = logits + prev[rows, :].astype(F32)
        r0, r1 = column(router, route[rows, 0:1]), column(router, route[rows, 1:2])
        top = jnp.maximum(r0, r1)
        e0, e1 = jnp.exp(r0 - top), jnp.exp(r1 - top)
        g0, g1 = e0 / (e0 + e1), e1 / (e0 + e1)
        made = jnp.where(lane == 0, g0, jnp.where(lane == 1, g1, 0.0))
        for c in range(2):
            a, b = column(logits, CHOICES + 2 * c), column(logits, CHOICES + 2 * c + 1)
            top = jnp.maximum(a, b)
            ea, eb = jnp.exp(a - top), jnp.exp(b - top)
            made = jnp.where(lane == 2 + 2 * c, ea / (ea + eb), made)
            made = jnp.where(lane == 3 + 2 * c, eb / (ea + eb), made)
        aux[rows, :] = made
        g = cot[rows, :].astype(F32)
        tg0[rows, :] = (g0 * g).astype(BF)
        tg1[rows, :] = (g1 * g).astype(BF)

    def dispatch(b, carry):
        ids = lax.broadcasted_iota(jnp.int32, (256, SEQ), 0) + b * 256
        p0 = jnp.where(slot_row[0:1, :] == ids, 1.0, 0.0)
        p1 = jnp.where(slot_row[1:2, :] == ids, 1.0, 0.0)
        sent[pl.ds(b * 2, 2), 0] = dot((p0 + p1).astype(BF), act[...]).astype(BF).reshape(2, CAP, D)
        sg = dot(p0.astype(BF), tg0[...]) + dot(p1.astype(BF), tg1[...])
        sent[pl.ds(b * 2, 2), 1] = sg.astype(BF).reshape(2, CAP, D)
        return carry

    lax.fori_loop(0, SLOTS // 256, dispatch, 0)


def seq_block(width, part, col=0):
    return pl.BlockSpec((SEQ, width), lambda i, part=part, col=col: (part, col))


def fixed(shape, *at):
    at = at or (0,) * len(shape)
    return pl.BlockSpec(shape, lambda i, at=at: at)


def lasting(microseconds):
    return pl.CostEstimate(flops=microseconds * 10**9 + 1, bytes_accessed=0, transcendentals=0)


def kernel_params():
    return pltpu.CompilerParams(dimension_semantics=("arbitrary",), vmem_limit_bytes=VMEM_MOST)


def forward_part(part, t, packed, vecs):
    return pl.pallas_call(
        forward_body,
        grid=(1,),
        in_specs=[
            seq_block(D, part), seq_block(D, part), seq_block(128, part), seq_block(2, part),
            fixed((None, 2, SEQ), part, 0, 0), seq_block(1, part), fixed((None, 1, SEQ), part, 0, 0),
            seq_block(128, part), seq_block(128, part),
            fixed((D, 3 * D), 0, 0), fixed((D, D), 0, 3), fixed((D, 128), 0, 24), fixed((8, D)),
        ],
        out_specs=[
            fixed((EXPERTS, 2, CAP, D)), fixed((SEQ, 3 * D)), fixed((SEQ, D)), fixed((SEQ, D)),
            fixed((16, SEQ)), fixed((SEQ, 128)),
        ],
        out_shape=[
            jax.ShapeDtypeStruct((EXPERTS, 2, CAP, D), BF),
            jax.ShapeDtypeStruct((SEQ, 3 * D), BF),
            jax.ShapeDtypeStruct((SEQ, D), BF),
            jax.ShapeDtypeStruct((SEQ, D), F32),
            jax.ShapeDtypeStruct((16, SEQ), F32),
            jax.ShapeDtypeStruct((SEQ, 128), F32),
        ],
        scratch_shapes=[
            pltpu.VMEM((SEQ, D), BF), pltpu.VMEM((SEQ, SEQ), F32), pltpu.VMEM((SEQ, D), BF),
            pltpu.VMEM((SEQ, D), BF), pltpu.VMEM((SEQ, 128), F32),
        ],
        compiler_params=kernel_params(),
        cost_estimate=lasting(100),
    )(
        t["tokens"], t["cotangent"], t["prev"], t["routes"], t["slot_row"], t["seg_col"], t["seg_row"],
        t["cos"], t["sin"], packed, packed, packed, vecs,
    )


def combine_body(
    prior, back, resid, cot, aux, slot, route, att, w_out, w_small, vecs, p_out, p_small, p_rows,
    out, rgrad, router_out, agrad, out_w, small_w, rows_w,
):
    @pl.when(pl.program_id(0) == 0)
    def _():
        if prior:
            out_w[...], small_w[...], rows_w[...] = p_out[...], p_small[...], p_rows[...]
        else:
            out_w[...] = jnp.zeros_like(out_w)
            small_w[...] = jnp.zeros_like(small_w)
            rows_w[...] = jnp.zeros_like(rows_w)

    gain_two = vecs[1:2, :]
    consts = (vecs[2:3, :], vecs[3:4, :])
    res = resid[...]
    g = cot[...].astype(F32)
    inverse = lax.rsqrt(row_mean(res * res) + EPSILON)
    unit = res * inverse
    normed = unit * gain_two
    lane = lanes(HALF)
    gates = (aux[:, 0:1], aux[:, 1:2])
    cg = ((aux[:, 2:3], aux[:, 3:4]), (aux[:, 4:5], aux[:, 5:6]))
    ids = lax.broadcasted_iota(jnp.int32, (HALF, SLOTS), 1)
    picks = [jnp.where(slot[:, k : k + 1] == ids, 1.0, 0.0) for k in range(2)]
    rows = back[:, 0].reshape(SLOTS, D)
    g_normed = jnp.sum(g * normed, axis=1, keepdims=True)
    g_const = [jnp.sum(g * v, axis=1, keepdims=True) for v in consts]
    gate_grads, straight, total = [], 0.0, res
    const_mask = [
        [jnp.where(route[:, k : k + 1] == EXPERTS + 2 + c, 1.0, 0.0) for c in range(2)] for k in range(2)
    ]
    for k in range(2):
        combined = dot(picks[k].astype(BF), rows)
        direct = jnp.where(route[:, k : k + 1] == EXPERTS + 1, 1.0, 0.0)
        for c in range(2):
            direct += const_mask[k][c] * cg[c][0]
        grad = jnp.sum(g * combined, axis=1, keepdims=True) + direct * g_normed
        for c in range(2):
            grad += const_mask[k][c] * cg[c][1] * g_const[c]
        gate_grads.append(grad)
        straight += gates[k] * direct
        total = total + gates[k] * combined
    total = total + straight * normed
    logit_grad = 0.0
    made = [jnp.zeros((1, D), F32)] * 2
    for c in range(2):
        share = const_mask[0][c] * gates[0] + const_mask[1][c] * gates[1]
        weight = share * cg[c][1]
        total = total + weight * consts[c]
        made[c] = jnp.sum(weight * g, axis=0, keepdims=True)
        first, second = share * g_normed, share * g_const[c]
        inner = cg[c][0] * first + cg[c][1] * second
        for i, v in enumerate((first, second)):
            logit_grad += jnp.where(lane == CHOICES + 2 * c + i, cg[c][i] * (v - inner), 0.0)
    out[...] = total.astype(BF)
    mean_grad = gates[0] * gate_grads[0] + gates[1] * gate_grads[1]
    router = 0.0
    for k in range(2):
        router += jnp.where(lane == route[:, k : k + 1], gates[k] * (gate_grads[k] - mean_grad), 0.0)
    router_out[...] = router[:, :CHOICES]
    logit_low = (router + logit_grad).astype(BF)
    small_w[...] += dot_tn(normed.astype(BF), logit_low)
    normed_grad = dot_nt(logit_low, w_small[...])
    normed_grad += dot((picks[0] + picks[1]).astype(BF), back[:, 1].reshape(SLOTS, D))
    normed_grad += straight * g
    scaled = normed_grad * gain_two
    gain_grad = jnp.sum(normed_grad * unit, axis=0, keepdims=True)
    residual_grad = g + inverse * (scaled - unit * row_mean(scaled * unit))
    rgrad[...] = residual_grad
    low = residual_grad.astype(BF)
    agrad[...] = dot_nt(low, w_out[...]).astype(BF)
    out_w[...] += dot_tn(att[...], low)
    rows_w[0:1, :] += made[0]
    rows_w[1:2, :] += made[1]
    rows_w[2:3, :] += gain_grad


def combine_part(part, back, kept, t, packed, vecs, prior):
    _, _, att, resid, _, aux = kept

    def tile(width, mine=True):
        base = 0 if mine else 2 * part
        return pl.BlockSpec((HALF, width), lambda i, base=base: (base + i, 0))

    sums = [
        jax.ShapeDtypeStruct((D, D), F32), jax.ShapeDtypeStruct((D, 128), F32), jax.ShapeDtypeStruct((8, D), F32)
    ]
    sum_specs = [fixed((D, D)), fixed((D, 128)), fixed((8, D))]
    body = functools.partial(combine_body, prior is not None)
    if prior is None:
        given = []

        def body(*refs):
            combine_body(False, *refs[:10], None, None, None, *refs[10:])

    else:
        given = list(prior)
    return pl.pallas_call(
        body,
        grid=(2,),
        in_specs=[
            fixed((EXPERTS, 2, CAP, D)), tile(D), tile(D, False), tile(128), tile(2, False), tile(2, False),
            tile(D), fixed((D, D), 0, 3), fixed((D, 128), 0, 24), fixed((8, D)),
        ] + (sum_specs if given else []),
        out_specs=[tile(D), tile(D), tile(CHOICES), tile(D)] + sum_specs,
        out_shape=[
            jax.ShapeDtypeStruct((SEQ, D), BF), jax.ShapeDtypeStruct((SEQ, D), F32),
            jax.ShapeDtypeStruct((SEQ, CHOICES), F32), jax.ShapeDtypeStruct((SEQ, D), BF),
        ] + sums,
        compiler_params=kernel_params(),
        cost_estimate=lasting(0),
    )(back, resid, t["cotangent"], aux, t["slots"], t["routes"], att, packed, packed, vecs, *given)


def attention_back_body(
    qkv, agrad, lse, seg_col, seg_row, cos, sin, w_qkv, tok, vecs, rgrad, grad_in, qkv_grad, act, gain_w, bias
):
    for b in range(2):
        rows = slice(b * HALF, (b + 1) * HALF)
        ki = lax.broadcasted_iota(jnp.int32, (HALF, SEQ), 0) + b * HALF
        qi = lax.broadcasted_iota(jnp.int32, (HALF, SEQ), 1)
        ok = (qi >= ki) & (seg_col[rows, :] == seg_row[...])
        bias[rows, :] = jnp.where(ok, 0.0, FLOOR_SCORE)
    masks = head_masks()
    scale = 1.0 / math.sqrt(HEAD_DIM)

    def one_pair(p, carry):
        at = [pl.ds(pl.multiple_of(i * D + p * 128, 128), 128) for i in range(3)]
        q, k, v = [qkv[:, a] for a in at]
        da = agrad[:, at[0]]
        kg, vg, qg = [None, None], [None, None], [None, None]

        def add(store, i, value):
            store[i] = value if store[i] is None else store[i] + value

        for h in range(2):
            qh, dh = q * masks[h], da * masks[h]
            probs, grads, keyed = [], [], []
            for b in range(2):
                keys, first = slice(b * HALF, (b + 1) * HALF), b * HALF
                kh = k[keys, :] * masks[h]
                st = dot_nt(kh, q[first:, :]) + bias[keys, first:]
                probs.append(jnp.exp(st - lse[pl.ds(2 * p + h, 1), first:]))
                grads.append(dot_nt(v[keys, :] * masks[h], da[first:, :]))
                keyed.append(kh)
            inner = [jnp.sum(probs[b] * grads[b], axis=0, keepdims=True) for b in range(2)]
            late = inner[0][:, HALF:] + inner[1]
            whole = jnp.concatenate([inner[0][:, :HALF], late], axis=1)
            for b, mean in enumerate((whole, late)):
                first = b * HALF
                ds = (probs[b] * (grads[b] - mean)).astype(BF)
                add(kg, b, dot(ds, qh[first:, :]))
                add(vg, b, dot(probs[b].astype(BF), dh[first:, :]))
                full = dot_tn(ds, keyed[b])
                if b == 0:
                    add(qg, 0, full[:HALF, :])
                    add(qg, 1, full[HALF:, :])
                else:
                    add(qg, 1, full)
        for b in range(2):
            rows = slice(b * HALF, (b + 1) * HALF)
            c, s = cos[rows, :], sin[rows, :]
            qb = qg[b] * scale
            qkv_grad[rows, at[0]] = (qb * c - swap_halves(qb) * s).astype(BF)
            qkv_grad[rows, at[1]] = (kg[b] * c - swap_halves(kg[b]) * s).astype(BF)
            qkv_grad[rows, at[2]] = vg[b].astype(BF)
        return carry

    lax.fori_loop(0, PAIRS, one_pair, 0)
    gain_one = vecs[0:1, :]
    gain_grad = 0.0
    for b in range(2):
        rows = slice(b * HALF, (b + 1) * HALF)
        x = tok[rows, :].astype(F32)
        inverse = lax.rsqrt(row_mean(x * x) + EPSILON)
        unit = x * inverse
        act[rows, :] = (unit * gain_one).astype(BF)
        grad = dot_nt(qkv_grad[rows, :], w_qkv[...])
        scaled = grad * gain_one
        gain_grad += jnp.sum(grad * unit, axis=0, keepdims=True)
        grad_in[rows, :] = rgrad[rows, :] + inverse * (scaled - unit * row_mean(scaled * unit))
    gain_w[...] = jnp.broadcast_to(gain_grad, gain_w.shape)


def attention_back(part, kept, rgrad, agrad, t, packed, vecs):
    _, qkv, _, _, lse, _ = kept
    return pl.pallas_call(
        attention_back_body,
        grid=(1,),
        in_specs=[
            fixed((SEQ, 3 * D)), fixed((SEQ, D)), fixed((16, SEQ)),
            seq_block(1, part), fixed((None, 1, SEQ), part, 0, 0), seq_block(128, part), seq_block(128, part),
            fixed((D, 3 * D), 0, 0), seq_block(D, part), fixed((8, D)), fixed((SEQ, D)),
        ],
        out_specs=[fixed((SEQ, D)), fixed((SEQ, 3 * D)), fixed((SEQ, D)), fixed((8, D))],
        out_shape=[
            jax.ShapeDtypeStruct((SEQ, D), F32), jax.ShapeDtypeStruct((SEQ, 3 * D), BF),
            jax.ShapeDtypeStruct((SEQ, D), BF), jax.ShapeDtypeStruct((8, D), F32),
        ],
        scratch_shapes=[pltpu.VMEM((SEQ, SEQ), F32)],
        compiler_params=kernel_params(),
        cost_estimate=lasting(0),
    )(
        qkv, agrad, lse, t["seg_col"], t["seg_row"], t["cos"], t["sin"], packed, t["tokens"], vecs, rgrad
    )


def mixer_wgrad_body(parts, groups, *refs):
    core, acts, grads, gains = refs[0], refs[1 : 1 + parts], refs[1 + parts : 1 + 2 * parts], refs[1 + 2 * parts : 1 + 3 * parts]
    out_w, small, rows, give, keep, turned, last = refs[1 + 3 * parts :]
    step, half = pl.program_id(0), D // 2
    chunk = half // groups

    def scattered(store, across, value):
        for group in range(groups):
            for c in range(2):
                kept = (core[0] == c).astype(jnp.int32)
                at = pl.ds(pl.multiple_of(kept * half + group * chunk, 16), chunk)
                first = (2 * group + c) * chunk
                store[at, across] = value[first : first + chunk, :]

    @pl.when(step == 0)
    def _():
        for i in range(parts):
            scattered(turned, slice(i * SEQ, (i + 1) * SEQ), acts[i][...].T)

    @pl.when(step < 9)
    def _():
        made = dot(turned[...], jnp.concatenate([v[...] for v in grads], axis=0)).astype(BF)
        give[...] = made[:half, :]
        keep[...] = made[half:, :]

    @pl.when((step >= 9) & (step < 12))
    def _():
        scattered(last, slice(0, 256), out_w[...].astype(BF))
        give[...] = last[:half, :]
        keep[...] = last[half:, :]

    @pl.when(step == 12)
    def _():
        gain_one = sum(v[0:1, :] for v in gains)
        line = lax.broadcasted_iota(jnp.int32, (128, D), 0)
        stacked = 0.0
        for i, row in enumerate((rows[0:1, :], rows[1:2, :], gain_one, rows[2:3, :])):
            stacked += jnp.where(line == 16 + i, row, 0.0)
        scattered(last, slice(0, 128), (small[...] + stacked.T).astype(BF))
        give[:, :128] = last[:half, :128]
        keep[:, :128] = last[half:, :128]
        give[:, 128:] = jnp.zeros((half, 128), BF)
        keep[:, 128:] = jnp.zeros((half, 128), BF)


def mixer_wgrad(acts, grads, gains, out_w, small, rows, groups, core):
    parts = len(acts)
    half = pl.BlockSpec((D // 2, 256), lambda i: (0, i))
    out = jax.ShapeDtypeStruct((D // 2, 4 * D + 256), BF)
    return pl.pallas_call(
        functools.partial(mixer_wgrad_body, parts, groups),
        grid=(13,),
        in_specs=[pl.BlockSpec(memory_space=pltpu.SMEM)]
        + [fixed((SEQ, D))] * parts
        + [pl.BlockSpec((SEQ, 256), lambda i: (0, jnp.minimum(i, 8)))] * parts
        + [fixed((8, D))] * parts
        + [pl.BlockSpec((D, 256), lambda i: (0, jnp.clip(i - 9, 0, 2))), fixed((D, 128)), fixed((8, D))],
        out_specs=[half, half],
        out_shape=[out, out],
        scratch_shapes=[pltpu.VMEM((D, parts * SEQ), BF), pltpu.VMEM((D, 256), BF)],
        compiler_params=kernel_params(),
        cost_estimate=lasting(0),
    )(jnp.stack([core]).astype(jnp.int32), *acts, *grads, *gains, out_w, small, rows)


def tables(tokens, cotangent, prev_logits, routes, capacity, segments, positions):
    parts = tokens.shape[0] // SEQ
    slots = jnp.concatenate(
        [pair_slots(routes[i * SEQ : (i + 1) * SEQ], capacity) for i in range(parts)]
    )
    lane = jnp.arange(128) % HEAD_DIM
    frequency = jnp.exp((lane % (HEAD_DIM // 2)).astype(F32) * (-2.0 * math.log(ROPE_BASE) / HEAD_DIM))
    angles = positions.astype(F32)[:, None] * frequency[None, :]
    sign = jnp.where(lane < HEAD_DIM // 2, -1.0, 1.0)
    return dict(
        tokens=tokens,
        cotangent=cotangent,
        prev=jnp.pad(prev_logits, ((0, 0), (0, 128 - CHOICES))),
        routes=routes,
        slots=slots,
        slot_row=slots.reshape(parts, SEQ, 2).transpose(0, 2, 1),
        seg_col=segments[:, None],
        seg_row=segments.reshape(parts, 1, SEQ),
        cos=jnp.cos(angles),
        sin=jnp.sin(angles) * sign,
    )


FC = 512


def expert_rows_body(x_ref, g_ref, wg_ref, wu_ref, wd_ref, hid_ref, dg_ref, du_ref, out_ref, acc, racc):
    step = pl.program_id(0)
    x = x_ref[:, 0].reshape(-1, D)
    g = g_ref[:, 0].reshape(-1, D)
    wg, wu, wd = wg_ref[...], wu_ref[...], wd_ref[...]
    gate = dot(x, wg)
    up = dot(x, wu)
    hgrad = dot_nt(g, wd).astype(BF).astype(F32)
    sig = 1.0 / (1.0 + jnp.exp(-gate))
    act = gate * sig
    hidden = (act * up).astype(BF)
    dgate = (hgrad * up * sig * (1.0 + gate * (1.0 - sig))).astype(BF)
    dup = (hgrad * act).astype(BF)
    hid_ref[...] = hidden
    dg_ref[...] = dgate
    du_ref[...] = dup
    prod = dot(hidden, wd)
    rgrad = dot_nt(dgate, wg) + dot_nt(dup, wu)

    @pl.when(step == 0)
    def _():
        acc[...] = prod
        racc[...] = rgrad

    @pl.when(step > 0)
    def _():
        acc[...] += prod
        racc[...] += rgrad

    @pl.when(step == pl.num_programs(0) - 1)
    def _():
        out_ref[:, 0] = acc[...].astype(BF).reshape(-1, CAP, D)
        out_ref[:, 1] = racc[...].astype(BF).reshape(-1, CAP, D)


def expert_rows(received, w_gate_up, w_down):
    n = received.shape[0]
    rows = n * CAP
    steps = FF // FC
    wide = jax.ShapeDtypeStruct((rows, FF), BF)
    block = pl.BlockSpec((rows, FC), lambda j: (0, j))
    return pl.pallas_call(
        expert_rows_body,
        grid=(steps,),
        in_specs=[
            pl.BlockSpec((n, 1, CAP, D), lambda j: (0, 0, 0, 0)),
            pl.BlockSpec((n, 1, CAP, D), lambda j: (0, 1, 0, 0)),
            pl.BlockSpec((D, FC), lambda j: (0, j)),
            pl.BlockSpec((D, FC), lambda j: (0, steps + j)),
            pl.BlockSpec((FC, D), lambda j: (j, 0)),
        ],
        out_specs=[block, block, block, pl.BlockSpec((n, 2, CAP, D), lambda j: (0, 0, 0, 0))],
        out_shape=[wide, wide, wide, jax.ShapeDtypeStruct((n, 2, CAP, D), BF)],
        scratch_shapes=[pltpu.VMEM((rows, D), F32), pltpu.VMEM((rows, D), F32)],
        compiler_params=pltpu.CompilerParams(
            dimension_semantics=("arbitrary",), vmem_limit_bytes=VMEM_MOST
        ),
        cost_estimate=lasting(28),
    )(received, received, w_gate_up, w_gate_up, w_down)


FW = 512


def down_wgrad_body(parts, *refs):
    hid, received, out = refs[:parts], refs[parts : 2 * parts], refs[2 * parts]
    rows = jnp.concatenate([v[:, 0].reshape(-1, D) for v in received], axis=0)
    out[...] = dot_tn(jnp.concatenate([v[...] for v in hid], axis=0), rows).astype(BF)


def down_wgrad(received, hid):
    parts, (n, _, _, _) = len(received), received[0].shape
    return pl.pallas_call(
        functools.partial(down_wgrad_body, parts),
        grid=(FF // FW,),
        in_specs=[pl.BlockSpec((n * CAP, FW), lambda j: (0, j))] * parts
        + [pl.BlockSpec((n, 1, CAP, D), lambda j: (0, 1, 0, 0))] * parts,
        out_specs=pl.BlockSpec((FW, D), lambda j: (j, 0)),
        out_shape=jax.ShapeDtypeStruct((FF, D), BF),
        compiler_params=kernel_params(),
        cost_estimate=lasting(10),
    )(*hid, *received)


def gate_up_wgrad_body(parts, *refs):
    received, dg, du = refs[:parts], refs[parts : 2 * parts], refs[2 * parts : 3 * parts]
    out, xt = refs[3 * parts :]
    rows = received[0].shape[0] * CAP

    @pl.when(pl.program_id(0) == 0)
    def _():
        for i in range(parts):
            xt[:, i * rows : (i + 1) * rows] = received[i][:, 0].reshape(rows, D).T

    for k, grads in enumerate((dg, du)):
        out[k] = dot(xt[...], jnp.concatenate([v[...] for v in grads], axis=0)).astype(BF)


def gate_up_wgrad(received, dg, du):
    parts, (n, _, _, _) = len(received), received[0].shape
    return pl.pallas_call(
        functools.partial(gate_up_wgrad_body, parts),
        grid=(FF // FW,),
        in_specs=[pl.BlockSpec((n, 1, CAP, D), lambda j: (0, 0, 0, 0))] * parts
        + [pl.BlockSpec((n * CAP, FW), lambda j: (0, j))] * (2 * parts),
        out_specs=pl.BlockSpec((2, D, FW), lambda j: (0, 0, j)),
        out_shape=jax.ShapeDtypeStruct((2, D, FF), BF),
        scratch_shapes=[pltpu.VMEM((D, parts * n * CAP), BF)],
        compiler_params=kernel_params(),
        cost_estimate=lasting(0),
    )(*received, *dg, *du)


def place_body(spots, count, *refs):
    offsets, blocks, outs, sems = refs[0], refs[1 : 1 + count], refs[1 + count : -1], refs[-1]
    copies = []
    for i, (block, row, rows, column, columns, out) in enumerate(spots):
        down = pl.ds(pl.multiple_of(offsets[2 * i], 16), rows)
        across = pl.ds(pl.multiple_of(offsets[2 * i + 1], 128), columns)
        copies.append(
            pltpu.make_async_copy(
                blocks[block].at[pl.ds(row, rows), pl.ds(column, columns)],
                outs[out].at[down, across],
                sems.at[i],
            )
        )
    for copy in copies:
        copy.start()
    for copy in copies:
        copy.wait()


def place(blocks, spots, offsets, shapes):
    anywhere = pl.BlockSpec(memory_space=pl.ANY)
    return pl.pallas_call(
        functools.partial(place_body, spots, len(blocks)),
        in_specs=[pl.BlockSpec(memory_space=pltpu.SMEM)] + [anywhere] * len(blocks),
        out_specs=[pl.BlockSpec(memory_space=pltpu.VMEM)] * len(shapes),
        out_shape=[jax.ShapeDtypeStruct(v, BF) for v in shapes],
        scratch_shapes=[pltpu.SemaphoreType.DMA((len(spots),))],
        compiler_params=pltpu.CompilerParams(vmem_limit_bytes=VMEM_MOST),
        cost_estimate=lasting(0),
    )(jnp.stack(offsets).astype(jnp.int32), *blocks)


def pick(value, index, axis=0):
    return lax.dynamic_index_in_dim(value, index, axis, False)


def added(*values):
    return sum(v.astype(F32) for v in values).astype(BF)


class Paired:
    axes = ("half", "low", "inner", "side", "core")
    fsdp = ("half", "low", "inner")
    expert = ("side", "core")
    rows = ("side", "low", "inner")
    route_axes = ("half", "low", "inner", "core")
    near = 896
    cut = 3072

    def __init__(self, mesh):
        self.mesh = Mesh(mesh.devices.reshape(2, 2, 2, 2, 2), self.axes)
        self.routes = []
        for turn in range(4):
            pairs = []
            for z in range(4):
                for y in range(2):
                    for c in range(2):
                        half, inner = (z ^ turn) >> 1, (z ^ turn) & 1
                        pairs.append(((z * 2 + y) * 2 + c, ((half * 2 + c) * 2 + inner) * 2 + y))
            self.routes.append(pairs)

    @staticmethod
    def swap(value, axis="core"):
        return lax.ppermute(value, axis, [(0, 1), (1, 0)])

    @staticmethod
    def along(value, turn):
        return lax.ppermute(value, ("half", "low"), [(i, i ^ turn) for i in range(4)])

    @staticmethod
    def spot():
        z = lax.axis_index("half") * 2 + lax.axis_index("low")
        return z, lax.axis_index("inner"), lax.axis_index("side"), lax.axis_index("core")

    @staticmethod
    def joined(gate_up, down):
        high, edge = gate_up.shape[1], D - 256
        tail = down[:, 2 * high :]
        half = tail.shape[1] // 2
        under = jnp.concatenate([tail[:, :half, edge:], tail[:, half:, edge:]], axis=2)
        last = jnp.concatenate([tail[:, :, :edge], under], axis=1)
        cut = Paired.cut
        rest = jnp.concatenate([gate_up[:, :, cut:], down[:, :high], down[:, high : 2 * high], last], axis=2)
        return gate_up[:, :, :cut], rest

    @staticmethod
    def rects(high, deep):
        half, edge, at = deep // 2 - high, D - 256, 2 * FF - Paired.cut
        yield 0, high, at, D, 0, 0
        yield 0, high, at + D, D, high, 0
        yield 0, 2 * half, at + 2 * D, edge, 2 * high, 0
        yield 2 * half, half, at + 2 * D, 256, 2 * high, edge
        yield 2 * half, half, at + 2 * D + 256, 256, 2 * high + half, edge

    def send(self, joined, turn, part):
        mine = pick(joined[part], (self.spot()[0] ^ turn) & 1)
        return lax.ppermute(mine, self.route_axes, self.routes[turn])

    def gather_shared(self, shard, weights, early):
        z, y, x, c = self.spot()
        rows, width = shard.shape
        rows, width = rows // 2, width // 2
        mine = lax.dynamic_slice(shard, (c * rows, x * width), (rows, width))
        stack = jnp.concatenate([mine] + [self.along(mine, turn) for turn in (1, 2, 3)])
        stack, joined, early = lax.optimization_barrier((stack, self.joined(*weights), early))
        sent = {(2, 0): (self.send(joined, 2, 0), None)}
        over_y, over_x = self.swap(stack, "inner"), self.swap(stack, "side")
        far = self.swap(over_y[:, : self.near], "side"), self.swap(over_x[:, self.near :], "inner")
        blocks = [stack, over_y, over_x, *far]
        flips = [(0, 0, 0), (1, 0, 0), (0, 1, 0), (1, 1, 0), (1, 1, self.near)]
        spots, offsets = [], []
        for i, (dy, dx, column) in enumerate(flips + flips):
            core = c if i < len(flips) else 1 - c
            for turn in range(4):
                spots.append((i, turn * rows, rows, 0, blocks[i % len(flips)].shape[1], 0))
                offsets += [((z ^ turn) * 2 + (y ^ dy)) * 2 * rows + core * rows, (x ^ dx) * width + column]
        blocks += [self.swap(v) for v in blocks]
        blocks, joined, sent = lax.optimization_barrier((blocks, joined, sent))
        [full] = place(blocks, spots, offsets, [(16 * rows, 2 * width)])
        return full, early, (joined, sent)

    def gather_more(self, held, value, names):
        joined, sent = held
        more = {v: (self.send(joined, *v), None) for v in names}
        waiting = [v for v, (_, other) in sent.items() if other is None][:2]
        done = {**sent, **{v: (sent[v][0], self.swap(sent[v][0])) for v in waiting}}
        value, joined, sent = lax.optimization_barrier((value, joined, {**done, **more}))
        return (joined, sent), value

    def split(self):
        return 8, lax.axis_index("core")

    def reduce_first(self, give, keep):
        z, y, x, c = self.spot()
        width = give.shape[-1] // 2
        near = (width // 128 + 1) // 2 * 128
        parts = added(keep, self.swap(give)).reshape(4, 2, -1, 2 * width)

        def columns(value, first, count):
            return lax.dynamic_slice_in_dim(value, first, count, value.ndim - 1)

        one = added(columns(parts, x * width, near), self.swap(columns(parts, (1 - x) * width, near), "side"))
        two = jnp.concatenate([parts[..., near:width], parts[..., width + near :]], axis=3)
        two = added(pick(two, y, 1), self.swap(pick(two, 1 - y, 1), "inner"))
        return one, two

    def reduce_last(self, one, two):
        z, y, x, c = self.spot()
        rest = two.shape[2] // 2
        one = added(pick(one, y, 1), self.swap(pick(one, 1 - y, 1), "inner"))
        near = lax.dynamic_slice_in_dim(two, x * rest, rest, 2)
        two = added(near, self.swap(lax.dynamic_slice_in_dim(two, (1 - x) * rest, rest, 2), "side"))
        both = jnp.concatenate([one, two], axis=2)
        mine = added(pick(both, z), *[self.along(pick(both, z ^ turn), turn) for turn in (1, 2, 3)])
        other = self.swap(mine, "side")
        line = jnp.where(x == 0, jnp.concatenate([mine, other], 1), jnp.concatenate([other, mine], 1))
        other = self.swap(line)
        both = jnp.where(c == 0, jnp.concatenate([line, other]), jnp.concatenate([other, line]))
        return both.astype(F32)

    def gather_expert(self, held, shapes):
        sent = held[1]
        c = lax.axis_index("core")
        here = lax.axis_index("half") * 2 + lax.axis_index("inner")
        both = [sent[turn, part] for turn in range(4) for part in range(2)]
        blocks = [v for v, _ in both] + [self.swap(v) if other is None else other for v, other in both]
        high, deep = shapes[0][1], shapes[1][1]
        spots, offsets, zero = [], [], jnp.int32(0)
        for i in range(0, 16, 2):
            shard = (here ^ (i // 2 % 4)) * 2 + (c if i < 8 else 1 - c)
            spots += [(i, 0, high, 0, self.cut, 0), (i + 1, 0, high, 0, 2 * FF - self.cut, 0)]
            offsets += [shard * high, zero, shard * high, zero + self.cut]
            for row, rows, column, columns, to_row, to_column in self.rects(high, deep):
                spots.append((i + 1, row, rows, column, columns, 1))
                offsets += [shard * deep + to_row, zero + to_column]
        return place(blocks, spots, offsets, [(8 * high, 2 * FF), (8 * deep, D)])

    def scatter_start(self, grad, axis):
        c = lax.axis_index("core")
        shape = grad.shape
        grad = grad.reshape(shape[:axis] + (4, 2, shape[axis] // 8) + shape[axis + 1 :])
        return added(pick(grad, c, axis + 1), self.swap(pick(grad, 1 - c, axis + 1)))

    def scatter_send(self, parts, axis):
        here = lax.axis_index("half") * 2 + lax.axis_index("inner")
        got = {}
        for turn in (2, 3, 0, 1):
            back = [(b, a) for a, b in self.routes[turn]]
            got[turn] = lax.ppermute(pick(parts, here ^ turn, axis), self.route_axes, back)
        return got

    def scatter_end(self, got, axis):
        even = (self.spot()[0] & 1) == 0
        first, second = [got[i].astype(F32) + got[i + 2].astype(F32) for i in range(2)]
        return jnp.stack([jnp.where(even, first, second), jnp.where(even, second, first)])


class Plain:
    axes = ("outer", "inner", "expert")
    fsdp = ("outer", "inner")
    expert = ("expert",)
    rows = ("expert", "inner")

    def __init__(self, mesh):
        fsdp, expert = mesh.shape["fsdp"], mesh.shape["expert"]
        inner = EXPERTS // expert
        self.mesh = Mesh(mesh.devices.reshape(fsdp // inner, inner, expert), self.axes)

    def gather_shared(self, shard, weights, early):
        return lax.all_gather(shard, self.fsdp, axis=0, tiled=True), early, weights

    def gather_more(self, held, value, names):
        return held, value

    def split(self):
        return 1, jnp.int32(1)

    def reduce_first(self, give, keep):
        return jnp.concatenate([give, keep]), None

    def reduce_last(self, total, _):
        total = lax.psum_scatter(total, self.axes, scatter_dimension=0, tiled=True)
        return lax.all_gather(total, self.expert, axis=0, tiled=True).astype(F32)

    def gather_expert(self, weights, shapes):
        full = []
        for weight in weights:
            own = lax.all_to_all(weight, "inner", 0, 0, tiled=True)
            own = lax.all_gather(own, "outer", axis=0, tiled=True)
            full.append(own.reshape((-1,) + weight.shape[2:]))
        return full

    def scatter_start(self, grad, axis):
        return grad

    def scatter_send(self, grad, axis):
        return grad

    def scatter_end(self, grad, axis):
        inner = lax.axis_size("inner")
        part = lax.psum_scatter(grad, "outer", scatter_dimension=axis, tiled=True)
        shape = part.shape
        part = part.reshape(shape[:axis] + (inner, shape[axis] // inner) + shape[axis + 1 :])
        part = jnp.moveaxis(part, axis, 0)
        return lax.all_to_all(part, "inner", 0, 0, tiled=True).astype(F32)


def solution(mesh):
    plan = Paired(mesh) if (mesh.shape["fsdp"], mesh.shape["expert"]) == (8, 4) else Plain(mesh)

    def on_device(
        tokens, cotangent, prev_logits, routes, capacity, segments, positions,
        w_qkv, w_out, gate_matrix, const_values, attn_gain, moe_gain, w_gate_up, w_down,
    ):
        rows = w_qkv.shape[0]
        pad = jnp.zeros((rows, 256 - 20), BF)
        small = jnp.concatenate(
            [gate_matrix, const_values, attn_gain[:, None], moe_gain[:, None], pad], axis=1
        )
        shard = jnp.concatenate([w_qkv, w_out, small], axis=1)
        t = tables(tokens, cotangent, prev_logits, routes, capacity, segments, positions)
        packed, t, held = plan.gather_shared(shard, (w_gate_up, w_down), t)
        columns = packed[:, 4 * D + 16 : 4 * D + 20].astype(F32).T
        vecs = jnp.concatenate([columns[2:], columns[:2], jnp.zeros((4, D), F32)])
        parts = tokens.shape[0] // SEQ
        kept, sends, shared = [], [], packed
        for i in range(parts):
            if i == 1:
                held, (shared, kept[0][5]) = plan.gather_more(held, (packed, kept[0][5]), ((2, 1), (0, 0), (0, 1), (1, 0)))
            kept.append(list(forward_part(i, t, shared, vecs)))
            sends.append(kept[i][0])
        held, sends[-1] = plan.gather_more(held, sends[-1], ((3, 0), (3, 1), (1, 1)))
        gate_up_full, down_full = plan.gather_expert(held, (w_gate_up.shape, w_down.shape))
        received = [lax.all_to_all(v, plan.rows, 0, 0, tiled=True) for v in sends]
        made = [expert_rows(r, gate_up_full, down_full) for r in received]
        hid, dg, du = [[m[i] for m in made] for i in range(3)]
        backs = [m[3] for m in made]
        gate_up_w = gate_up_wgrad(received, dg, du)
        backs[-1], hid, gate_up_w = lax.optimization_barrier((backs[-1], hid, gate_up_w))
        returned = [lax.all_to_all(v, plan.rows, 0, 0, tiled=True) for v in backs]
        gate_up_sums = plan.scatter_start(gate_up_w, 1)
        down_w = down_wgrad(received, hid)
        returned[0], gate_up_sums, down_w = lax.optimization_barrier((returned[0], gate_up_sums, down_w))
        gate_up_got = plan.scatter_send(gate_up_sums, 1)
        down_sums = plan.scatter_start(down_w, 0)
        firsts, lasts, sums = [], [], None
        for i in range(parts):
            *first, out_w, small_w, rows_w = combine_part(i, returned[i], kept[i], t, packed, vecs, sums)
            sums = (out_w, small_w, rows_w)
            firsts.append(first)
            if i == parts - 1:
                held = (gate_up_got, down_sums, first[1], [v[3] for v in lasts])
                gate_up_got, down_sums, first[1], _ = lax.optimization_barrier(held)
                down_got = plan.scatter_send(down_sums, 0)
            lasts.append(attention_back(i, kept[i], first[1], first[3], t, packed, vecs))
            if i == 0:
                returned[-1], sums, _ = lax.optimization_barrier((returned[-1], sums, lasts[0][3]))
        acts = [v[2] for v in lasts]
        halves = mixer_wgrad(
            acts, [v[1] for v in lasts], [v[3] for v in lasts], *sums, *plan.split()
        )
        halves, down_got = lax.optimization_barrier((halves, down_got))
        down_total = plan.scatter_end(down_got, 0)
        total = plan.reduce_last(*plan.reduce_first(*halves))
        gate_up_total = plan.scatter_end(gate_up_got, 1)
        gate_up_total = jnp.concatenate([gate_up_total[:, 0], gate_up_total[:, 1]], axis=2)
        return (
            jnp.concatenate([v[0] for v in firsts]),
            jnp.concatenate([v[0] for v in lasts]),
            jnp.concatenate([v[2] for v in firsts]),
            total[:, : 3 * D],
            total[:, 3 * D : 4 * D],
            total[:, 4 * D : 4 * D + 16],
            total[:, 4 * D + 16 : 4 * D + 18],
            total[:, 4 * D + 18],
            total[:, 4 * D + 19],
            gate_up_total,
            down_total,
        )

    every = plan.fsdp + plan.expert
    split = P(every, None)
    shard = P(plan.fsdp, None)
    line = P(plan.fsdp)
    whole = P(plan.expert, plan.fsdp, None)
    return jax.shard_map(
        on_device,
        mesh=plan.mesh,
        in_specs=(
            split, split, split, split, P(), P(every), P(every),
            shard, shard, shard, shard, line, line, whole, whole,
        ),
        out_specs=(split, split, split, shard, shard, shard, shard, line, line, whole, whole),
        check_vma=False,
    )
```
